32 devices in a mesh: stream: 2 (over core), dp: 16 (over z, y, x).
Axes of the slice: x: 2, y: 2, z: 4, core: 2. Of those that a mesh axis runs over, the one named last changes fastest.
Arguments:
- x_in: bfloat16 [2, 64, 128, 768], P('stream', 'dp'), may hold values from -6 to 6
- lengths: int32 [64], P('dp'), may hold values from 33 to 100, as said below
- drops: int32 [64], P('dp'), may hold values 0 or 1
- proj_master: float32 [2, 2, 3, 768, 768], P('stream', None, None, 'dp'), may hold values from -0.21875 to 0.21875
- out_master: float32 [2, 2, 768, 768], P('stream', None, 'dp'), may hold values from -1.25 to 1.25
- ffn_in_master: float32 [2, 768, 3072], P('stream', 'dp'), may hold values from -0.21875 to 0.21875
- ffn_out_master: float32 [2, 3072, 768], P('stream', 'dp'), may hold values from -0.109375 to 0.109375
- join_master: float32 [2, 2, 768, 768], P('stream', None, 'dp'), may hold values from -0.21875 to 0.21875
- vectors: float32 [2, 7, 768], P('stream', None, 'dp'), may hold values from -2 to 2.2
- cotangent: bfloat16 [2, 64, 128, 768], P('stream', 'dp'), may hold values from -6 to 6
Outputs:
- joined: bfloat16 [2, 64, 128, 768], P('stream', 'dp')
- x_grad: bfloat16 [2, 64, 128, 768], P('stream', 'dp')
- proj_grad: float32 [2, 2, 3, 768, 768], P('stream', None, None, 'dp')
- out_grad: float32 [2, 2, 768, 768], P('stream', None, 'dp')
- ffn_in_grad: float32 [2, 768, 3072], P('stream', 'dp')
- ffn_out_grad: float32 [2, 3072, 768], P('stream', 'dp')
- join_grad: float32 [2, 2, 768, 768], P('stream', None, 'dp')
- vectors_grad: float32 [2, 7, 768], P('stream', None, 'dp')
The draws below stay inside these ranges and needn't reach their ends.
Inputs may be any that keep to these rules, and one draw needn't show every extreme that they name: `lengths`: each page holds 33 to 100 regions; some page holds exactly 100.
All inputs are finite; a program needn't handle non-finite values. No bound on the sum of `drops` on one device may be relied on, other than what follows from the above.
Results may differ from the reference program's by a relative error of at most 0.023.
Values may be sent and summed in bfloat16 or wider, within the bound.
A program may use at most 256 MiB of HBM per device.

```python
import math
import jax
import jax.numpy as jnp
from jax import lax

D = 768
HEADS = 12
FF = 3072
PAD = 128
MAXLEN = 100
PAGES = 64


def draw_lengths(key, part):
    key = jax.random.fold_in(key, 5)
    first_key, second_key = jax.random.split(key)
    counts = jax.random.randint(first_key, (PAGES,), MAXLEN // 3, MAXLEN + 1)
    fullest = jax.random.randint(second_key, (), 0, PAGES)
    return jnp.where(jnp.arange(PAGES) == fullest, MAXLEN, counts).astype(jnp.int32)


def draw_vectors(key, part):
    key = jax.random.fold_in(key, 11)
    noise = jnp.clip(jax.random.normal(key, (2, 7, D), jnp.float32), -4.0, 4.0)
    base = jnp.array([1.0, 0.0, 1.0, 0.0, 1.0, 0.0, 0.0], jnp.float32)[None, :, None]
    spread = jnp.array([0.3, 0.3, 0.3, 0.3, 0.3, 0.3, 0.5], jnp.float32)[None, :, None]
    return base + spread * noise


def plant(values, key, low, largest):
    shape = values.shape
    spot = [jax.random.randint(jax.random.fold_in(key, axis), (), 0, shape[axis]) for axis in range(len(shape))]
    values = values.at[tuple(spot)].set(low)
    longest = shape.index(max(shape))
    spot[longest] = (spot[longest] + 1) % shape[longest]
    return values.at[tuple(spot)].set(largest)


def block_scale(own_key, extent, shards, low, high):
    factor_of, own = 1.0, jax.random.fold_in(own_key, 6)
    for position, blocks in shards:
        steps = jnp.exp(jax.random.uniform(jax.random.fold_in(own, position), (blocks,), jnp.float32, low / len(shards), high / len(shards)))
        factor_of = factor_of * jnp.repeat(steps, extent[position] // blocks).reshape([-1 if axis == position else 1 for axis in range(len(extent))])
    return factor_of


def normal_values(key, extent, deviation, reach, cuts=(), kind=jnp.bfloat16):
    level = block_scale(key, extent, cuts, -0.22, 0.18) if cuts else 1.0
    values = jax.random.normal(key, extent, jnp.float32) * deviation * level
    return jnp.minimum(jnp.maximum(values, -reach), reach).astype(kind)


def setup_inputs(seed: int = 0) -> dict:
    seeds = jax.random.split(jax.random.key(seed), 11)
    return {
        "x_in": normal_values(seeds[0], (2, PAGES, PAD, D), 1.0, 6.0, ((0, 2), (1, 16))),
        "lengths": draw_lengths(jax.random.fold_in(seeds[10], 71), 0),
        "drops": plant((jax.random.randint(seeds[2], (PAGES,), 0, 4) < 1).astype(jnp.int32), jax.random.fold_in(seeds[2], 1), 0, 1),
        "proj_master": normal_values(seeds[3], (2, 2, 3, D, D), D ** -0.5, 0.21875, ((0, 2), (3, 16)), jnp.float32),
        "out_master": normal_values(seeds[4], (2, 2, D, D), (D // 32) ** -0.5, 1.25, ((0, 2), (2, 16)), jnp.float32),
        "ffn_in_master": normal_values(seeds[5], (2, D, FF), D ** -0.5, 0.21875, ((0, 2), (1, 16)), jnp.float32),
        "ffn_out_master": normal_values(seeds[6], (2, FF, D), FF ** -0.5, 0.109375, ((0, 2), (1, 16)), jnp.float32),
        "join_master": normal_values(seeds[7], (2, 2, D, D), D ** -0.5, 0.21875, ((0, 2), (2, 16)), jnp.float32),
        "vectors": draw_vectors(jax.random.fold_in(seeds[10], 71), 0),
        "cotangent": normal_values(seeds[9], (2, PAGES, PAD, D), 1.0, 6.0, ((0, 2), (1, 16))),
    }


@jax.custom_vjp
def low(v):
    return lax.optimization_barrier(v.astype(jnp.bfloat16)).astype(jnp.float32)

@jax.custom_vjp
def low_back(v):
    return v

def low_keep(v):
    return (low(v), None)

def low_pass(kept, grad):
    return (grad,)

def back_keep(v):
    return (v, None)

def back_low(kept, grad):
    return (low(grad),)
low.defvjp(low_keep, low_pass)
low_back.defvjp(back_keep, back_low)
EPSILON = 1e-05

def product(left, right):
    return jnp.matmul(left, right, precision=lax.Precision.HIGHEST)

def norm_rows(values, gain, shift):
    centre = values - lax.optimization_barrier(jnp.mean(values, axis=-1, keepdims=True))
    spread = lax.optimization_barrier(jnp.mean(centre * centre, axis=-1, keepdims=True))
    return centre * lax.rsqrt(spread + EPSILON) * gain + shift

def split_heads(values):
    return values.reshape(values.shape[0], values.shape[1], HEADS, D // HEADS)

def attend(query, keys, values, key_mask):
    scale = (D // HEADS) ** (-0.5)
    scores = jnp.einsum('gqhe,gkhe->ghqk', split_heads(query), split_heads(keys), precision=lax.Precision.HIGHEST) * scale
    scores = low_back(scores)
    scores = jnp.where(key_mask[:, None, None, :], scores, -1e+30)
    top = lax.optimization_barrier(jnp.max(scores, axis=-1, keepdims=True))
    weights = jnp.exp(scores - top)
    probs = weights / lax.optimization_barrier(jnp.sum(weights, axis=-1, keepdims=True))
    mixed = jnp.einsum('ghqk,gkhe->gqhe', low(probs), split_heads(values), precision=lax.Precision.HIGHEST)
    return mixed.reshape(query.shape)

def layer(inputs, proj, outw, ffin, ffout, join, vecs, key_mask, keep):
    proj = low(proj)
    outw = low(outw)
    ffin = low(ffin)
    ffout = low(ffout)
    join = low(join)
    vecs = low(vecs)
    row_mask = key_mask[..., None].astype(inputs.dtype)
    keep_rows = keep[:, None, None]
    keys = [low_back(low(product(inputs[side], proj[side, 0, 1]))) for side in range(2)]
    values = [low_back(low(product(inputs[side], proj[side, 0, 2]))) for side in range(2)]
    states = []
    for side in range(2):
        other = 1 - side
        source = inputs[side]
        query = low_back(low(product(source, proj[side, 0, 0])))
        cross = low_back(low(attend(query, keys[other], values[other], key_mask)))
        branch = low_back(product(cross, outw[side, 0])) * keep_rows
        first = norm_rows(source + branch, vecs[side, 0], vecs[side, 1])
        first_low = low(first)
        query2 = low_back(low(product(first_low, proj[side, 1, 0])))
        keys2 = low_back(low(product(first_low, proj[side, 1, 1])))
        values2 = low_back(low(product(first_low, proj[side, 1, 2])))
        selfout = low_back(low(attend(query2, keys2, values2, key_mask)))
        second = norm_rows(first + low_back(product(selfout, outw[side, 1])), vecs[side, 2], vecs[side, 3])
        hidden = low_back(product(low(second), ffin[side]))
        active = low(jax.nn.gelu(hidden, approximate=False))
        third = norm_rows(second + low_back(product(active, ffout[side])), vecs[side, 4], vecs[side, 5])
        states.append(low(third))
    results = []
    for side in range(2):
        partner = low_back(states[1 - side])
        logits = low_back(product(states[side], join[side, 0]) + product(partner, join[side, 1]) + vecs[side, 6])
        gate = jax.nn.sigmoid(logits)
        results.append((gate * states[side] + (1.0 - gate) * partner) * row_mask)
    return jnp.stack(results)

def reference(x_in, lengths, drops, proj_master, out_master, ffn_in_master, ffn_out_master, join_master, vectors, cotangent):
    group = math.gcd(PAGES, 32)
    count = PAGES // group
    inputs = x_in.astype(jnp.float32).reshape(2, count, group, PAD, D).transpose(1, 0, 2, 3, 4)
    cots = cotangent.astype(jnp.float32).reshape(2, count, group, PAD, D).transpose(1, 0, 2, 3, 4)
    lens = lengths.reshape(count, group).astype(jnp.int32)
    flags = drops.reshape(count, group).astype(jnp.int32)
    masters = (proj_master, out_master, ffn_in_master, ffn_out_master, join_master, vectors)
    zeros = tuple((jnp.zeros_like(item) for item in masters))

    def step(totals, item):
        block, block_cot, block_len, block_flag = item
        key_mask = jnp.arange(PAD, dtype=jnp.int32)[None, :] < block_len[:, None]
        keep = (1 - block_flag).astype(block.dtype)

        def forward(inputs_here, *weights):
            return layer(inputs_here, *weights, key_mask, keep)
        result, pull = jax.vjp(forward, block, *masters)
        grads = pull(block_cot)
        totals = tuple((total + grad for total, grad in zip(totals, grads[1:])))
        return (totals, (result.astype(jnp.bfloat16), grads[0].astype(jnp.bfloat16)))
    totals, (results, input_grads) = lax.scan(step, zeros, (inputs, cots, lens, flags))
    joined = results.transpose(1, 0, 2, 3, 4).reshape(2, PAGES, PAD, D)
    x_grad = input_grads.transpose(1, 0, 2, 3, 4).reshape(2, PAGES, PAD, D)
    return (joined, x_grad, totals[0], totals[1], totals[2], totals[3], totals[4], totals[5])
```

```python
import math
from functools import partial

import jax
import jax.numpy as jnp
from jax import lax
from jax.experimental import pallas as pl
from jax.experimental.pallas import tpu as pltpu
from jax.sharding import PartitionSpec as P

HEADS = 12

EPSILON = 1e-05
VMEM_LIMIT = 62 * 2**20
TRANSFERS = 300
MESH = pl.DeviceIdType.MESH
LOW = jnp.bfloat16
FULL = jnp.float32
LINE, PLANE = 4, 4
RANKS = LINE * PLANE
HALF = LINE // 2
KV_CROSS, QO_CROSS, QK_SELF, VO_SELF, JOIN = range(5)
SQUARES = 5
FFN_OUT_ROWS, FFN_IN_ROWS = 10, 14
ITEMS = (
    (KV_CROSS, 0, 1),
    (KV_CROSS, 1, 1),
    (QO_CROSS, 0, 2),
    (QK_SELF, 0, 2),
    (VO_SELF, 0, 2),
    (JOIN, 0, 2),
    (JOIN, 0, 1),
    (JOIN, 1, 1),
)
VECTORS = None
H2, FFN, STATE, ERR, FFN_BACK = range(5)
CORNER_RING, SIDE_RING, LINE_RING, HOP_RING, PAIR_RING = 3, 4, 5, 5, 3
BLOCK = 64
KEPT = 112
TILE = 256
TILES = tuple(pl.ds(at, TILE) for at in range(0, 768, TILE))
HEAD = 64
PAIR = 2 * HEAD


class Links:
    def __init__(self, send_sems, recv_sems):
        self.stream = lax.axis_index("stream")
        self.me = lax.axis_index("dp")
        self.z = self.me // PLANE
        self.q = self.me % PLANE
        self.qx = self.q + 1 - 2 * (self.q % 2)
        self.qy = (self.q + 2) % PLANE
        self.qd = PLANE - 1 - self.q
        self.xx, self.yy = self.q % 2, self.q // 2
        self.columns = (self.q, self.qx, self.qy, self.qd)
        self.z_near = self.z + 1 - 2 * (self.z % 2)
        self.z_two = (self.z + 2) % LINE
        self.z_third = LINE - 1 - self.z
        self.middle = (self.z == 1) | (self.z == 2)
        self.x = (self.stream, self.z * PLANE + self.qx)
        self.y = (self.stream, self.z * PLANE + self.qy)
        self.near, self.two, self.third = (
            (self.stream, at * PLANE + self.q) for at in (self.z_near, self.z_two, self.z_third)
        )
        self.twin = (1 - self.stream, self.me)
        self.sems = (send_sems, recv_sems)
        self.used = 0

    def greet(self):
        for peer in (self.x, self.y, self.near, self.two, self.third, self.twin):
            pl.semaphore_signal(
                pltpu.get_barrier_semaphore(), inc=1, device_id=peer, device_id_type=MESH
            )

    def met(self):
        pl.semaphore_wait(pltpu.get_barrier_semaphore(), 6)

    def copy(self, source, target, peer, landing=None):
        number = self.used
        self.used += 1
        return pltpu.make_async_remote_copy(
            src_ref=source,
            dst_ref=target,
            send_sem=self.sems[0].at[number],
            recv_sem=self.sems[1].at[number if landing is None else landing],
            device_id=peer,
            device_id_type=MESH,
        )

    def send(self, source, target, peer):
        copy = self.copy(source, target, peer)
        copy.start()
        return copy


class LineGather:
    def __init__(self, view, links):
        self.view, self.k = view, links

    def launch(self):
        k = self.k
        own = self.view(k.z)
        self.near = k.send(own, own, k.near)
        self.two = k.send(own, own, k.two)
        landing = k.used
        self.third = k.copy(own, own, k.third)
        passed = self.view(k.z_two)
        self.passed = k.copy(passed, passed, k.near, landing)
        pl.when(k.middle)(self.third.start)

    def relay(self):
        self.two.wait_recv()
        pl.when(self.k.middle)(self.passed.start)

    def arrive(self):
        self.near.wait_recv()
        self.third.wait_recv()

    def drain(self):
        self.near.wait_send()
        self.two.wait_send()

        @pl.when(self.k.middle)
        def _():
            self.third.wait_send()
            self.passed.wait_send()


class LineSum:
    def __init__(self, view, room, links, straight=False):
        self.view, self.room, self.k, self.straight = view, room, links, straight

    def launch(self):
        k = self.k
        self.spots, self.hop = self.room()
        self.near = k.send(self.view(k.z_near), self.spots(0), k.near)
        away = self.view(k.z_third)
        self.third = k.copy(away, self.spots(2), k.third)
        if self.straight:
            self.third.start()
            self.two = k.send(self.view(k.z_two), self.spots(1), k.two)
            return
        self.passed = k.copy(away, self.hop, k.near)
        pl.when(k.middle)(self.third.start)
        pl.when(jnp.logical_not(k.middle))(self.passed.start)

    def bridge(self):
        k = self.k
        if self.straight:
            return
        part = self.view(k.z_two)

        @pl.when(k.middle)
        def _():
            self.passed.wait_recv()
            part[...] = total(part, self.hop).astype(part.dtype)

        self.two = k.send(part, self.spots(1), k.two)

    def collect(self, put):
        k = self.k
        self.near.wait_recv()
        self.two.wait_recv()
        terms = [self.view(k.z), self.spots(0), self.spots(1)]
        if self.straight:
            self.third.wait_recv()
            put(total(*terms, self.spots(2)))
            return

        @pl.when(k.middle)
        def _():
            self.third.wait_recv()
            put(total(*terms, self.spots(2)))

        pl.when(jnp.logical_not(k.middle))(lambda: put(total(*terms)))

    def drain(self):
        self.near.wait_send()
        self.two.wait_send()
        if self.straight:
            self.third.wait_send()
            return
        pl.when(self.k.middle)(self.third.wait_send)
        pl.when(jnp.logical_not(self.k.middle))(self.passed.wait_send)


class GatherByLine:
    def __init__(self, view, links):
        self.view, self.k = view, links
        self.line = LineGather(lambda z: view(z, links.q), links)

    def L(self):
        self.line.launch()

    def R(self):
        self.line.relay()

    def X(self):
        k = self.k
        self.line.arrive()
        column = self.view(slice(None), k.q)
        self.sides = [k.send(column, column, k.x), k.send(column, column, k.y)]

    def C(self):
        k = self.k
        for copy in self.sides:
            copy.wait_recv()
        one, two = self.view(slice(0, HALF), k.qx), self.view(slice(HALF, LINE), k.qy)
        self.corners = [k.send(one, one, k.y), k.send(two, two, k.x)]

    def F(self):
        for copy in self.corners:
            copy.wait_recv()
        for copy in self.sides + self.corners:
            copy.wait_send()
        self.line.drain()


class GatherByPlane:
    def __init__(self, view, links):
        self.view, self.k = view, links
        self.lines = [
            LineGather(partial(lambda q, z: view(z, q), q), links) for q in links.columns
        ]

    def X(self):
        k = self.k
        own = self.view(k.z, k.q)
        self.sides = [k.send(own, own, k.x), k.send(own, own, k.y)]

    def C(self):
        k = self.k
        for copy in self.sides:
            copy.wait_recv()
        one, two = self.view(k.z, k.qx, 0, 1), self.view(k.z, k.qy, 1, 1)
        self.corners = [k.send(one, one, k.y), k.send(two, two, k.x)]

    def L(self, column):
        if column == 3:
            for copy in self.corners:
                copy.wait_recv()
        self.lines[column].launch()

    def R(self, column):
        self.lines[column].relay()

    def F(self):
        for line in self.lines:
            line.arrive()
        for line in self.lines:
            line.drain()
        for copy in self.sides + self.corners:
            copy.wait_send()


class ScatterByPlane:
    def __init__(self, view, room, put, links, straight):
        self.view, self.room, self.put, self.k = view, room, put, links
        self.line = LineSum(lambda z: view(z, links.q), room.line, links, straight)

    def C(self):
        k = self.k
        self.corners, self.sides = self.room.plane()
        low, high = slice(0, HALF), slice(HALF, LINE)
        self.one = [
            k.send(self.view(low, k.qd), self.corners(0), k.x),
            k.send(self.view(high, k.qd), self.corners(1), k.y),
        ]
        self.two = [
            k.send(self.view(low, k.qx), self.sides(0, low), k.x),
            k.send(self.view(high, k.qy), self.sides(1, high), k.y),
        ]

    def X(self):
        k = self.k
        low, high = slice(0, HALF), slice(HALF, LINE)
        for number, half, q in ((0, low, k.qy), (1, high, k.qx)):
            self.one[number].wait_recv()
            part = self.view(half, q)
            part[...] = total(part, self.corners(number)).astype(part.dtype)
        self.two += [
            k.send(self.view(high, k.qx), self.sides(0, high), k.x),
            k.send(self.view(low, k.qy), self.sides(1, low), k.y),
        ]

    def L(self):
        k = self.k
        for copy in self.two:
            copy.wait_recv()
        part = self.view(slice(None), k.q)
        everything = slice(None)
        part[...] = total(part, self.sides(0, everything), self.sides(1, everything)).astype(part.dtype)
        self.line.launch()

    def B(self):
        self.line.bridge()

    def F(self):
        self.line.collect(self.put.sums)
        self.put.store()
        for copy in self.one + self.two:
            copy.wait_send()
        self.line.drain()


class PairGatherByLine:
    def __init__(self, view, links, first=None):
        self.view, self.k, self.first = view, links, first
        self.line = LineGather(lambda z: view(z, links.yy), links)

    def L(self):
        if self.first is not None:
            self.first().wait_recv()
        self.line.launch()

    def R(self):
        self.line.relay()

    def X(self):
        k = self.k
        self.line.arrive()
        column = self.view(slice(None), k.yy)
        self.side = k.send(column, column, k.y)

    def F(self):
        self.side.wait_recv()
        self.side.wait_send()
        self.line.drain()
        if self.first is not None:
            self.first().wait_send()


class PairGatherByPlane:
    def __init__(self, view, links):
        self.view, self.k = view, links
        self.lines = [
            LineGather(partial(lambda y, z: view(z, y), y), links) for y in (links.yy, 1 - links.yy)
        ]

    def X(self):
        k = self.k
        own = self.view(k.z, k.yy)
        self.side = k.send(own, own, k.y)

    def L(self, row):
        if row == 1:
            self.side.wait_recv()
        self.lines[row].launch()

    def R(self, row):
        self.lines[row].relay()

    def F(self):
        for line in self.lines:
            line.arrive()
        for line in self.lines:
            line.drain()
        self.side.wait_send()


class PairScatterByPlane:
    def __init__(self, view, room, put, links):
        self.view, self.room, self.put, self.k = view, room, put, links
        self.line = LineSum(lambda z: view(z, links.yy), room.line, links)

    def C(self):
        k = self.k
        self.side = self.room.column()
        self.two = k.send(self.view(slice(None), 1 - k.yy), self.side, k.y)

    def L(self):
        k = self.k
        self.two.wait_recv()
        part = self.view(slice(None), k.yy)
        part[...] = total(part, self.side).astype(part.dtype)
        self.line.launch()

    def B(self):
        self.line.bridge()

    def F(self):
        self.line.collect(self.put.sums)
        self.put.store()
        self.two.wait_send()
        self.line.drain()

    def G(self):
        self.put.G()


class PairScatterByLine:
    def __init__(self, view, side, room, put, links):
        self.view, self.side, self.put, self.k = view, side, put, links
        self.rows = (1 - links.yy, links.yy)
        self.lines = [
            LineSum(partial(lambda y, z: view(z, y), y), room.line, links) for y in self.rows
        ]

    def L(self, row):
        self.lines[row].launch()

    def B(self, row):
        self.lines[row].bridge()

    def M(self, row):
        part = self.view(self.k.z, self.rows[row])

        def put(value):
            part[...] = value.astype(part.dtype)

        self.lines[row].collect(put)

    def X(self):
        k = self.k
        self.two = k.send(self.view(k.z, 1 - k.yy), self.side, k.y)

    def F(self):
        k = self.k
        self.two.wait_recv()
        self.put.sums(total(self.view(k.z, k.yy), self.side))
        self.put.store()
        self.two.wait_send()
        for line in self.lines:
            line.drain()


def total(*refs):
    result = refs[0][...].astype(FULL)
    for ref in refs[1:]:
        result = result + ref[...].astype(FULL)
    return result


class Room:
    def __init__(self, size, corners, sides, lines, hops, used):
        self.size, self.used = size, used
        self.corners, self.sides, self.lines, self.hops = corners, sides, lines, hops

    def slot(self, ring):
        number = self.used.setdefault(id(ring), 0)
        self.used[id(ring)] += 1
        return ring.at[number % ring.shape[0]]

    def column(self):
        return self.slot(self.sides)

    def plane(self):
        corners, sides = self.slot(self.corners), self.slot(self.sides)
        some = pl.ds(0, self.size)
        return (lambda n: corners.at[n, :, some]), (lambda n, half: sides.at[half, n, some])

    def line(self):
        lines, hops = self.slot(self.lines), self.slot(self.hops)
        some = pl.ds(0, self.size)
        return (lambda n: lines.at[n, some]), hops.at[some]


class VectorRoom(Room):
    def plane(self):
        return (lambda n: self.corners.at[n]), (lambda n, half: self.sides.at[n, half])

    def line(self):
        return (lambda n: self.lines.at[n]), self.hops


class Put:
    def __init__(self, stage, targets, sems, first):
        self.stage, self.targets, self.sems, self.first = stage, targets, sems, first
        self.copies = []

    def sums(self, values):
        for i in range(len(self.targets)):
            self.stage(i)[...] = values[i]

    def store(self):
        for i, target in enumerate(self.targets):
            copy = pltpu.make_async_copy(self.stage(i), target, self.sems.at[self.first + i])
            copy.start()
            self.copies.append(copy)


class PutVectors:
    def __init__(self, target):
        self.target, self.copies = target, []

    def sums(self, values):
        rows, _, width = self.target.shape
        for row in range(rows):
            self.target[row] = values[row : row + 1, :width]

    def store(self):
        pass


def layer_kernel(
    rows,
    lengths,
    drops,
    x_in,
    cot_in,
    proj,
    outw,
    fin,
    fout,
    join,
    vec,
    joined,
    x_grad,
    proj_g,
    out_g,
    fin_g,
    fout_g,
    join_g,
    vec_g,
    sq,
    fi,
    wd,
    halves,
    vecs,
    corners,
    sides,
    lines,
    hops,
    side_room,
    pair_lines,
    pair_hops,
    vcorners,
    vsides,
    vlines,
    vhop,
    vw,
    vg,
    part,
    x,
    cot,
    nothing,
    h2a,
    ea,
    act,
    mid,
    slope,
    probs,
    unit,
    inv,
    work,
    load_sems,
    page_sems,
    store_sems,
    send_sems,
    recv_sems,
    ready,
):
    k = Links(send_sems, recv_sems)
    width = sq.shape[-1]
    count = x.shape[0]
    pages, slots = x_in.shape[:2]
    pairs = width // PAIR
    scale = HEAD**-0.5
    (k1, v1, q1, o1, h1, q2, k2, v2, o2, state, far, edge, back) = range(13)
    mine, theirs = pl.ds(0, count), pl.ds(count, count)
    acc, res, grd = (work.at[pl.ds(i * count, count)] for i in range(3))

    def weight(group, index):
        return sq[group, :, :, index].reshape(width, width)

    def in_weight(block):
        return fi[:, :, block].reshape(width, width)

    def out_weight(block):
        return wd[2 * block : 2 * block + 2].reshape(width, width)

    def free(slot):
        return mid.at[slot // 2, pl.ds((slot % 2) * count, count)]

    def spare(slot):
        return slope.at[slot // 2, pl.ds((slot % 2) * count, count)]

    def times(left, right):
        return jnp.dot(left, right, preferred_element_type=FULL)

    def times_transposed(left, right):
        return lax.dot_general(left, right, (((1,), (1,)), ((), ())), preferred_element_type=FULL)

    def outer(left, right):
        return lax.dot_general(left, right, (((0,), (0,)), ((), ())), preferred_element_type=FULL)

    def loop(first, last, body):
        def step(i, carry):
            body(i)
            return carry

        lax.fori_loop(first, last, step, 0)

    def by_rows(body, first=0, last=None):
        def step(i):
            body(pl.ds(pl.multiple_of(i * BLOCK, BLOCK), BLOCK), i)

        loop(first, count // BLOCK if last is None else last, step)

    def rows_of(i):
        return lax.broadcasted_iota(jnp.int32, (BLOCK, 1), 0) + i * BLOCK

    def narrow(source, target):
        def step(at, i):
            del i
            target[at] = source[at].astype(LOW)

        by_rows(step)

    def row_mask(i):
        row, mask = rows_of(i), jnp.zeros((BLOCK, 1), FULL)
        for page in range(pages):
            first = page * KEPT
            mask = jnp.where((row >= first) & (row < first + lengths[page]), 1.0, mask)
        return mask

    def keep(i):
        row, kept = rows_of(i), jnp.zeros((BLOCK, 1), FULL)
        for page in range(pages):
            kept = jnp.where(row >= page * KEPT, (1 - drops[page]).astype(FULL), kept)
        return kept

    def rows_in(slot):
        return act.at[slot, pl.ds(0, count)]

    def vector(row):
        return vw[row : row + 1, :]

    def norm(number, at, values):
        centre = values - jnp.mean(values, axis=-1, keepdims=True)
        inverse = lax.rsqrt(jnp.mean(centre * centre, axis=-1, keepdims=True) + EPSILON)
        plain = centre * inverse
        unit[number, at] = plain.astype(LOW)
        inv[number, at] = inverse
        return plain * vector(2 * number) + vector(2 * number + 1)

    def fold(values):
        return jnp.sum(values.reshape(BLOCK // 8, 8, width), axis=0)

    def norm_back(number, grad, after):
        part[...] = jnp.zeros_like(part)

        def step(at, i):
            value = grad(at)
            plain = unit[number, at].astype(FULL)
            part[0] += fold(value * plain)
            part[1] += fold(value)
            scaled = value * vector(2 * number)
            inner = (
                scaled
                - jnp.mean(scaled, axis=-1, keepdims=True)
                - plain * jnp.mean(scaled * plain, axis=-1, keepdims=True)
            )
            result = inv[number, at] * inner
            grd[at] = result
            after(at, i, result)

        by_rows(step)
        for i in range(2):
            vg[2 * number + i : 2 * number + i + 1, :] = jnp.sum(part[i], axis=0, keepdims=True)

    def split_heads(values):
        first = lax.broadcasted_iota(jnp.int32, values.shape, 1) < HEAD
        zero = jnp.zeros_like(values)
        return jnp.concatenate([jnp.where(first, values, zero), jnp.where(first, zero, values)], axis=0)

    def join_heads(values):
        first = lax.broadcasted_iota(jnp.int32, (KEPT, PAIR), 1) < HEAD
        return jnp.where(first, values[:KEPT], values[KEPT:])

    def by_heads(half, body):
        group = 3

        def step(i):
            page = i // (pairs // group)
            start = pl.multiple_of(page * KEPT, KEPT)
            at, keys_at = pl.ds(start, KEPT), pl.ds(start, slots)
            for j in range(group):
                pair = (i % (pairs // group)) * group + j
                lanes = pl.ds(pl.multiple_of(pair * PAIR, PAIR), PAIR)
                body(page, at, keys_at, lanes, i * group + j)

        steps = pages * (pairs // group)
        loop(half * (steps // 2), steps if half else steps // 2, step)

    def attend(half, which, query, keys, values, result):
        def body(page, at, keys_at, lanes, number):
            scores = times_transposed(split_heads(act[query, at, lanes]), act[keys, keys_at, lanes]) * scale
            spot = lax.broadcasted_iota(jnp.int32, scores.shape, 1)
            scores = jnp.where(spot < lengths[page], scores, -1e30)
            weights = jnp.exp(scores - jnp.max(scores, axis=-1, keepdims=True))
            chance = weights * (1.0 / jnp.sum(weights, axis=-1, keepdims=True))
            chance = chance.astype(LOW)
            probs[which, number] = chance
            act[result, at, lanes] = join_heads(times(chance, act[values, keys_at, lanes])).astype(LOW)

        by_heads(half, body)

    def attend_back(half, which, query, keys, values):
        grad, to_query, to_keys, to_values = free(0), spare(0), spare(1), spare(2)

        def body(page, at, keys_at, lanes, number):
            del page
            chance = probs[which, number]
            spread = split_heads(grad[at, lanes])
            pull = times_transposed(spread, act[values, keys_at, lanes])
            wide_chance = chance.astype(FULL)
            inner = pull - jnp.sum(pull * wide_chance, axis=-1, keepdims=True)
            delta = (wide_chance * inner).astype(LOW)
            to_query[at, lanes] = (join_heads(times(delta, act[keys, keys_at, lanes])) * scale).astype(LOW)
            key_grad = outer(delta, split_heads(act[query, at, lanes]))[:KEPT]
            to_keys[at, lanes] = (key_grad * scale).astype(LOW)
            to_values[at, lanes] = outer(chance, spread)[:KEPT].astype(LOW)

        by_heads(half, body)

    def square_grad(group, index, left, right):
        sq[group, :, :, index] = outer(left, right).astype(LOW).reshape(LINE, PLANE, rows, width)

    def view(item):
        if item is VECTORS:
            return lambda z, q: vecs.at[z, q]
        group, start, size = item
        return lambda z, q, first=0, some=size: sq.at[group, z, q, pl.ds(start + first, some)]

    def outputs(item):
        group, start, size = item
        places = []
        for i in range(start, start + size):
            if group == JOIN:
                places.append(join_g.at[i])
            elif group == KV_CROSS:
                places.append(proj_g.at[1 + i])
            elif group == QK_SELF:
                places.append(proj_g.at[3 + i])
            elif i == 1:
                places.append(out_g.at[0 if group == QO_CROSS else 1])
            else:
                places.append(proj_g.at[0 if group == QO_CROSS else 5])
        return places

    def put_for(item):
        if item is VECTORS:
            return PutVectors(vec_g)
        first = 2 * item[0] + item[1]
        return Put(lambda i: work.at[pl.ds((first + i) * rows, rows)], outputs(item), store_sems, first)

    used = {}

    def gather(item, by=GatherByLine):
        return by(view(item), k)

    def keep_scatter(item):
        scatters.append(item)
        return item

    def scatter(item, straight=False):
        if item is VECTORS:
            room = VectorRoom(0, vcorners, vsides, vlines, vhop, used)
        else:
            room = Room(item[2], corners, sides, lines, hops, used)
        return keep_scatter(ScatterByPlane(view(item), room, put_for(item), k, straight))

    def out_view(z, y):
        return wd.at[z, y]

    def in_view(z, y):
        return fi.at[z, pl.ds(2 * y, 2)]

    def stage_of(first):
        return lambda i: work.at[pl.ds((first + i) * rows, rows)]

    class PutOut(Put):
        def sums(self, values):
            for i in range(4):
                self.stage(i)[...] = values[i // 2, i % 2]

    class PutIn(Put):
        def sums(self, values):
            for i in range(4):
                self.stage(i)[...] = values[i // 2, i % 2]

        def two_rows(self, first, x_):
            return work.at[pl.ds(pl.multiple_of((first + 2 * x_) * rows, rows), 2 * rows)]

        def half(self, h, block):
            return work[(2 * h + block) * rows : (2 * h + block + 1) * rows]

        def store(self):
            self.two_rows(0, k.xx)[...] = self.two_rows(FFN_IN_ROWS, k.xx)[...]
            other = self.two_rows(FFN_IN_ROWS, 1 - k.xx)[...]
            halves[0] = other.astype(LOW).reshape(2, rows, width)
            self.swap = k.send(halves.at[0], halves.at[1], k.x)

        def G(self):
            self.swap.wait()
            other = halves[1].astype(FULL).reshape(2 * rows, width)
            self.two_rows(0, 1 - k.xx)[...] = other
            piece = width // 4
            for j in range(4):
                block, first = j // 2, (j % 2) * 2 * piece
                parts = [
                    self.half(h, block)[:, first + g * piece : first + (g + 1) * piece]
                    for g in range(2)
                    for h in range(2)
                ]
                self.stage(j)[...] = jnp.concatenate(parts, axis=1)
            Put.store(self)

    scatters = []
    pair_room = Room(2, corners, sides, pair_lines, pair_hops, used)
    put_out = PutOut(
        stage_of(FFN_OUT_ROWS),
        [fout_g.at[pl.ds(i * rows, rows)] for i in range(4)],
        store_sems,
        FFN_OUT_ROWS,
    )
    put_in = PutIn(
        stage_of(FFN_IN_ROWS),
        [fin_g.at[:, pl.ds(i * width, width)] for i in range(4)],
        store_sems,
        FFN_IN_ROWS,
    )
    gFO = PairGatherByPlane(out_view, k)
    gFI = PairGatherByLine(in_view, k, lambda: swaps["in"])
    sFO = keep_scatter(PairScatterByLine(out_view, side_room, pair_room, put_out, k))
    sFI = keep_scatter(PairScatterByPlane(in_view, pair_room, put_in, k))
    gK = gather(ITEMS[0])
    gV = gather(ITEMS[1])
    gQO = gather(ITEMS[2])
    gQK = gather(ITEMS[3])
    gVO = gather(ITEMS[4])
    gJ = gather(ITEMS[5], GatherByPlane)
    gvec = gather(VECTORS)
    sK = scatter(ITEMS[0])
    sV = scatter(ITEMS[1])
    sQO = scatter(ITEMS[2])
    sQK = scatter(ITEMS[3])
    sVO = scatter(ITEMS[4])
    sJ0 = scatter(ITEMS[6])
    sJ1 = scatter(ITEMS[7])
    svec = scatter(VECTORS)
    swaps = {}

    def swap(name, source, target, peer=None):
        swaps[name] = k.send(source, target, k.twin if peer is None else peer)

    def swapped(*names):
        for name in names:
            swaps[name].wait()

    sources, first = [], 0
    for shard in (proj, outw, join, fout):
        sources.append((shard, pl.ds(first, shard.shape[0])))
        first += shard.shape[0]
    for j in range(4):
        sources.append((fin.at[:, pl.ds(j * width, width)], pl.ds(first, rows)))
        first += rows
    loads = [
        pltpu.make_async_copy(source, work.at[at], load_sems.at[i])
        for i, (source, at) in enumerate(sources)
    ]

    page_loads = [
        pltpu.make_async_copy(
            source.at[page, pl.ds(0, KEPT)],
            target.at[pl.ds(page * KEPT, KEPT)],
            page_sems.at[number * pages + page],
        )
        for number, (source, target) in enumerate(((x_in, x), (cot_in, cot)))
        for page in range(pages)
    ]
    page_copies = []

    def pages_out(source, target, number):
        for page in range(pages):
            for i, (piece, at) in enumerate(
                (
                    (source.at[pl.ds(page * KEPT, KEPT)], pl.ds(0, KEPT)),
                    (nothing, pl.ds(KEPT, slots - KEPT)),
                )
            ):
                sem = page_sems.at[2 * pages + (number * pages + page) * 2 + i]
                copy = pltpu.make_async_copy(piece, target.at[page, at], sem)
                copy.start()
                page_copies.append(copy)

    def cast(number):
        return work[number * rows : (number + 1) * rows].astype(LOW)

    def place(*blocks):
        for group, index, number in blocks:
            sq[group, k.z, k.q, index] = cast(number)

    def place_out():
        for j in range(4):
            wd[k.z, k.yy, j // 2, j % 2] = cast(FFN_OUT_ROWS + j)

    def place_in():
        piece = width // 4
        for h in range(2):
            for block in range(2):
                parts = [
                    cast(FFN_IN_ROWS + 2 * block + j)[:, (2 * g + h) * piece : (2 * g + h + 1) * piece]
                    for j in range(2)
                    for g in range(2)
                ]
                halves[h, block] = jnp.concatenate(parts, axis=1)
        fi[k.z, k.q] = halves[k.xx]
        swap("in", halves.at[1 - k.xx], fi.at[k.z, k.q], k.x)

    def start():
        k.greet()
        for copy in loads + page_loads:
            copy.start()
        vecs[k.z, k.q] = jnp.zeros(vecs.shape[2:], FULL)
        for row in range(vec.shape[0]):
            vecs[k.z, k.q, row : row + 1, :rows] = vec[row]
        loads[0].wait()
        place((KV_CROSS, 0, 1), (KV_CROSS, 1, 2))
        k.met()

    def cast1():
        loads[2].wait()
        loads[3].wait()
        place((JOIN, 0, 8), (JOIN, 1, 9))
        place_out()

    def cast2():
        for copy in (loads[1], *loads[4:], *page_loads):
            copy.wait()
        place((QO_CROSS, 0, 0), (QO_CROSS, 1, 6), (QK_SELF, 0, 3), (QK_SELF, 1, 4))
        place((VO_SELF, 0, 5), (VO_SELF, 1, 7))
        place_in()
        nothing[...] = jnp.zeros_like(nothing)
        for one in (k1, v1, k2, v2):
            act[one, pl.ds(count, slots - KEPT)] = jnp.zeros((slots - KEPT, width), LOW)

    def kv0():
        free(0)[...] = times(x[...], weight(KV_CROSS, 0)).astype(LOW)
        swap("keys", free(0), rows_in(k1))

    def kv1():
        free(1)[...] = times(x[...], weight(KV_CROSS, 1)).astype(LOW)
        swap("values", free(1), rows_in(v1))

    def vectors():
        sums = jnp.zeros((8, width), FULL)
        zeros = jnp.zeros((8, width - 128), FULL)
        for d in range(RANKS):
            tile = jnp.concatenate([vecs[d // PLANE, d % PLANE], zeros], axis=1)
            sums = sums + (pltpu.roll(tile, d * rows, 1) if d else tile)
        vw[...] = sums.astype(LOW).astype(FULL)

    def project_q1():
        rows_in(q1)[...] = times(x[...], weight(QO_CROSS, 0)).astype(LOW)
        swapped("keys", "values")

    def ln1():
        acc[...] = times(rows_in(o1)[...], weight(QO_CROSS, 1))

        def step(at, i):
            value = norm(0, at, x[at].astype(FULL) + acc[at] * keep(i))
            res[at] = value
            act[h1, at] = value.astype(LOW)

        by_rows(step)

    def project_self(slot_, group, index):
        rows_in(slot_)[...] = times(rows_in(h1)[...], weight(group, index)).astype(LOW)

    def in_two(step, name, buffer, target, peer):
        half = (count // BLOCK + 1) // 2
        for number, first, last in ((0, 0, half), (1, half, count // BLOCK)):
            by_rows(step, first, last)
            at = pl.ds(first * BLOCK, (last - first) * BLOCK)
            swap((name, number), buffer.at[at], target.at[at], peer)

    def ln2():
        acc[...] = times(rows_in(o2)[...], weight(VO_SELF, 1))

        def step(at, i):
            del i
            value = norm(1, at, res[at] + acc[at])
            res[at] = value
            h2a[at] = value.astype(LOW)

        in_two(step, H2, h2a, h2a.at[theirs], k.x)

    def ffn_in(whose, block):
        if whose is theirs and block == 0:
            swapped((H2, 0), (H2, 1))
        first = 0 if whose is mine else count
        acc[...] = times(h2a[whose], in_weight(block))

        def step(at, i):
            value = acc[at]
            share = 0.5 + 0.5 * lax.erf(value * (0.5**0.5))
            bell = jnp.exp(value * value * -0.5) * (1.0 / (2.0 * math.pi) ** 0.5)
            to = pl.ds(pl.multiple_of(first + i * BLOCK, BLOCK), BLOCK)
            mid[block, to] = (value * share).astype(LOW)
            slope[block, to] = (share + value * bell).astype(LOW)

        by_rows(step)

    def ffn_out_theirs():
        acc[...] = times(mid[0, theirs], out_weight(0))
        acc[...] += times(mid[1, theirs], out_weight(1))
        narrow(acc, rows_in(edge))
        swap(FFN, rows_in(edge), rows_in(back), k.x)

    def ffn_out_mine():
        for block in range(2):
            res[...] += times(mid[block, mine], out_weight(block))

    def ln3():
        swapped(FFN)

        def step(at, i):
            del i
            value = res[at] + act[back, at].astype(FULL)
            act[state, at] = norm(2, at, value).astype(LOW)

        in_two(step, STATE, rows_in(state), rows_in(far), k.twin)

    def join_own():
        acc[...] = times(rows_in(state)[...], weight(JOIN, 0))

    def join_far():
        swapped((STATE, 0), (STATE, 1))
        acc[...] += times(rows_in(far)[...], weight(JOIN, 1))

    def gate():
        part[...] = jnp.zeros_like(part)

        def step(at, i):
            own = act[state, at].astype(FULL)
            other = act[far, at].astype(FULL)
            share = jax.nn.sigmoid(acc[at] + vector(6))
            mask = row_mask(i)
            grad = cot[at].astype(FULL) * mask
            cot[at] = ((share * own + (1.0 - share) * other) * mask).astype(LOW)
            to_own, to_other = grad * share, grad * (1.0 - share)
            logits = (to_own * (own - other) * (1.0 - share)).astype(LOW)
            ea[at] = logits
            part[0] += fold(logits.astype(FULL))
            res[at] = to_own
            grd[at] = to_other

        by_rows(step)
        vg[6:7, :] = jnp.sum(part[0], axis=0, keepdims=True)
        vg[7:8, :] = jnp.zeros((1, width), FULL)
        pages_out(cot, joined, 0)

    def join_back():
        logits = ea.at[mine]
        rows_in(edge)[...] = (grd[...] + times_transposed(logits[...], weight(JOIN, 1))).astype(LOW)
        swap("edge", rows_in(edge), rows_in(back))
        square_grad(JOIN, 1, rows_in(far)[...], logits[...])

    def join_back_own():
        logits = ea.at[mine]
        res[...] += times_transposed(logits[...], weight(JOIN, 0))
        square_grad(JOIN, 0, rows_in(state)[...], logits[...])

    def keep_err(at, i, result):
        del i
        ea[at] = result.astype(LOW)

    def keep_branch(at, i, result):
        ea[at] = (result * keep(i)).astype(LOW)

    def ln3_back():
        swapped("edge")
        norm_back(2, lambda at: res[at] + act[back, at].astype(FULL), keep_err)
        swap(ERR, ea.at[mine], ea.at[theirs], k.x)

    def hidden_back(whose, block):
        if whose is theirs and block == 0:
            swapped(ERR)
        first = 0 if whose is mine else count
        acc[...] = times_transposed(ea[whose], out_weight(block))

        def step(at, i):
            to = pl.ds(pl.multiple_of(first + i * BLOCK, BLOCK), BLOCK)
            slope[block, to] = (acc[at] * slope[block, to].astype(FULL)).astype(LOW)

        by_rows(step)

    def out_grad(block):
        for at in TILES:
            grad = outer(mid[block], ea[:, at]).astype(LOW)
            wd[2 * block : 2 * block + 2, :, :, :, :, at] = grad.reshape(2, 2, 2, 2, rows, TILE)
        if block == 1:
            pl.semaphore_signal(ready, inc=1, device_id=k.twin, device_id_type=MESH)

    def ffn_in_back_theirs():
        acc[...] = times_transposed(slope[0, theirs], in_weight(0))
        acc[...] += times_transposed(slope[1, theirs], in_weight(1))
        narrow(acc, rows_in(edge))
        swap(FFN_BACK, rows_in(edge), rows_in(far), k.x)

    def ffn_in_back_mine():
        for block in range(2):
            grd[...] += times_transposed(slope[block, mine], in_weight(block))

    def in_grad(block):
        for at in TILES:
            grad = outer(h2a[...], slope[block, :, at]).astype(LOW)
            fi[:, :, block, :, at] = grad.reshape(LINE, PLANE, rows, TILE)

    def ln2_back():
        swapped(FFN_BACK)
        norm_back(1, lambda at: grd[at] + act[far, at].astype(FULL), keep_err)
        free(0)[...] = times_transposed(ea[mine], weight(VO_SELF, 1)).astype(LOW)
        square_grad(VO_SELF, 1, rows_in(o2)[...], ea[mine])

    def self_back(group, index, which):
        grd[...] += times_transposed(spare(which)[...], weight(group, index))
        square_grad(group, index, rows_in(h1)[...], spare(which)[...])

    def ln1_back():
        norm_back(0, lambda at: grd[at], keep_branch)
        for d in range(RANKS):
            moved = pltpu.roll(vg[...], width - d * rows, 1) if d else vg[...]
            vecs[d // PLANE, d % PLANE] = moved[:, :128]
        free(0)[...] = times_transposed(ea[mine], weight(QO_CROSS, 1)).astype(LOW)
        square_grad(QO_CROSS, 1, rows_in(o1)[...], ea[mine])

    def cross_query_back():
        pl.semaphore_wait(ready, 1)
        swap("back_keys", spare(1), free(2))
        swap("back_values", spare(2), free(3))
        grd[...] += times_transposed(spare(0)[...], weight(QO_CROSS, 0))
        square_grad(QO_CROSS, 0, x[...], spare(0)[...])

    def cross_back(index):
        swapped(("back_keys", "back_values")[index])
        grd[...] += times_transposed(free(2 + index)[...], weight(KV_CROSS, index))
        square_grad(KV_CROSS, index, x[...], free(2 + index)[...])

    def last_cross_back():
        cross_back(1)
        narrow(grd, ea)
        pages_out(ea.at[mine], x_grad, 1)

    start(); gV.L(); gvec.L(); cast1(); gJ.X(); gK.L(); gFO.X(); cast2(); gV.R(); gvec.R(); gQO.L(); gK.R(); gV.X()
    gvec.X(); gK.X(); gQK.L(); gJ.C(); gVO.L(); gV.C(); gvec.C(); gK.C(); gQO.R(); gQO.X(); gK.F(); gFI.L(); kv0()
    gV.F(); gvec.F(); vectors(); gQK.R(); gQK.X(); gQO.C(); gVO.R(); gFI.R(); gFO.L(0); gJ.L(2); kv1(); gVO.X()
    gQO.F(); gQK.C(); gFO.L(1); gVO.C(); project_q1(); attend(0, 0, q1, k1, v1, o1); gFI.X(); gQK.F()
    attend(1, 0, q1, k1, v1, o1); gJ.L(3); ln1(); project_self(q2, QK_SELF, 0); gFO.R(0); gVO.F()
    project_self(k2, QK_SELF, 1); project_self(v2, VO_SELF, 0); attend(0, 1, q2, k2, v2, o2)
    attend(1, 1, q2, k2, v2, o2); ln2(); gJ.L(1); gFO.R(1); gJ.L(0); gFI.F(); ffn_in(mine, 0); gJ.R(3)
    ffn_in(mine, 1); ffn_in(theirs, 0); ffn_in(theirs, 1); gFO.F(); gJ.R(2); ffn_out_theirs(); ffn_out_mine()
    gJ.R(0); gJ.R(1); ln3(); gJ.F(); join_own(); join_far(); gate(); join_back(); sJ1.C(); join_back_own()
    ln3_back(); hidden_back(mine, 1); hidden_back(mine, 0); ffn_in_back_mine(); sJ1.X(); sJ0.C()
    hidden_back(theirs, 0); hidden_back(theirs, 1); ffn_in_back_theirs(); sJ1.L(); out_grad(0); in_grad(1); sJ0.X()
    sJ1.B(); in_grad(0); sFI.C(); out_grad(1); sFO.L(0); ln2_back(); sFO.L(1); attend_back(0, 1, q2, k2, v2)
    sJ1.F(); attend_back(1, 1, q2, k2, v2); self_back(VO_SELF, 0, 2); sJ0.L(); sVO.C(); sFO.B(0)
    self_back(QK_SELF, 0, 0); self_back(QK_SELF, 1, 1); sFI.L(); sQK.C(); ln1_back(); sFO.B(1)
    attend_back(0, 0, q1, k1, v1); sVO.X(); sJ0.B(); sQK.X(); attend_back(1, 0, q1, k1, v1); sFI.B()
    cross_query_back(); sQO.C(); svec.C(); sJ0.F(); sVO.L(); sQK.L(); cross_back(0); sQO.X(); svec.X(); sQK.B()
    last_cross_back(); sVO.B(); sK.C(); sQO.L(); svec.L(); sFO.M(0); sV.C(); sQO.B(); svec.B(); sK.X(); sV.X()
    sQK.F(); sFO.M(1); sFI.F(); sFO.X(); sK.L(); sV.L(); sK.B(); sFI.G(); sV.B(); sQO.F(); svec.F(); sFO.F(); sK.F()
    sVO.F(); sV.F()
    for copy in page_copies:
        copy.wait()
    for item in scatters:
        for copy in item.put.copies:
            copy.wait()


def hand_over(count, *refs):
    sources, targets, rooms, sems = refs[:count], refs[count : 2 * count], refs[2 * count : -1], refs[-1]
    loads = [
        pltpu.make_async_copy(source, room, sems.at[0, i])
        for i, (source, room) in enumerate(zip(sources, rooms))
    ]
    stores = [
        pltpu.make_async_copy(room, target, sems.at[1, i])
        for i, (room, target) in enumerate(zip(rooms, targets))
    ]
    for copy in loads:
        copy.start()
    for load, copy in zip(loads, stores):
        load.wait()
        copy.start()
    for copy in stores:
        copy.wait()


def run_layer(x_in, lengths, drops, proj, outw, fin, fout, join, vectors, cot):
    pages, slots, width = x_in.shape[1:]
    rows = proj.shape[3]
    count = pages * KEPT
    vec = jnp.transpose(vectors, (1, 0, 2))
    vmem = pl.BlockSpec(memory_space=pltpu.VMEM)
    smem = pl.BlockSpec(memory_space=pltpu.SMEM)
    hbm = pl.BlockSpec(memory_space=pl.ANY)
    slab = (2, rows, width)
    scratch = [
        pltpu.VMEM((SQUARES, LINE, PLANE) + slab, LOW),
        pltpu.VMEM((LINE, PLANE) + slab, LOW),
        pltpu.VMEM((LINE, 2, 2) + slab, LOW),
        pltpu.VMEM((2,) + slab, LOW),
        pltpu.VMEM((LINE, PLANE, 8, 128), FULL),
        pltpu.VMEM((CORNER_RING, 2, HALF) + slab, LOW),
        pltpu.VMEM((SIDE_RING, LINE, 2) + slab, LOW),
        pltpu.VMEM((LINE_RING, LINE - 1) + slab, LOW),
        pltpu.VMEM((HOP_RING,) + slab, LOW),
        pltpu.VMEM((2,) + slab, LOW),
        pltpu.VMEM((PAIR_RING, LINE - 1, 2) + slab, LOW),
        pltpu.VMEM((PAIR_RING, 2) + slab, LOW),
        pltpu.VMEM((2, HALF, 8, 128), FULL),
        pltpu.VMEM((2, LINE, 8, 128), FULL),
        pltpu.VMEM((LINE - 1, 8, 128), FULL),
        pltpu.VMEM((8, 128), FULL),
        pltpu.VMEM((8, width), FULL),
        pltpu.VMEM((8, width), FULL),
        pltpu.VMEM((2, 8, width), FULL),
        pltpu.VMEM((count, width), LOW),
        pltpu.VMEM((count, width), LOW),
        pltpu.VMEM((slots - KEPT, width), LOW),
        pltpu.VMEM((2 * count, width), LOW),
        pltpu.VMEM((2 * count, width), LOW),
        pltpu.VMEM((13, count + slots - KEPT, width), LOW),
        pltpu.VMEM((2, 2 * count, width), LOW),
        pltpu.VMEM((2, 2 * count, width), LOW),
        pltpu.VMEM((2, pages * (width // PAIR), 2 * KEPT, slots), LOW),
        pltpu.VMEM((3, count, width), LOW),
        pltpu.VMEM((3, count, 1), FULL),
        pltpu.VMEM((3 * count, width), FULL),
        pltpu.SemaphoreType.DMA((8,)),
        pltpu.SemaphoreType.DMA((6 * pages,)),
        pltpu.SemaphoreType.DMA((18,)),
        pltpu.SemaphoreType.DMA((TRANSFERS,)),
        pltpu.SemaphoreType.DMA((TRANSFERS,)),
        pltpu.SemaphoreType.REGULAR,
    ]
    shapes = (
        ((pages, slots, width), LOW),
        ((pages, slots, width), LOW),
        ((6, rows, width), FULL),
        ((2, rows, width), FULL),
        ((rows, 4 * width), FULL),
        ((4 * rows, width), FULL),
        ((2, rows, width), FULL),
        ((vectors.shape[1], 1, rows), FULL),
    )
    results = pl.pallas_call(
        partial(layer_kernel, rows),
        out_shape=[jax.ShapeDtypeStruct(*shape) for shape in shapes],
        in_specs=[smem, smem] + [hbm] * 7 + [vmem],
        out_specs=[hbm] * 7 + [vmem],
        scratch_shapes=scratch,
        compiler_params=pltpu.CompilerParams(
            collective_id=0, has_side_effects=True, vmem_limit_bytes=VMEM_LIMIT
        ),
    )(
        lengths,
        drops,
        x_in[0],
        cot[0],
        proj.reshape(6 * rows, width),
        outw.reshape(2 * rows, width),
        fin[0],
        fout[0],
        join.reshape(2 * rows, width),
        vec,
    )
    results = pl.pallas_call(
        partial(hand_over, len(shapes)),
        out_shape=[jax.ShapeDtypeStruct(*shape) for shape in shapes],
        in_specs=[hbm] * len(shapes),
        out_specs=[hbm] * len(shapes),
        scratch_shapes=[pltpu.VMEM(*shape) for shape in shapes]
        + [pltpu.SemaphoreType.DMA((2, len(shapes)))],
        compiler_params=pltpu.CompilerParams(vmem_limit_bytes=VMEM_LIMIT),
    )(*results)
    joined, x_grad, proj_g, out_g, fin_g, fout_g, join_g, vec_g = results
    return (
        joined[None],
        x_grad[None],
        proj_g.reshape(proj.shape),
        out_g[None],
        fin_g[None],
        fout_g[None],
        join_g[None],
        jnp.transpose(vec_g, (1, 0, 2)),
    )


def fits(ranks, x_in, proj, fout):
    rows, width = proj.shape[3:]
    return (
        ranks == RANKS
        and x_in.shape[1] == 4
        and x_in.shape[2] == 2 * HEAD
        and rows % 16 == 0
        and rows <= 128
        and width == HEADS * HEAD
        and fout.shape[1] == 4 * rows
    )


def swapped(array, axis, stride):
    return lax.ppermute(array, axis, [(i, i ^ 1 << stride) for i in range(lax.axis_size(axis))])


def product(left, right):
    return jnp.dot(left, right, preferred_element_type=jnp.float32)


def outer_sum(left, right):
    return lax.dot_general(
        left, right, (((0,), (0,)), ((), ())), preferred_element_type=jnp.float32
    )


def times_transposed(left, right):
    return lax.dot_general(
        left, right, (((1,), (1,)), ((), ())), preferred_element_type=jnp.float32
    )


def norm_forward(values, gain, shift):
    centre = values - jnp.mean(values, axis=-1, keepdims=True)
    inverse = lax.rsqrt(jnp.mean(centre * centre, axis=-1, keepdims=True) + EPSILON)
    unit = centre * inverse
    return (unit * gain + shift, unit, inverse)


def norm_backward(grad, unit, inverse, gain):
    scaled = grad * gain
    inner = (
        scaled
        - jnp.mean(scaled, axis=-1, keepdims=True)
        - unit * jnp.mean(scaled * unit, axis=-1, keepdims=True)
    )
    return (inverse * inner, jnp.sum(grad * unit, axis=0), jnp.sum(grad, axis=0))


def heads_view(values, pages):
    return values.reshape(pages, values.shape[0] // pages, HEADS, values.shape[1] // HEADS)


def masked_scores(query, keys, key_mask, pages):
    scale = (query.shape[1] // HEADS) ** (-0.5)
    scores = (
        jnp.einsum(
            "pqhe,pkhe->phqk",
            heads_view(query, pages),
            heads_view(keys, pages),
            preferred_element_type=jnp.float32,
        )
        * scale
    )
    return jnp.where(key_mask[:, None, None, :], scores, -1e30)


def attend_forward(query, keys, values, key_mask, pages):
    scores = masked_scores(query, keys, key_mask, pages)
    top = jnp.max(scores, axis=-1, keepdims=True)
    weights = jnp.exp(scores - top)
    total = jnp.sum(weights, axis=-1, keepdims=True)
    probs = (weights / total).astype(jnp.bfloat16)
    mixed = jnp.einsum(
        "phqk,pkhe->pqhe", probs, heads_view(values, pages), preferred_element_type=jnp.float32
    )
    return (mixed.reshape(query.shape).astype(jnp.bfloat16), top + jnp.log(total))


def attend_backward(grad_out, query, keys, values, key_mask, logsum, pages):
    scale = (query.shape[1] // HEADS) ** (-0.5)
    probs = jnp.exp(masked_scores(query, keys, key_mask, pages) - logsum)
    grad_heads = heads_view(grad_out, pages)
    grad_probs = jnp.einsum(
        "pqhe,pkhe->phqk", grad_heads, heads_view(values, pages), preferred_element_type=jnp.float32
    )
    grad_scores = (
        probs * (grad_probs - jnp.sum(grad_probs * probs, axis=-1, keepdims=True))
    ).astype(jnp.bfloat16)
    grad_query = (
        jnp.einsum(
            "phqk,pkhe->pqhe",
            grad_scores,
            heads_view(keys, pages),
            preferred_element_type=jnp.float32,
        )
        * scale
    )
    grad_keys = (
        jnp.einsum(
            "phqk,pqhe->pkhe",
            grad_scores,
            heads_view(query, pages),
            preferred_element_type=jnp.float32,
        )
        * scale
    )
    grad_values = jnp.einsum(
        "phqk,pqhe->pkhe",
        probs.astype(jnp.bfloat16),
        grad_heads,
        preferred_element_type=jnp.float32,
    )
    shape = query.shape
    return (
        grad_query.reshape(shape).astype(jnp.bfloat16),
        grad_keys.reshape(shape).astype(jnp.bfloat16),
        grad_values.reshape(shape).astype(jnp.bfloat16),
    )


def local(
    x_in,
    lengths,
    drops,
    proj_master,
    out_master,
    ffn_in_master,
    ffn_out_master,
    join_master,
    vectors,
    cotangent,
):
    if fits(lax.axis_size("dp"), x_in, proj_master, ffn_out_master):
        return run_layer(
            x_in,
            lengths,
            drops,
            proj_master,
            out_master,
            ffn_in_master,
            ffn_out_master,
            join_master,
            vectors,
            cotangent,
        )
    pages = x_in.shape[1]
    slots = x_in.shape[2]
    width = x_in.shape[3]
    rows = pages * slots
    gathered = (
        lax.all_gather(proj_master.astype(jnp.bfloat16), "dp", axis=3, tiled=True),
        lax.all_gather(out_master.astype(jnp.bfloat16), "dp", axis=2, tiled=True),
        lax.all_gather(ffn_in_master.astype(jnp.bfloat16), "dp", axis=1, tiled=True),
        lax.all_gather(ffn_out_master.astype(jnp.bfloat16), "dp", axis=1, tiled=True),
        lax.all_gather(join_master.astype(jnp.bfloat16), "dp", axis=2, tiled=True),
        lax.all_gather(vectors.astype(jnp.bfloat16), "dp", axis=2, tiled=True),
    )
    proj_w = gathered[0][0]
    out_w = gathered[1][0]
    ffin_w = gathered[2][0]
    ffout_w = gathered[3][0]
    join_w = gathered[4][0]
    vec_w = gathered[5][0].astype(jnp.float32)
    key_mask = jnp.arange(slots, dtype=jnp.int32)[None, :] < lengths[:, None]
    row_mask = key_mask.reshape(rows, 1).astype(jnp.float32)
    keep = (1 - drops).astype(jnp.float32)
    keep_rows = jnp.broadcast_to(keep[:, None], (pages, slots)).reshape(rows, 1)
    source = x_in[0].reshape(rows, width)
    own_keys = product(source, proj_w[0, 1]).astype(jnp.bfloat16)
    own_values = product(source, proj_w[0, 2]).astype(jnp.bfloat16)
    far_keys, far_values = swapped((own_keys, own_values), "stream", 0)
    cross_query = product(source, proj_w[0, 0]).astype(jnp.bfloat16)
    cross_out, cross_logsum = attend_forward(cross_query, far_keys, far_values, key_mask, pages)
    first, unit_one, inverse_one = norm_forward(
        source.astype(jnp.float32) + product(cross_out, out_w[0]) * keep_rows, vec_w[0], vec_w[1]
    )
    first_low = first.astype(jnp.bfloat16)
    self_query = product(first_low, proj_w[1, 0]).astype(jnp.bfloat16)
    self_keys = product(first_low, proj_w[1, 1]).astype(jnp.bfloat16)
    self_values = product(first_low, proj_w[1, 2]).astype(jnp.bfloat16)
    self_out, self_logsum = attend_forward(self_query, self_keys, self_values, key_mask, pages)
    second, unit_two, inverse_two = norm_forward(
        first + product(self_out, out_w[1]), vec_w[2], vec_w[3]
    )
    second_low = second.astype(jnp.bfloat16)
    hidden = product(second_low, ffin_w)
    gelu_exact = partial(jax.nn.gelu, approximate=False)
    active_f32, gelu_pull = jax.vjp(gelu_exact, hidden)
    active = active_f32.astype(jnp.bfloat16)
    third, unit_three, inverse_three = norm_forward(
        second + product(active, ffout_w), vec_w[4], vec_w[5]
    )
    state = third.astype(jnp.bfloat16)
    far_state = swapped(state, "stream", 0)
    state_f32 = state.astype(jnp.float32)
    far_f32 = far_state.astype(jnp.float32)
    gate = jax.nn.sigmoid(product(state, join_w[0]) + product(far_state, join_w[1]) + vec_w[6])
    joined = ((gate * state_f32 + (1.0 - gate) * far_f32) * row_mask).astype(jnp.bfloat16)
    grad_joined = cotangent[0].reshape(rows, width).astype(jnp.float32) * row_mask
    grad_logits = (grad_joined * (state_f32 - far_f32) * gate * (1.0 - gate)).astype(jnp.bfloat16)
    grad_join = jnp.stack([outer_sum(state, grad_logits), outer_sum(far_state, grad_logits)])
    grad_bias = jnp.sum(grad_logits.astype(jnp.float32), axis=0)
    grad_far = (grad_joined * (1.0 - gate) + times_transposed(grad_logits, join_w[1])).astype(
        jnp.bfloat16
    )
    returned = swapped(grad_far, "stream", 0)
    grad_third = (
        grad_joined * gate + times_transposed(grad_logits, join_w[0]) + returned.astype(jnp.float32)
    )
    grad_res3, gain_three, shift_three = norm_backward(
        grad_third, unit_three, inverse_three, vec_w[4]
    )
    grad_res3_low = grad_res3.astype(jnp.bfloat16)
    grad_ffout = outer_sum(active, grad_res3_low)
    grad_hidden = gelu_pull(times_transposed(grad_res3_low, ffout_w))[0].astype(jnp.bfloat16)
    grad_ffin = outer_sum(second_low, grad_hidden)
    grad_second = grad_res3 + times_transposed(grad_hidden, ffin_w)
    grad_res2, gain_two, shift_two = norm_backward(grad_second, unit_two, inverse_two, vec_w[2])
    grad_res2_low = grad_res2.astype(jnp.bfloat16)
    grad_out_self = outer_sum(self_out, grad_res2_low)
    grad_self_out = times_transposed(grad_res2_low, out_w[1]).astype(jnp.bfloat16)
    grad_q2, grad_k2, grad_v2 = attend_backward(
        grad_self_out, self_query, self_keys, self_values, key_mask, self_logsum, pages
    )
    grad_proj_self = jnp.stack(
        [
            outer_sum(first_low, grad_q2),
            outer_sum(first_low, grad_k2),
            outer_sum(first_low, grad_v2),
        ]
    )
    grad_first = (
        grad_res2
        + times_transposed(grad_q2, proj_w[1, 0])
        + times_transposed(grad_k2, proj_w[1, 1])
        + times_transposed(grad_v2, proj_w[1, 2])
    )
    grad_res1, gain_one, shift_one = norm_backward(grad_first, unit_one, inverse_one, vec_w[0])
    grad_branch = (grad_res1 * keep_rows).astype(jnp.bfloat16)
    grad_out_cross = outer_sum(cross_out, grad_branch)
    grad_cross_out = times_transposed(grad_branch, out_w[0]).astype(jnp.bfloat16)
    grad_q1, grad_far_keys, grad_far_values = attend_backward(
        grad_cross_out, cross_query, far_keys, far_values, key_mask, cross_logsum, pages
    )
    back_keys, back_values = swapped((grad_far_keys, grad_far_values), "stream", 0)
    grad_proj_cross = jnp.stack(
        [outer_sum(source, grad_q1), outer_sum(source, back_keys), outer_sum(source, back_values)]
    )
    grad_source = (
        grad_res1
        + times_transposed(grad_q1, proj_w[0, 0])
        + times_transposed(back_keys, proj_w[0, 1])
        + times_transposed(back_values, proj_w[0, 2])
    )
    grad_proj = jnp.stack([grad_proj_cross, grad_proj_self])[None]
    grad_out = jnp.stack([grad_out_cross, grad_out_self])[None]
    grad_vectors = jnp.stack(
        [gain_one, shift_one, gain_two, shift_two, gain_three, shift_three, grad_bias]
    )[None]
    all_sums = (
        lax.psum_scatter(grad_proj, "dp", scatter_dimension=3, tiled=True),
        lax.psum_scatter(grad_out, "dp", scatter_dimension=2, tiled=True),
        lax.psum_scatter(grad_ffin[None], "dp", scatter_dimension=1, tiled=True),
        lax.psum_scatter(grad_ffout[None], "dp", scatter_dimension=1, tiled=True),
        lax.psum_scatter(grad_join[None], "dp", scatter_dimension=2, tiled=True),
        lax.psum_scatter(grad_vectors, "dp", scatter_dimension=2, tiled=True),
    )
    proj_part, out_part, ffin_part, ffout_part, join_part, vectors_part = all_sums
    joined_out = joined.reshape(1, pages, slots, width)
    x_grad = grad_source.astype(jnp.bfloat16).reshape(1, pages, slots, width)
    return (joined_out, x_grad, proj_part, out_part, ffin_part, ffout_part, join_part, vectors_part)


def solution(mesh):
    placed = (
        P("stream", "dp", None, None),
        P("dp"),
        P("dp"),
        P("stream", None, None, "dp", None),
        P("stream", None, "dp", None),
        P("stream", "dp", None),
        P("stream", "dp", None),
        P("stream", None, "dp", None),
        P("stream", None, "dp"),
        P("stream", "dp", None, None),
    )
    return jax.shard_map(
        local,
        mesh=mesh,
        in_specs=placed,
        out_specs=(
            P("stream", "dp", None, None),
            P("stream", "dp", None, None),
            P("stream", None, None, "dp", None),
            P("stream", None, "dp", None),
            P("stream", "dp", None),
            P("stream", "dp", None),
            P("stream", None, "dp", None),
            P("stream", None, "dp"),
        ),
        check_vma=False,
    )
```

```python
import math
from functools import partial

import jax
import jax.numpy as jnp
from jax import lax
from jax.experimental import pallas as pl
from jax.experimental.pallas import tpu as pltpu
from jax.sharding import PartitionSpec as P

HEADS = 12

EPSILON = 1e-05
VMEM_LIMIT = 62 * 2**20
TRANSFERS = 300
MESH = pl.DeviceIdType.MESH
LOW = jnp.bfloat16
FULL = jnp.float32
LINE, PLANE = 4, 4
RANKS = LINE * PLANE
HALF = LINE // 2
KV_CROSS, QO_CROSS, QK_SELF, VO_SELF, JOIN = range(5)
SQUARES = 5
FFN_OUT_ROWS, FFN_IN_ROWS = 10, 14
ITEMS = (
    (KV_CROSS, 0, 1),
    (KV_CROSS, 1, 1),
    (QO_CROSS, 0, 2),
    (QK_SELF, 0, 2),
    (VO_SELF, 0, 2),
    (JOIN, 0, 2),
    (JOIN, 0, 1),
    (JOIN, 1, 1),
)
VECTORS = None
H2, FFN, STATE, ERR, FFN_BACK = range(5)
CORNER_RING, SIDE_RING, LINE_RING, HOP_RING, PAIR_RING = 3, 4, 5, 5, 3
BLOCK = 64
KEPT = 112
TILE = 256
TILES = tuple(pl.ds(at, TILE) for at in range(0, 768, TILE))
HEAD = 64
PAIR = 2 * HEAD


class Links:
    def __init__(self, send_sems, recv_sems):
        self.stream = lax.axis_index("stream")
        self.me = lax.axis_index("dp")
        self.z = self.me // PLANE
        self.q = self.me % PLANE
        self.qx = self.q + 1 - 2 * (self.q % 2)
        self.qy = (self.q + 2) % PLANE
        self.qd = PLANE - 1 - self.q
        self.xx, self.yy = self.q % 2, self.q // 2
        self.columns = (self.q, self.qx, self.qy, self.qd)
        self.z_near = self.z + 1 - 2 * (self.z % 2)
        self.z_two = (self.z + 2) % LINE
        self.z_third = LINE - 1 - self.z
        self.middle = (self.z == 1) | (self.z == 2)
        self.x = (self.stream, self.z * PLANE + self.qx)
        self.y = (self.stream, self.z * PLANE + self.qy)
        self.near, self.two, self.third = (
            (self.stream, at * PLANE + self.q) for at in (self.z_near, self.z_two, self.z_third)
        )
        self.twin = (1 - self.stream, self.me)
        self.sems = (send_sems, recv_sems)
        self.used = 0

    def greet(self):
        for peer in (self.x, self.y, self.near, self.two, self.third, self.twin):
            pl.semaphore_signal(
                pltpu.get_barrier_semaphore(), inc=1, device_id=peer, device_id_type=MESH
            )

    def met(self):
        pl.semaphore_wait(pltpu.get_barrier_semaphore(), 6)

    def copy(self, source, target, peer, landing=None):
        number = self.used
        self.used += 1
        return pltpu.make_async_remote_copy(
            src_ref=source,
            dst_ref=target,
            send_sem=self.sems[0].at[number],
            recv_sem=self.sems[1].at[number if landing is None else landing],
            device_id=peer,
            device_id_type=MESH,
        )

    def send(self, source, target, peer):
        copy = self.copy(source, target, peer)
        copy.start()
        return copy


class LineGather:
    def __init__(self, view, links):
        self.view, self.k = view, links

    def launch(self):
        k = self.k
        own = self.view(k.z)
        self.near = k.send(own, own, k.near)
        self.two = k.send(own, own, k.two)
        landing = k.used
        self.third = k.copy(own, own, k.third)
        passed = self.view(k.z_two)
        self.passed = k.copy(passed, passed, k.near, landing)
        pl.when(k.middle)(self.third.start)

    def relay(self):
        self.two.wait_recv()
        pl.when(self.k.middle)(self.passed.start)

    def arrive(self):
        self.near.wait_recv()
        self.third.wait_recv()

    def drain(self):
        self.near.wait_send()
        self.two.wait_send()

        @pl.when(self.k.middle)
        def _():
            self.third.wait_send()
            self.passed.wait_send()


class LineSum:
    def __init__(self, view, room, links, straight=False):
        self.view, self.room, self.k, self.straight = view, room, links, straight

    def launch(self):
        k = self.k
        self.spots, self.hop = self.room()
        self.near = k.send(self.view(k.z_near), self.spots(0), k.near)
        away = self.view(k.z_third)
        self.third = k.copy(away, self.spots(2), k.third)
        if self.straight:
            self.third.start()
            self.two = k.send(self.view(k.z_two), self.spots(1), k.two)
            return
        self.passed = k.copy(away, self.hop, k.near)
        pl.when(k.middle)(self.third.start)
        pl.when(jnp.logical_not(k.middle))(self.passed.start)

    def bridge(self):
        k = self.k
        if self.straight:
            return
        part = self.view(k.z_two)

        @pl.when(k.middle)
        def _():
            self.passed.wait_recv()
            part[...] = total(part, self.hop).astype(part.dtype)

        self.two = k.send(part, self.spots(1), k.two)

    def collect(self, put):
        k = self.k
        self.near.wait_recv()
        self.two.wait_recv()
        terms = [self.view(k.z), self.spots(0), self.spots(1)]
        if self.straight:
            self.third.wait_recv()
            put(total(*terms, self.spots(2)))
            return

        @pl.when(k.middle)
        def _():
            self.third.wait_recv()
            put(total(*terms, self.spots(2)))

        pl.when(jnp.logical_not(k.middle))(lambda: put(total(*terms)))

    def drain(self):
        self.near.wait_send()
        self.two.wait_send()
        if self.straight:
            self.third.wait_send()
            return
        pl.when(self.k.middle)(self.third.wait_send)
        pl.when(jnp.logical_not(self.k.middle))(self.passed.wait_send)


class GatherByLine:
    def __init__(self, view, links):
        self.view, self.k = view, links
        self.line = LineGather(lambda z: view(z, links.q), links)

    def L(self):
        self.line.launch()

    def R(self):
        self.line.relay()

    def X(self):
        k = self.k
        self.line.arrive()
        column = self.view(slice(None), k.q)
        self.sides = [k.send(column, column, k.x), k.send(column, column, k.y)]

    def C(self):
        k = self.k
        for copy in self.sides:
            copy.wait_recv()
        one, two = self.view(slice(0, HALF), k.qx), self.view(slice(HALF, LINE), k.qy)
        self.corners = [k.send(one, one, k.y), k.send(two, two, k.x)]

    def F(self):
        for copy in self.corners:
            copy.wait_recv()
        for copy in self.sides + self.corners:
            copy.wait_send()
        self.line.drain()


class GatherByPlane:
    def __init__(self, view, links, size):
        self.view, self.k, self.size = view, links, size
        self.lines = [
            LineGather(partial(lambda q, z: view(z, q), q), links) for q in links.columns
        ]

    def X(self):
        k = self.k
        own = self.view(k.z, k.q)
        self.sides = [k.send(own, own, k.x), k.send(own, own, k.y)]

    def C(self):
        k = self.k
        for copy in self.sides:
            copy.wait_recv()
        one = self.view(k.z, k.qx, 0, 1)
        self.corners = [k.send(one, one, k.y)]
        if self.size == 2:
            two = self.view(k.z, k.qy, 1, 1)
            self.corners.append(k.send(two, two, k.x))

    def L(self, column):
        if column == 3:
            for copy in self.corners:
                copy.wait_recv()
        self.lines[column].launch()

    def R(self, column):
        self.lines[column].relay()

    def F(self):
        for line in self.lines:
            line.arrive()
        for line in self.lines:
            line.drain()
        for copy in self.sides + self.corners:
            copy.wait_send()


class ScatterByPlane:
    def __init__(self, view, room, put, links, straight):
        self.view, self.room, self.put, self.k = view, room, put, links
        self.line = LineSum(lambda z: view(z, links.q), room.line, links, straight)

    def C(self):
        k = self.k
        self.corners, self.sides = self.room.plane()
        low, high = slice(0, HALF), slice(HALF, LINE)
        self.one = [
            k.send(self.view(low, k.qd), self.corners(0), k.x),
            k.send(self.view(high, k.qd), self.corners(1), k.y),
        ]
        self.two = [
            k.send(self.view(low, k.qx), self.sides(0, low), k.x),
            k.send(self.view(high, k.qy), self.sides(1, high), k.y),
        ]

    def X(self):
        k = self.k
        low, high = slice(0, HALF), slice(HALF, LINE)
        for number, half, q in ((0, low, k.qy), (1, high, k.qx)):
            self.one[number].wait_recv()
            part = self.view(half, q)
            part[...] = total(part, self.corners(number)).astype(part.dtype)
        self.two += [
            k.send(self.view(high, k.qx), self.sides(0, high), k.x),
            k.send(self.view(low, k.qy), self.sides(1, low), k.y),
        ]

    def L(self):
        k = self.k
        for copy in self.two:
            copy.wait_recv()
        part = self.view(slice(None), k.q)
        everything = slice(None)
        part[...] = total(part, self.sides(0, everything), self.sides(1, everything)).astype(part.dtype)
        self.line.launch()

    def B(self):
        self.line.bridge()

    def F(self):
        self.line.collect(self.put.sums)
        self.put.store()
        for copy in self.one + self.two:
            copy.wait_send()
        self.line.drain()


class PairGatherByLine:
    def __init__(self, view, links, first=None):
        self.view, self.k, self.first = view, links, first
        self.line = LineGather(lambda z: view(z, links.yy), links)

    def L(self):
        if self.first is not None:
            self.first().wait_recv()
        self.line.launch()

    def R(self):
        self.line.relay()

    def X(self):
        k = self.k
        self.line.arrive()
        column = self.view(slice(None), k.yy)
        self.side = k.send(column, column, k.y)

    def F(self):
        self.side.wait_recv()
        self.side.wait_send()
        self.line.drain()
        if self.first is not None:
            self.first().wait_send()


class PairGatherByPlane:
    def __init__(self, view, links):
        self.view, self.k = view, links
        self.lines = [
            LineGather(partial(lambda y, z: view(z, y), y), links) for y in (links.yy, 1 - links.yy)
        ]

    def X(self):
        k = self.k
        own = self.view(k.z, k.yy)
        self.side = k.send(own, own, k.y)

    def L(self, row):
        if row == 1:
            self.side.wait_recv()
        self.lines[row].launch()

    def R(self, row):
        self.lines[row].relay()

    def F(self):
        for line in self.lines:
            line.arrive()
        for line in self.lines:
            line.drain()
        self.side.wait_send()


class PairScatterByPlane:
    def __init__(self, view, room, put, links):
        self.view, self.room, self.put, self.k = view, room, put, links
        self.line = LineSum(lambda z: view(z, links.yy), room.line, links)

    def C(self):
        k = self.k
        self.side = self.room.column()
        self.two = k.send(self.view(slice(None), 1 - k.yy), self.side, k.y)

    def L(self):
        k = self.k
        self.two.wait_recv()
        part = self.view(slice(None), k.yy)
        part[...] = total(part, self.side).astype(part.dtype)
        self.line.launch()

    def B(self):
        self.line.bridge()

    def F(self):
        self.line.collect(self.put.sums)
        self.put.store()
        self.two.wait_send()
        self.line.drain()

    def G(self):
        self.put.G()


class PairScatterByLine:
    def __init__(self, view, side, room, put, links):
        self.view, self.side, self.put, self.k = view, side, put, links
        self.rows = (1 - links.yy, links.yy)
        self.lines = [
            LineSum(partial(lambda y, z: view(z, y), y), room.line, links) for y in self.rows
        ]

    def L(self, row):
        self.lines[row].launch()

    def B(self, row):
        self.lines[row].bridge()

    def M(self, row):
        part = self.view(self.k.z, self.rows[row])

        def put(value):
            part[...] = value.astype(part.dtype)

        self.lines[row].collect(put)

    def X(self):
        k = self.k
        self.two = k.send(self.view(k.z, 1 - k.yy), self.side, k.y)

    def F(self):
        k = self.k
        self.two.wait_recv()
        self.put.sums(total(self.view(k.z, k.yy), self.side))
        self.put.store()
        self.two.wait_send()
        for line in self.lines:
            line.drain()


def total(*refs):
    result = refs[0][...].astype(FULL)
    for ref in refs[1:]:
        result = result + ref[...].astype(FULL)
    return result


class Room:
    def __init__(self, size, corners, sides, lines, hops, used):
        self.size, self.used = size, used
        self.corners, self.sides, self.lines, self.hops = corners, sides, lines, hops

    def slot(self, ring):
        number = self.used.setdefault(id(ring), 0)
        self.used[id(ring)] += 1
        return ring.at[number % ring.shape[0]]

    def column(self):
        return self.slot(self.sides)

    def plane(self):
        corners, sides = self.slot(self.corners), self.slot(self.sides)
        some = pl.ds(0, self.size)
        return (lambda n: corners.at[n, :, some]), (lambda n, half: sides.at[half, n, some])

    def line(self):
        lines, hops = self.slot(self.lines), self.slot(self.hops)
        some = pl.ds(0, self.size)
        return (lambda n: lines.at[n, some]), hops.at[some]


class VectorRoom(Room):
    def plane(self):
        return (lambda n: self.corners.at[n]), (lambda n, half: self.sides.at[n, half])

    def line(self):
        return (lambda n: self.lines.at[n]), self.hops


class Put:
    def __init__(self, stage, targets, sems, first):
        self.stage, self.targets, self.sems, self.first = stage, targets, sems, first
        self.copies = []

    def sums(self, values):
        for i in range(len(self.targets)):
            self.stage(i)[...] = values[i]

    def store(self):
        for i, target in enumerate(self.targets):
            copy = pltpu.make_async_copy(self.stage(i), target, self.sems.at[self.first + i])
            copy.start()
            self.copies.append(copy)


class PutVectors:
    def __init__(self, target):
        self.target, self.copies = target, []

    def sums(self, values):
        rows, _, width = self.target.shape
        for row in range(rows):
            self.target[row] = values[row : row + 1, :width]

    def store(self):
        pass


def layer_kernel(
    rows,
    lengths,
    drops,
    x_in,
    cot_in,
    proj,
    outw,
    fin,
    fout,
    join,
    vec,
    joined,
    x_grad,
    proj_g,
    out_g,
    fin_g,
    fout_g,
    join_g,
    vec_g,
    sq,
    fi,
    wd,
    halves,
    vecs,
    corners,
    sides,
    lines,
    hops,
    side_room,
    pair_lines,
    pair_hops,
    vcorners,
    vsides,
    vlines,
    vhop,
    vw,
    vg,
    part,
    x,
    cot,
    nothing,
    h2a,
    ea,
    act,
    mid,
    slope,
    probs,
    unit,
    inv,
    work,
    load_sems,
    page_sems,
    store_sems,
    send_sems,
    recv_sems,
    ready,
):
    k = Links(send_sems, recv_sems)
    width = sq.shape[-1]
    count = x.shape[0]
    pages, slots = x_in.shape[:2]
    pairs = width // PAIR
    scale = HEAD**-0.5
    (k1, v1, q1, o1, h1, q2, k2, v2, o2, state, far, edge, back) = range(13)
    mine, theirs = pl.ds(0, count), pl.ds(count, count)
    acc, res, grd = (work.at[pl.ds(i * count, count)] for i in range(3))

    def weight(group, index):
        return sq[group, :, :, index].reshape(width, width)

    def in_weight(block):
        return fi[:, :, block].reshape(width, width)

    def out_weight(block):
        return wd[2 * block : 2 * block + 2].reshape(width, width)

    def free(slot):
        return mid.at[slot // 2, pl.ds((slot % 2) * count, count)]

    def spare(slot):
        return slope.at[slot // 2, pl.ds((slot % 2) * count, count)]

    def times(left, right):
        return jnp.dot(left, right, preferred_element_type=FULL)

    def times_transposed(left, right):
        return lax.dot_general(left, right, (((1,), (1,)), ((), ())), preferred_element_type=FULL)

    def outer(left, right):
        return lax.dot_general(left, right, (((0,), (0,)), ((), ())), preferred_element_type=FULL)

    def loop(first, last, body):
        def step(i, carry):
            body(i)
            return carry

        lax.fori_loop(first, last, step, 0)

    def by_rows(body, first=0, last=None):
        def step(i):
            body(pl.ds(pl.multiple_of(i * BLOCK, BLOCK), BLOCK), i)

        loop(first, count // BLOCK if last is None else last, step)

    def rows_of(i):
        return lax.broadcasted_iota(jnp.int32, (BLOCK, 1), 0) + i * BLOCK

    def narrow(source, target):
        def step(at, i):
            del i
            target[at] = source[at].astype(LOW)

        by_rows(step)

    def row_mask(i):
        row, mask = rows_of(i), jnp.zeros((BLOCK, 1), FULL)
        for page in range(pages):
            first = page * KEPT
            mask = jnp.where((row >= first) & (row < first + lengths[page]), 1.0, mask)
        return mask

    def keep(i):
        row, kept = rows_of(i), jnp.zeros((BLOCK, 1), FULL)
        for page in range(pages):
            kept = jnp.where(row >= page * KEPT, (1 - drops[page]).astype(FULL), kept)
        return kept

    def rows_in(slot):
        return act.at[slot, pl.ds(0, count)]

    def vector(row):
        return vw[row : row + 1, :]

    def norm(number, at, values):
        centre = values - jnp.mean(values, axis=-1, keepdims=True)
        inverse = lax.rsqrt(jnp.mean(centre * centre, axis=-1, keepdims=True) + EPSILON)
        plain = centre * inverse
        unit[number, at] = plain.astype(LOW)
        inv[number, at] = inverse
        return plain * vector(2 * number) + vector(2 * number + 1)

    def fold(values):
        return jnp.sum(values.reshape(BLOCK // 8, 8, width), axis=0)

    def norm_back(number, grad, after, run=None):
        part[...] = jnp.zeros_like(part)

        def step(at, i):
            value = grad(at)
            plain = unit[number, at].astype(FULL)
            part[0] += fold(value * plain)
            part[1] += fold(value)
            scaled = value * vector(2 * number)
            inner = (
                scaled
                - jnp.mean(scaled, axis=-1, keepdims=True)
                - plain * jnp.mean(scaled * plain, axis=-1, keepdims=True)
            )
            result = inv[number, at] * inner
            grd[at] = result
            after(at, i, result)

        (by_rows if run is None else run)(step)
        for i in range(2):
            vg[2 * number + i : 2 * number + i + 1, :] = jnp.sum(part[i], axis=0, keepdims=True)

    def split_heads(values):
        first = lax.broadcasted_iota(jnp.int32, values.shape, 1) < HEAD
        zero = jnp.zeros_like(values)
        return jnp.concatenate([jnp.where(first, values, zero), jnp.where(first, zero, values)], axis=0)

    def join_heads(values):
        first = lax.broadcasted_iota(jnp.int32, (KEPT, PAIR), 1) < HEAD
        return jnp.where(first, values[:KEPT], values[KEPT:])

    def by_heads(half, body):
        group = 3

        def step(i):
            page = i // (pairs // group)
            start = pl.multiple_of(page * KEPT, KEPT)
            at, keys_at = pl.ds(start, KEPT), pl.ds(start, slots)
            for j in range(group):
                pair = (i % (pairs // group)) * group + j
                lanes = pl.ds(pl.multiple_of(pair * PAIR, PAIR), PAIR)
                body(page, at, keys_at, lanes, i * group + j)

        steps = pages * (pairs // group)
        loop(half * (steps // 2), steps if half else steps // 2, step)

    def attend(half, which, query, keys, values, result):
        def body(page, at, keys_at, lanes, number):
            scores = times_transposed(split_heads(act[query, at, lanes]), act[keys, keys_at, lanes]) * scale
            spot = lax.broadcasted_iota(jnp.int32, scores.shape, 1)
            scores = jnp.where(spot < lengths[page], scores, -1e30)
            weights = jnp.exp(scores - jnp.max(scores, axis=-1, keepdims=True))
            chance = weights * (1.0 / jnp.sum(weights, axis=-1, keepdims=True))
            chance = chance.astype(LOW)
            probs[which, number] = chance
            act[result, at, lanes] = join_heads(times(chance, act[values, keys_at, lanes])).astype(LOW)

        by_heads(half, body)

    def attend_back(half, which, query, keys, values):
        grad, to_query, to_keys, to_values = free(0), spare(0), spare(1), spare(2)

        def body(page, at, keys_at, lanes, number):
            del page
            chance = probs[which, number]
            spread = split_heads(grad[at, lanes])
            pull = times_transposed(spread, act[values, keys_at, lanes])
            wide_chance = chance.astype(FULL)
            inner = pull - jnp.sum(pull * wide_chance, axis=-1, keepdims=True)
            delta = (wide_chance * inner).astype(LOW)
            to_query[at, lanes] = (join_heads(times(delta, act[keys, keys_at, lanes])) * scale).astype(LOW)
            key_grad = outer(delta, split_heads(act[query, at, lanes]))[:KEPT]
            to_keys[at, lanes] = (key_grad * scale).astype(LOW)
            to_values[at, lanes] = outer(chance, spread)[:KEPT].astype(LOW)

        by_heads(half, body)

    def square_grad(group, index, left, right):
        sq[group, :, :, index] = outer(left, right).astype(LOW).reshape(LINE, PLANE, rows, width)

    def view(item):
        if item is VECTORS:
            return lambda z, q: vecs.at[z, q]
        group, start, size = item
        return lambda z, q, first=0, some=size: sq.at[group, z, q, pl.ds(start + first, some)]

    def outputs(item):
        group, start, size = item
        places = []
        for i in range(start, start + size):
            if group == JOIN:
                places.append(join_g.at[i])
            elif group == KV_CROSS:
                places.append(proj_g.at[1 + i])
            elif group == QK_SELF:
                places.append(proj_g.at[3 + i])
            elif i == 1:
                places.append(out_g.at[0 if group == QO_CROSS else 1])
            else:
                places.append(proj_g.at[0 if group == QO_CROSS else 5])
        return places

    def put_for(item):
        if item is VECTORS:
            return PutVectors(vec_g)
        first = 2 * item[0] + item[1]
        return Put(lambda i: work.at[pl.ds((first + i) * rows, rows)], outputs(item), store_sems, first)

    used = {}

    def gather(item):
        return GatherByLine(view(item), k)

    def gather_by_plane(item):
        return GatherByPlane(view(item), k, item[2])

    def keep_scatter(item):
        scatters.append(item)
        return item

    def scatter(item, straight=False):
        if item is VECTORS:
            room = VectorRoom(0, vcorners, vsides, vlines, vhop, used)
        else:
            room = Room(item[2], corners, sides, lines, hops, used)
        return keep_scatter(ScatterByPlane(view(item), room, put_for(item), k, straight))

    def out_view(z, y):
        return wd.at[z, y]

    def in_view(z, y):
        return fi.at[z, pl.ds(2 * y, 2)]

    def stage_of(first):
        return lambda i: work.at[pl.ds((first + i) * rows, rows)]

    class PutOut(Put):
        def sums(self, values):
            for i in range(4):
                self.stage(i)[...] = values[i // 2, i % 2]

    class PutIn(Put):
        def sums(self, values):
            for i in range(4):
                self.stage(i)[...] = values[i // 2, i % 2]

        def two_rows(self, first, x_):
            return work.at[pl.ds(pl.multiple_of((first + 2 * x_) * rows, rows), 2 * rows)]

        def half(self, h, block):
            return work[(2 * h + block) * rows : (2 * h + block + 1) * rows]

        def store(self):
            self.two_rows(0, k.xx)[...] = self.two_rows(FFN_IN_ROWS, k.xx)[...]
            other = self.two_rows(FFN_IN_ROWS, 1 - k.xx)[...]
            halves[0] = other.astype(LOW).reshape(2, rows, width)
            self.swap = k.send(halves.at[0], halves.at[1], k.x)

        def G(self):
            self.swap.wait()
            other = halves[1].astype(FULL).reshape(2 * rows, width)
            self.two_rows(0, 1 - k.xx)[...] = other
            piece = width // 4
            for j in range(4):
                block, first = j // 2, (j % 2) * 2 * piece
                parts = [
                    self.half(h, block)[:, first + g * piece : first + (g + 1) * piece]
                    for g in range(2)
                    for h in range(2)
                ]
                self.stage(j)[...] = jnp.concatenate(parts, axis=1)
            Put.store(self)

    scatters = []
    pair_room = Room(2, corners, sides, pair_lines, pair_hops, used)
    put_out = PutOut(
        stage_of(FFN_OUT_ROWS),
        [fout_g.at[pl.ds(i * rows, rows)] for i in range(4)],
        store_sems,
        FFN_OUT_ROWS,
    )
    put_in = PutIn(
        stage_of(FFN_IN_ROWS),
        [fin_g.at[:, pl.ds(i * width, width)] for i in range(4)],
        store_sems,
        FFN_IN_ROWS,
    )
    gFO = PairGatherByPlane(out_view, k)
    gFI = PairGatherByLine(in_view, k, lambda: swaps["in"])
    sFO = keep_scatter(PairScatterByLine(out_view, side_room, pair_room, put_out, k))
    sFI = keep_scatter(PairScatterByPlane(in_view, pair_room, put_in, k))
    gK = gather(ITEMS[0])
    gV = gather(ITEMS[1])
    gQO = gather(ITEMS[2])
    gQK = gather(ITEMS[3])
    gVO = gather(ITEMS[4])
    gJ = gather_by_plane(ITEMS[5])
    gvec = gather(VECTORS)
    sK = scatter(ITEMS[0])
    sV = scatter(ITEMS[1])
    sQO = scatter(ITEMS[2])
    sQK = scatter(ITEMS[3])
    sVO = scatter(ITEMS[4])
    sJ0 = scatter(ITEMS[6])
    sJ1 = scatter(ITEMS[7])
    svec = scatter(VECTORS)
    swaps = {}

    def swap(name, source, target, peer=None):
        swaps[name] = k.send(source, target, k.twin if peer is None else peer)

    def swapped(*names):
        for name in names:
            swaps[name].wait()

    sources, first = [], 0
    for shard in (proj, outw, join, fout):
        sources.append((shard, pl.ds(first, shard.shape[0])))
        first += shard.shape[0]
    for j in range(4):
        sources.append((fin.at[:, pl.ds(j * width, width)], pl.ds(first, rows)))
        first += rows
    loads = [
        pltpu.make_async_copy(source, work.at[at], load_sems.at[i])
        for i, (source, at) in enumerate(sources)
    ]

    page_loads = [
        pltpu.make_async_copy(
            source.at[page, pl.ds(0, KEPT)],
            target.at[pl.ds(page * KEPT, KEPT)],
            page_sems.at[number * pages + page],
        )
        for number, (source, target) in enumerate(((x_in, x), (cot_in, cot)))
        for page in range(pages)
    ]
    page_copies = []

    def pages_out(source, target, number):
        for page in range(pages):
            for i, (piece, at) in enumerate(
                (
                    (source.at[pl.ds(page * KEPT, KEPT)], pl.ds(0, KEPT)),
                    (nothing, pl.ds(KEPT, slots - KEPT)),
                )
            ):
                sem = page_sems.at[2 * pages + (number * pages + page) * 2 + i]
                copy = pltpu.make_async_copy(piece, target.at[page, at], sem)
                copy.start()
                page_copies.append(copy)

    def cast(number):
        return work[number * rows : (number + 1) * rows].astype(LOW)

    def place(*blocks):
        for group, index, number in blocks:
            sq[group, k.z, k.q, index] = cast(number)

    def place_out():
        for j in range(4):
            wd[k.z, k.yy, j // 2, j % 2] = cast(FFN_OUT_ROWS + j)

    def place_in():
        piece = width // 4
        for h in range(2):
            for block in range(2):
                parts = [
                    cast(FFN_IN_ROWS + 2 * block + j)[:, (2 * g + h) * piece : (2 * g + h + 1) * piece]
                    for j in range(2)
                    for g in range(2)
                ]
                halves[h, block] = jnp.concatenate(parts, axis=1)
        fi[k.z, k.q] = halves[k.xx]
        swap("in", halves.at[1 - k.xx], fi.at[k.z, k.q], k.x)

    def start():
        k.greet()
        for copy in loads + page_loads:
            copy.start()
        vecs[k.z, k.q] = jnp.zeros(vecs.shape[2:], FULL)
        for row in range(vec.shape[0]):
            vecs[k.z, k.q, row : row + 1, :rows] = vec[row]
        loads[0].wait()
        place((KV_CROSS, 0, 1), (KV_CROSS, 1, 2))
        k.met()

    def cast1():
        loads[2].wait()
        loads[3].wait()
        place((JOIN, 0, 8), (JOIN, 1, 9))
        place_out()

    def cast2():
        for copy in (loads[1], *loads[4:], *page_loads):
            copy.wait()
        place((QO_CROSS, 0, 0), (QO_CROSS, 1, 6), (QK_SELF, 0, 3), (QK_SELF, 1, 4))
        place((VO_SELF, 0, 5), (VO_SELF, 1, 7))
        place_in()
        nothing[...] = jnp.zeros_like(nothing)
        for one in (k1, v1, k2, v2):
            act[one, pl.ds(count, slots - KEPT)] = jnp.zeros((slots - KEPT, width), LOW)

    def kv0():
        free(0)[...] = times(x[...], weight(KV_CROSS, 0)).astype(LOW)
        swap("keys", free(0), rows_in(k1))

    def kv1():
        free(1)[...] = times(x[...], weight(KV_CROSS, 1)).astype(LOW)
        swap("values", free(1), rows_in(v1))

    def vectors():
        sums = jnp.zeros((8, width), FULL)
        zeros = jnp.zeros((8, width - 128), FULL)
        for d in range(RANKS):
            tile = jnp.concatenate([vecs[d // PLANE, d % PLANE], zeros], axis=1)
            sums = sums + (pltpu.roll(tile, d * rows, 1) if d else tile)
        vw[...] = sums.astype(LOW).astype(FULL)

    def project_q1():
        rows_in(q1)[...] = times(x[...], weight(QO_CROSS, 0)).astype(LOW)
        swapped("keys", "values")

    def ln1():
        acc[...] = times(rows_in(o1)[...], weight(QO_CROSS, 1))

        def step(at, i):
            value = norm(0, at, x[at].astype(FULL) + acc[at] * keep(i))
            res[at] = value
            act[h1, at] = value.astype(LOW)

        by_rows(step)

    def project_self(slot_, group, index):
        rows_in(slot_)[...] = times(rows_in(h1)[...], weight(group, index)).astype(LOW)

    def in_two(step, name, buffer, target, peer):
        half = (count // BLOCK + 1) // 2
        for number, first, last in ((0, 0, half), (1, half, count // BLOCK)):
            by_rows(step, first, last)
            at = pl.ds(first * BLOCK, (last - first) * BLOCK)
            swap((name, number), buffer.at[at], target.at[at], peer)

    def theirs_in_two(name, result, target):
        half = (count // BLOCK + 1) // 2 * BLOCK
        for number, first, size in ((0, 0, half), (1, half, count - half)):
            at = pl.ds(first, size)
            acc[at] = result(pl.ds(count + first, size))
            act[edge, at] = acc[at].astype(LOW)
            swap((name, number), act.at[edge, at], target.at[at], k.x)

    def ln2():
        acc[...] = times(rows_in(o2)[...], weight(VO_SELF, 1))

        def step(at, i):
            del i
            value = norm(1, at, res[at] + acc[at])
            res[at] = value
            h2a[at] = value.astype(LOW)

        in_two(step, H2, h2a, h2a.at[theirs], k.x)

    def ffn_in(whose, block):
        if whose is theirs and block == 0:
            swapped((H2, 0), (H2, 1))
        first = 0 if whose is mine else count
        acc[...] = times(h2a[whose], in_weight(block))

        def step(at, i):
            value = acc[at]
            share = 0.5 + 0.5 * lax.erf(value * (0.5**0.5))
            bell = jnp.exp(value * value * -0.5) * (1.0 / (2.0 * math.pi) ** 0.5)
            to = pl.ds(pl.multiple_of(first + i * BLOCK, BLOCK), BLOCK)
            mid[block, to] = (value * share).astype(LOW)
            slope[block, to] = (share + value * bell).astype(LOW)

        by_rows(step)

    def ffn_out_theirs():
        def rows_of_result(to):
            return times(mid[0, to], out_weight(0)) + times(mid[1, to], out_weight(1))

        theirs_in_two(FFN, rows_of_result, rows_in(back))

    def ffn_out_mine():
        for block in range(2):
            res[...] += times(mid[block, mine], out_weight(block))

    def ln3():
        swapped((FFN, 0), (FFN, 1))

        def step(at, i):
            del i
            value = res[at] + act[back, at].astype(FULL)
            act[state, at] = norm(2, at, value).astype(LOW)

        in_two(step, STATE, rows_in(state), rows_in(far), k.twin)

    def join_own():
        acc[...] = times(rows_in(state)[...], weight(JOIN, 0))

    def join_far():
        swapped((STATE, 0), (STATE, 1))
        acc[...] += times(rows_in(far)[...], weight(JOIN, 1))

    def gate():
        part[...] = jnp.zeros_like(part)

        def step(at, i):
            own = act[state, at].astype(FULL)
            other = act[far, at].astype(FULL)
            share = jax.nn.sigmoid(acc[at] + vector(6))
            mask = row_mask(i)
            grad = cot[at].astype(FULL) * mask
            cot[at] = ((share * own + (1.0 - share) * other) * mask).astype(LOW)
            to_own, to_other = grad * share, grad * (1.0 - share)
            logits = (to_own * (own - other) * (1.0 - share)).astype(LOW)
            ea[at] = logits
            part[0] += fold(logits.astype(FULL))
            res[at] = to_own
            grd[at] = to_other

        by_rows(step)
        vg[6:7, :] = jnp.sum(part[0], axis=0, keepdims=True)
        vg[7:8, :] = jnp.zeros((1, width), FULL)
        pages_out(cot, joined, 0)

    def join_back():
        logits = ea.at[mine]
        rows_in(edge)[...] = (grd[...] + times_transposed(logits[...], weight(JOIN, 1))).astype(LOW)
        swap("edge", rows_in(edge), rows_in(back))

    def join_back_own():
        logits = ea.at[mine]
        res[...] += times_transposed(logits[...], weight(JOIN, 0))

    def join_grad(index):
        square_grad(JOIN, index, rows_in(state + index)[...], rows_in(edge)[...])

    def keep_err(at, i, result):
        del i
        ea[at] = result.astype(LOW)

    def keep_branch(at, i, result):
        ea[at] = (result * keep(i)).astype(LOW)

    def ln3_back():
        swapped("edge")

        def grad(at):
            act[edge, at] = ea[at]
            return res[at] + act[back, at].astype(FULL)

        norm_back(2, grad, keep_err, lambda step: in_two(step, ERR, ea, ea.at[theirs], k.x))

    def hidden_back(whose, block):
        if whose is theirs and block == 0:
            swapped((ERR, 0), (ERR, 1))
        first = 0 if whose is mine else count
        acc[...] = times_transposed(ea[whose], out_weight(block))

        def step(at, i):
            to = pl.ds(pl.multiple_of(first + i * BLOCK, BLOCK), BLOCK)
            slope[block, to] = (acc[at] * slope[block, to].astype(FULL)).astype(LOW)

        by_rows(step)

    def out_grad(block):
        for at in TILES:
            grad = outer(mid[block], ea[:, at]).astype(LOW)
            wd[2 * block : 2 * block + 2, :, :, :, :, at] = grad.reshape(2, 2, 2, 2, rows, TILE)
        if block == 1:
            pl.semaphore_signal(ready, inc=1, device_id=k.twin, device_id_type=MESH)

    def ffn_in_back_theirs():
        def rows_of_result(to):
            one = times_transposed(slope[0, to], in_weight(0))
            return one + times_transposed(slope[1, to], in_weight(1))

        theirs_in_two(FFN_BACK, rows_of_result, rows_in(far))

    def ffn_in_back_mine():
        for block in range(2):
            grd[...] += times_transposed(slope[block, mine], in_weight(block))

    def in_grad(block):
        for at in TILES:
            grad = outer(h2a[...], slope[block, :, at]).astype(LOW)
            fi[:, :, block, :, at] = grad.reshape(LINE, PLANE, rows, TILE)

    def ln2_back():
        swapped((FFN_BACK, 0), (FFN_BACK, 1))
        norm_back(1, lambda at: grd[at] + act[far, at].astype(FULL), keep_err)
        free(0)[...] = times_transposed(ea[mine], weight(VO_SELF, 1)).astype(LOW)
        square_grad(VO_SELF, 1, rows_in(o2)[...], ea[mine])

    def self_back(group, index, which):
        grd[...] += times_transposed(spare(which)[...], weight(group, index))
        square_grad(group, index, rows_in(h1)[...], spare(which)[...])

    def ln1_back():
        norm_back(0, lambda at: grd[at], keep_branch)
        for d in range(RANKS):
            moved = pltpu.roll(vg[...], width - d * rows, 1) if d else vg[...]
            vecs[d // PLANE, d % PLANE] = moved[:, :128]
        free(0)[...] = times_transposed(ea[mine], weight(QO_CROSS, 1)).astype(LOW)
        square_grad(QO_CROSS, 1, rows_in(o1)[...], ea[mine])

    def cross_query_back():
        pl.semaphore_wait(ready, 1)
        swap("back_keys", spare(1), free(2))
        swap("back_values", spare(2), free(3))
        grd[...] += times_transposed(spare(0)[...], weight(QO_CROSS, 0))
        square_grad(QO_CROSS, 0, x[...], spare(0)[...])

    def cross_back(index):
        swapped(("back_keys", "back_values")[index])
        grd[...] += times_transposed(free(2 + index)[...], weight(KV_CROSS, index))
        square_grad(KV_CROSS, index, x[...], free(2 + index)[...])

    def last_cross_back():
        cross_back(1)
        narrow(grd, ea)
        pages_out(ea.at[mine], x_grad, 1)

    start(); cast1(); gV.L(); gvec.L(); gJ.X(); cast2(); gFO.X(); gQO.L(); gV.R(); gvec.R(); gJ.C(); gV.X()
    gvec.X(); gQO.R(); gK.L(); gQK.L(); gK.R(); gV.C(); gvec.C(); gVO.L(); gQO.X(); gK.X(); gQK.R(); gFI.L()
    gQO.C(); gQK.X(); gVO.R(); gK.C(); gFO.L(1); gVO.X(); gFI.R(); gK.F(); kv0(); gQO.F(); gFO.L(0); gV.F()
    gvec.F(); vectors(); kv1(); gQK.C(); project_q1(); attend(0, 0, q1, k1, v1, o1); attend(1, 0, q1, k1, v1, o1)
    gJ.L(3); ln1(); gVO.C(); gJ.L(2); gQK.F(); gFI.X(); gFO.R(1); project_self(q2, QK_SELF, 0)
    project_self(k2, QK_SELF, 1); gJ.L(0); gVO.F(); project_self(v2, VO_SELF, 0); attend(0, 1, q2, k2, v2, o2)
    attend(1, 1, q2, k2, v2, o2); ln2(); gFO.R(0); gJ.L(1); gFI.F(); ffn_in(theirs, 0); gFO.F(); ffn_in(theirs, 1)
    ffn_out_theirs(); gJ.R(0); ffn_in(mine, 1); gJ.R(2); gJ.R(3); gJ.R(1); ffn_in(mine, 0); ffn_out_mine(); ln3()
    gJ.F(); join_own(); join_far(); gate(); join_back(); join_back_own(); ln3_back(); join_grad(1)
    hidden_back(mine, 1); join_grad(0); sJ1.C(); hidden_back(mine, 0); ffn_in_back_mine(); hidden_back(theirs, 0)
    hidden_back(theirs, 1); sJ1.X(); ffn_in_back_theirs(); sJ0.C(); in_grad(0); in_grad(1); sFI.C(); sJ1.L()
    out_grad(0); out_grad(1); sFO.L(0); sJ1.B(); ln2_back(); attend_back(0, 1, q2, k2, v2); sJ0.X(); sFO.B(0)
    attend_back(1, 1, q2, k2, v2); self_back(VO_SELF, 0, 2); sVO.C(); sFI.L(); sJ0.L(); self_back(QK_SELF, 0, 0)
    self_back(QK_SELF, 1, 1); sJ1.F(); sVO.X(); sQK.C(); ln1_back(); sFO.L(1); attend_back(0, 0, q1, k1, v1)
    sJ0.B(); sFI.B(); attend_back(1, 0, q1, k1, v1); sVO.L(); sQK.X(); cross_query_back(); sFO.B(1); cross_back(0)
    sQO.C(); svec.C(); sFO.M(0); sQO.X(); svec.X(); sVO.B(); sK.C(); last_cross_back(); sFI.F(); sFO.M(1); sJ0.F()
    sQK.L(); sQK.B(); sK.X(); sV.C(); sQO.L(); svec.L(); sFI.G(); sQO.B(); svec.B(); sVO.F(); sV.X(); sK.L()
    sQK.F(); sFO.X(); sV.L(); sV.B(); sQO.F(); svec.F(); sK.B(); sV.F(); sFO.F(); sK.F()
    for copy in page_copies:
        copy.wait()
    for item in scatters:
        for copy in item.put.copies:
            copy.wait()


def hand_over(count, *refs):
    sources, targets, rooms, sems = refs[:count], refs[count : 2 * count], refs[2 * count : -1], refs[-1]
    loads = [
        pltpu.make_async_copy(source, room, sems.at[0, i])
        for i, (source, room) in enumerate(zip(sources, rooms))
    ]
    stores = [
        pltpu.make_async_copy(room, target, sems.at[1, i])
        for i, (room, target) in enumerate(zip(rooms, targets))
    ]
    for copy in loads:
        copy.start()
    for load, copy in zip(loads, stores):
        load.wait()
        copy.start()
    for copy in stores:
        copy.wait()


def run_layer(x_in, lengths, drops, proj, outw, fin, fout, join, vectors, cot):
    pages, slots, width = x_in.shape[1:]
    rows = proj.shape[3]
    count = pages * KEPT
    vec = jnp.transpose(vectors, (1, 0, 2))
    vmem = pl.BlockSpec(memory_space=pltpu.VMEM)
    smem = pl.BlockSpec(memory_space=pltpu.SMEM)
    hbm = pl.BlockSpec(memory_space=pl.ANY)
    slab = (2, rows, width)
    scratch = [
        pltpu.VMEM((SQUARES, LINE, PLANE) + slab, LOW),
        pltpu.VMEM((LINE, PLANE) + slab, LOW),
        pltpu.VMEM((LINE, 2, 2) + slab, LOW),
        pltpu.VMEM((2,) + slab, LOW),
        pltpu.VMEM((LINE, PLANE, 8, 128), FULL),
        pltpu.VMEM((CORNER_RING, 2, HALF) + slab, LOW),
        pltpu.VMEM((SIDE_RING, LINE, 2) + slab, LOW),
        pltpu.VMEM((LINE_RING, LINE - 1) + slab, LOW),
        pltpu.VMEM((HOP_RING,) + slab, LOW),
        pltpu.VMEM((2,) + slab, LOW),
        pltpu.VMEM((PAIR_RING, LINE - 1, 2) + slab, LOW),
        pltpu.VMEM((PAIR_RING, 2) + slab, LOW),
        pltpu.VMEM((2, HALF, 8, 128), FULL),
        pltpu.VMEM((2, LINE, 8, 128), FULL),
        pltpu.VMEM((LINE - 1, 8, 128), FULL),
        pltpu.VMEM((8, 128), FULL),
        pltpu.VMEM((8, width), FULL),
        pltpu.VMEM((8, width), FULL),
        pltpu.VMEM((2, 8, width), FULL),
        pltpu.VMEM((count, width), LOW),
        pltpu.VMEM((count, width), LOW),
        pltpu.VMEM((slots - KEPT, width), LOW),
        pltpu.VMEM((2 * count, width), LOW),
        pltpu.VMEM((2 * count, width), LOW),
        pltpu.VMEM((13, count + slots - KEPT, width), LOW),
        pltpu.VMEM((2, 2 * count, width), LOW),
        pltpu.VMEM((2, 2 * count, width), LOW),
        pltpu.VMEM((2, pages * (width // PAIR), 2 * KEPT, slots), LOW),
        pltpu.VMEM((3, count, width), LOW),
        pltpu.VMEM((3, count, 1), FULL),
        pltpu.VMEM((3 * count, width), FULL),
        pltpu.SemaphoreType.DMA((8,)),
        pltpu.SemaphoreType.DMA((6 * pages,)),
        pltpu.SemaphoreType.DMA((18,)),
        pltpu.SemaphoreType.DMA((TRANSFERS,)),
        pltpu.SemaphoreType.DMA((TRANSFERS,)),
        pltpu.SemaphoreType.REGULAR,
    ]
    shapes = (
        ((pages, slots, width), LOW),
        ((pages, slots, width), LOW),
        ((6, rows, width), FULL),
        ((2, rows, width), FULL),
        ((rows, 4 * width), FULL),
        ((4 * rows, width), FULL),
        ((2, rows, width), FULL),
        ((vectors.shape[1], 1, rows), FULL),
    )
    results = pl.pallas_call(
        partial(layer_kernel, rows),
        out_shape=[jax.ShapeDtypeStruct(*shape) for shape in shapes],
        in_specs=[smem, smem] + [hbm] * 7 + [vmem],
        out_specs=[hbm] * 7 + [vmem],
        scratch_shapes=scratch,
        compiler_params=pltpu.CompilerParams(
            collective_id=0, has_side_effects=True, vmem_limit_bytes=VMEM_LIMIT
        ),
    )(
        lengths,
        drops,
        x_in[0],
        cot[0],
        proj.reshape(6 * rows, width),
        outw.reshape(2 * rows, width),
        fin[0],
        fout[0],
        join.reshape(2 * rows, width),
        vec,
    )
    results = pl.pallas_call(
        partial(hand_over, len(shapes)),
        out_shape=[jax.ShapeDtypeStruct(*shape) for shape in shapes],
        in_specs=[hbm] * len(shapes),
        out_specs=[hbm] * len(shapes),
        scratch_shapes=[pltpu.VMEM(*shape) for shape in shapes]
        + [pltpu.SemaphoreType.DMA((2, len(shapes)))],
        compiler_params=pltpu.CompilerParams(vmem_limit_bytes=VMEM_LIMIT),
    )(*results)
    joined, x_grad, proj_g, out_g, fin_g, fout_g, join_g, vec_g = results
    return (
        joined[None],
        x_grad[None],
        proj_g.reshape(proj.shape),
        out_g[None],
        fin_g[None],
        fout_g[None],
        join_g[None],
        jnp.transpose(vec_g, (1, 0, 2)),
    )


def fits(ranks, x_in, proj, fout):
    rows, width = proj.shape[3:]
    return (
        ranks == RANKS
        and x_in.shape[1] == 4
        and x_in.shape[2] == 2 * HEAD
        and rows % 16 == 0
        and rows <= 128
        and width == HEADS * HEAD
        and fout.shape[1] == 4 * rows
    )


def swapped(array, axis, stride):
    return lax.ppermute(array, axis, [(i, i ^ 1 << stride) for i in range(lax.axis_size(axis))])


def product(left, right):
    return jnp.dot(left, right, preferred_element_type=jnp.float32)


def outer_sum(left, right):
    return lax.dot_general(
        left, right, (((0,), (0,)), ((), ())), preferred_element_type=jnp.float32
    )


def times_transposed(left, right):
    return lax.dot_general(
        left, right, (((1,), (1,)), ((), ())), preferred_element_type=jnp.float32
    )


def norm_forward(values, gain, shift):
    centre = values - jnp.mean(values, axis=-1, keepdims=True)
    inverse = lax.rsqrt(jnp.mean(centre * centre, axis=-1, keepdims=True) + EPSILON)
    unit = centre * inverse
    return (unit * gain + shift, unit, inverse)


def norm_backward(grad, unit, inverse, gain):
    scaled = grad * gain
    inner = (
        scaled
        - jnp.mean(scaled, axis=-1, keepdims=True)
        - unit * jnp.mean(scaled * unit, axis=-1, keepdims=True)
    )
    return (inverse * inner, jnp.sum(grad * unit, axis=0), jnp.sum(grad, axis=0))


def heads_view(values, pages):
    return values.reshape(pages, values.shape[0] // pages, HEADS, values.shape[1] // HEADS)


def masked_scores(query, keys, key_mask, pages):
    scale = (query.shape[1] // HEADS) ** (-0.5)
    scores = (
        jnp.einsum(
            "pqhe,pkhe->phqk",
            heads_view(query, pages),
            heads_view(keys, pages),
            preferred_element_type=jnp.float32,
        )
        * scale
    )
    return jnp.where(key_mask[:, None, None, :], scores, -1e30)


def attend_forward(query, keys, values, key_mask, pages):
    scores = masked_scores(query, keys, key_mask, pages)
    top = jnp.max(scores, axis=-1, keepdims=True)
    weights = jnp.exp(scores - top)
    total = jnp.sum(weights, axis=-1, keepdims=True)
    probs = (weights / total).astype(jnp.bfloat16)
    mixed = jnp.einsum(
        "phqk,pkhe->pqhe", probs, heads_view(values, pages), preferred_element_type=jnp.float32
    )
    return (mixed.reshape(query.shape).astype(jnp.bfloat16), top + jnp.log(total))


def attend_backward(grad_out, query, keys, values, key_mask, logsum, pages):
    scale = (query.shape[1] // HEADS) ** (-0.5)
    probs = jnp.exp(masked_scores(query, keys, key_mask, pages) - logsum)
    grad_heads = heads_view(grad_out, pages)
    grad_probs = jnp.einsum(
        "pqhe,pkhe->phqk", grad_heads, heads_view(values, pages), preferred_element_type=jnp.float32
    )
    grad_scores = (
        probs * (grad_probs - jnp.sum(grad_probs * probs, axis=-1, keepdims=True))
    ).astype(jnp.bfloat16)
    grad_query = (
        jnp.einsum(
            "phqk,pkhe->pqhe",
            grad_scores,
            heads_view(keys, pages),
            preferred_element_type=jnp.float32,
        )
        * scale
    )
    grad_keys = (
        jnp.einsum(
            "phqk,pqhe->pkhe",
            grad_scores,
            heads_view(query, pages),
            preferred_element_type=jnp.float32,
        )
        * scale
    )
    grad_values = jnp.einsum(
        "phqk,pqhe->pkhe",
        probs.astype(jnp.bfloat16),
        grad_heads,
        preferred_element_type=jnp.float32,
    )
    shape = query.shape
    return (
        grad_query.reshape(shape).astype(jnp.bfloat16),
        grad_keys.reshape(shape).astype(jnp.bfloat16),
        grad_values.reshape(shape).astype(jnp.bfloat16),
    )


def local(
    x_in,
    lengths,
    drops,
    proj_master,
    out_master,
    ffn_in_master,
    ffn_out_master,
    join_master,
    vectors,
    cotangent,
):
    if fits(lax.axis_size("dp"), x_in, proj_master, ffn_out_master):
        return run_layer(
            x_in,
            lengths,
            drops,
            proj_master,
            out_master,
            ffn_in_master,
            ffn_out_master,
            join_master,
            vectors,
            cotangent,
        )
    pages = x_in.shape[1]
    slots = x_in.shape[2]
    width = x_in.shape[3]
    rows = pages * slots
    gathered = (
        lax.all_gather(proj_master.astype(jnp.bfloat16), "dp", axis=3, tiled=True),
        lax.all_gather(out_master.astype(jnp.bfloat16), "dp", axis=2, tiled=True),
        lax.all_gather(ffn_in_master.astype(jnp.bfloat16), "dp", axis=1, tiled=True),
        lax.all_gather(ffn_out_master.astype(jnp.bfloat16), "dp", axis=1, tiled=True),
        lax.all_gather(join_master.astype(jnp.bfloat16), "dp", axis=2, tiled=True),
        lax.all_gather(vectors.astype(jnp.bfloat16), "dp", axis=2, tiled=True),
    )
    proj_w = gathered[0][0]
    out_w = gathered[1][0]
    ffin_w = gathered[2][0]
    ffout_w = gathered[3][0]
    join_w = gathered[4][0]
    vec_w = gathered[5][0].astype(jnp.float32)
    key_mask = jnp.arange(slots, dtype=jnp.int32)[None, :] < lengths[:, None]
    row_mask = key_mask.reshape(rows, 1).astype(jnp.float32)
    keep = (1 - drops).astype(jnp.float32)
    keep_rows = jnp.broadcast_to(keep[:, None], (pages, slots)).reshape(rows, 1)
    source = x_in[0].reshape(rows, width)
    own_keys = product(source, proj_w[0, 1]).astype(jnp.bfloat16)
    own_values = product(source, proj_w[0, 2]).astype(jnp.bfloat16)
    far_keys, far_values = swapped((own_keys, own_values), "stream", 0)
    cross_query = product(source, proj_w[0, 0]).astype(jnp.bfloat16)
    cross_out, cross_logsum = attend_forward(cross_query, far_keys, far_values, key_mask, pages)
    first, unit_one, inverse_one = norm_forward(
        source.astype(jnp.float32) + product(cross_out, out_w[0]) * keep_rows, vec_w[0], vec_w[1]
    )
    first_low = first.astype(jnp.bfloat16)
    self_query = product(first_low, proj_w[1, 0]).astype(jnp.bfloat16)
    self_keys = product(first_low, proj_w[1, 1]).astype(jnp.bfloat16)
    self_values = product(first_low, proj_w[1, 2]).astype(jnp.bfloat16)
    self_out, self_logsum = attend_forward(self_query, self_keys, self_values, key_mask, pages)
    second, unit_two, inverse_two = norm_forward(
        first + product(self_out, out_w[1]), vec_w[2], vec_w[3]
    )
    second_low = second.astype(jnp.bfloat16)
    hidden = product(second_low, ffin_w)
    gelu_exact = partial(jax.nn.gelu, approximate=False)
    active_f32, gelu_pull = jax.vjp(gelu_exact, hidden)
    active = active_f32.astype(jnp.bfloat16)
    third, unit_three, inverse_three = norm_forward(
        second + product(active, ffout_w), vec_w[4], vec_w[5]
    )
    state = third.astype(jnp.bfloat16)
    far_state = swapped(state, "stream", 0)
    state_f32 = state.astype(jnp.float32)
    far_f32 = far_state.astype(jnp.float32)
    gate = jax.nn.sigmoid(product(state, join_w[0]) + product(far_state, join_w[1]) + vec_w[6])
    joined = ((gate * state_f32 + (1.0 - gate) * far_f32) * row_mask).astype(jnp.bfloat16)
    grad_joined = cotangent[0].reshape(rows, width).astype(jnp.float32) * row_mask
    grad_logits = (grad_joined * (state_f32 - far_f32) * gate * (1.0 - gate)).astype(jnp.bfloat16)
    grad_join = jnp.stack([outer_sum(state, grad_logits), outer_sum(far_state, grad_logits)])
    grad_bias = jnp.sum(grad_logits.astype(jnp.float32), axis=0)
    grad_far = (grad_joined * (1.0 - gate) + times_transposed(grad_logits, join_w[1])).astype(
        jnp.bfloat16
    )
    returned = swapped(grad_far, "stream", 0)
    grad_third = (
        grad_joined * gate + times_transposed(grad_logits, join_w[0]) + returned.astype(jnp.float32)
    )
    grad_res3, gain_three, shift_three = norm_backward(
        grad_third, unit_three, inverse_three, vec_w[4]
    )
    grad_res3_low = grad_res3.astype(jnp.bfloat16)
    grad_ffout = outer_sum(active, grad_res3_low)
    grad_hidden = gelu_pull(times_transposed(grad_res3_low, ffout_w))[0].astype(jnp.bfloat16)
    grad_ffin = outer_sum(second_low, grad_hidden)
    grad_second = grad_res3 + times_transposed(grad_hidden, ffin_w)
    grad_res2, gain_two, shift_two = norm_backward(grad_second, unit_two, inverse_two, vec_w[2])
    grad_res2_low = grad_res2.astype(jnp.bfloat16)
    grad_out_self = outer_sum(self_out, grad_res2_low)
    grad_self_out = times_transposed(grad_res2_low, out_w[1]).astype(jnp.bfloat16)
    grad_q2, grad_k2, grad_v2 = attend_backward(
        grad_self_out, self_query, self_keys, self_values, key_mask, self_logsum, pages
    )
    grad_proj_self = jnp.stack(
        [
            outer_sum(first_low, grad_q2),
            outer_sum(first_low, grad_k2),
            outer_sum(first_low, grad_v2),
        ]
    )
    grad_first = (
        grad_res2
        + times_transposed(grad_q2, proj_w[1, 0])
        + times_transposed(grad_k2, proj_w[1, 1])
        + times_transposed(grad_v2, proj_w[1, 2])
    )
    grad_res1, gain_one, shift_one = norm_backward(grad_first, unit_one, inverse_one, vec_w[0])
    grad_branch = (grad_res1 * keep_rows).astype(jnp.bfloat16)
    grad_out_cross = outer_sum(cross_out, grad_branch)
    grad_cross_out = times_transposed(grad_branch, out_w[0]).astype(jnp.bfloat16)
    grad_q1, grad_far_keys, grad_far_values = attend_backward(
        grad_cross_out, cross_query, far_keys, far_values, key_mask, cross_logsum, pages
    )
    back_keys, back_values = swapped((grad_far_keys, grad_far_values), "stream", 0)
    grad_proj_cross = jnp.stack(
        [outer_sum(source, grad_q1), outer_sum(source, back_keys), outer_sum(source, back_values)]
    )
    grad_source = (
        grad_res1
        + times_transposed(grad_q1, proj_w[0, 0])
        + times_transposed(back_keys, proj_w[0, 1])
        + times_transposed(back_values, proj_w[0, 2])
    )
    grad_proj = jnp.stack([grad_proj_cross, grad_proj_self])[None]
    grad_out = jnp.stack([grad_out_cross, grad_out_self])[None]
    grad_vectors = jnp.stack(
        [gain_one, shift_one, gain_two, shift_two, gain_three, shift_three, grad_bias]
    )[None]
    all_sums = (
        lax.psum_scatter(grad_proj, "dp", scatter_dimension=3, tiled=True),
        lax.psum_scatter(grad_out, "dp", scatter_dimension=2, tiled=True),
        lax.psum_scatter(grad_ffin[None], "dp", scatter_dimension=1, tiled=True),
        lax.psum_scatter(grad_ffout[None], "dp", scatter_dimension=1, tiled=True),
        lax.psum_scatter(grad_join[None], "dp", scatter_dimension=2, tiled=True),
        lax.psum_scatter(grad_vectors, "dp", scatter_dimension=2, tiled=True),
    )
    proj_part, out_part, ffin_part, ffout_part, join_part, vectors_part = all_sums
    joined_out = joined.reshape(1, pages, slots, width)
    x_grad = grad_source.astype(jnp.bfloat16).reshape(1, pages, slots, width)
    return (joined_out, x_grad, proj_part, out_part, ffin_part, ffout_part, join_part, vectors_part)


def solution(mesh):
    placed = (
        P("stream", "dp", None, None),
        P("dp"),
        P("dp"),
        P("stream", None, None, "dp", None),
        P("stream", None, "dp", None),
        P("stream", "dp", None),
        P("stream", "dp", None),
        P("stream", None, "dp", None),
        P("stream", None, "dp"),
        P("stream", "dp", None, None),
    )
    return jax.shard_map(
        local,
        mesh=mesh,
        in_specs=placed,
        out_specs=(
            P("stream", "dp", None, None),
            P("stream", "dp", None, None),
            P("stream", None, None, "dp", None),
            P("stream", None, "dp", None),
            P("stream", "dp", None),
            P("stream", "dp", None),
            P("stream", None, "dp", None),
            P("stream", None, "dp"),
        ),
        check_vma=False,
    )
```

```python
import math
from functools import partial

import jax
import jax.numpy as jnp
from jax import lax
from jax.experimental import pallas as pl
from jax.experimental.pallas import tpu as pltpu
from jax.sharding import PartitionSpec as P

HEADS = 12

EPSILON = 1e-05
VMEM_LIMIT = 62 * 2**20
TRANSFERS = 300
MESH = pl.DeviceIdType.MESH
LOW = jnp.bfloat16
FULL = jnp.float32
LINE, PLANE = 4, 4
RANKS = LINE * PLANE
HALF = LINE // 2
KV_CROSS, QO_CROSS, QK_SELF, VO_SELF, JOIN = range(5)
SQUARES = 5
FFN_OUT_ROWS, FFN_IN_ROWS = 10, 14
ITEMS = (
    (KV_CROSS, 0, 1),
    (KV_CROSS, 1, 1),
    (QO_CROSS, 0, 2),
    (QK_SELF, 0, 2),
    (VO_SELF, 0, 2),
    (JOIN, 0, 2),
    (JOIN, 0, 1),
    (JOIN, 1, 1),
)
VECTORS = None
H2, FFN, STATE, ERR, FFN_BACK = range(5)
CORNER_RING, SIDE_RING, LINE_RING, HOP_RING, PAIR_RING = 3, 4, 5, 5, 3
BLOCK = 112
KEPT = 112
TILE = 256
TILES = tuple(pl.ds(at, TILE) for at in range(0, 768, TILE))
HEAD = 64
PAIR = 2 * HEAD


class Links:
    def __init__(self, send_sems, recv_sems):
        self.stream = lax.axis_index("stream")
        self.me = lax.axis_index("dp")
        self.z = self.me // PLANE
        self.q = self.me % PLANE
        self.qx = self.q + 1 - 2 * (self.q % 2)
        self.qy = (self.q + 2) % PLANE
        self.qd = PLANE - 1 - self.q
        self.xx, self.yy = self.q % 2, self.q // 2
        self.columns = (self.q, self.qx, self.qy, self.qd)
        self.z_near = self.z + 1 - 2 * (self.z % 2)
        self.z_two = (self.z + 2) % LINE
        self.z_third = LINE - 1 - self.z
        self.middle = (self.z == 1) | (self.z == 2)
        self.x = (self.stream, self.z * PLANE + self.qx)
        self.y = (self.stream, self.z * PLANE + self.qy)
        self.near, self.two, self.third = (
            (self.stream, at * PLANE + self.q) for at in (self.z_near, self.z_two, self.z_third)
        )
        self.twin = (1 - self.stream, self.me)
        self.sems = (send_sems, recv_sems)
        self.used = 0

    def greet(self):
        for peer in (self.x, self.y, self.near, self.two, self.third, self.twin):
            pl.semaphore_signal(
                pltpu.get_barrier_semaphore(), inc=1, device_id=peer, device_id_type=MESH
            )

    def met(self):
        pl.semaphore_wait(pltpu.get_barrier_semaphore(), 6)

    def copy(self, source, target, peer, landing=None):
        number = self.used
        self.used += 1
        return pltpu.make_async_remote_copy(
            src_ref=source,
            dst_ref=target,
            send_sem=self.sems[0].at[number],
            recv_sem=self.sems[1].at[number if landing is None else landing],
            device_id=peer,
            device_id_type=MESH,
        )

    def send(self, source, target, peer):
        copy = self.copy(source, target, peer)
        copy.start()
        return copy


class LineGather:
    def __init__(self, view, links):
        self.view, self.k = view, links

    def launch(self):
        k = self.k
        own = self.view(k.z)
        self.near = k.send(own, own, k.near)
        self.two = k.send(own, own, k.two)
        landing = k.used
        self.third = k.copy(own, own, k.third)
        passed = self.view(k.z_two)
        self.passed = k.copy(passed, passed, k.near, landing)
        pl.when(k.middle)(self.third.start)

    def relay(self):
        self.two.wait_recv()
        pl.when(self.k.middle)(self.passed.start)

    def arrive(self):
        self.near.wait_recv()
        self.third.wait_recv()

    def drain(self):
        self.near.wait_send()
        self.two.wait_send()

        @pl.when(self.k.middle)
        def _():
            self.third.wait_send()
            self.passed.wait_send()


class LineSum:
    def __init__(self, view, room, links, straight=False):
        self.view, self.room, self.k, self.straight = view, room, links, straight

    def launch(self):
        k = self.k
        self.spots, self.hop = self.room()
        self.near = k.send(self.view(k.z_near), self.spots(0), k.near)
        away = self.view(k.z_third)
        self.third = k.copy(away, self.spots(2), k.third)
        if self.straight:
            self.third.start()
            self.two = k.send(self.view(k.z_two), self.spots(1), k.two)
            return
        self.passed = k.copy(away, self.hop, k.near)
        pl.when(k.middle)(self.third.start)
        pl.when(jnp.logical_not(k.middle))(self.passed.start)

    def bridge(self):
        k = self.k
        if self.straight:
            return
        part = self.view(k.z_two)

        @pl.when(k.middle)
        def _():
            self.passed.wait_recv()
            part[...] = total(part, self.hop).astype(part.dtype)

        self.two = k.send(part, self.spots(1), k.two)

    def collect(self, put):
        k = self.k
        self.near.wait_recv()
        self.two.wait_recv()
        terms = [self.view(k.z), self.spots(0), self.spots(1)]
        if self.straight:
            self.third.wait_recv()
            put(total(*terms, self.spots(2)))
            return

        @pl.when(k.middle)
        def _():
            self.third.wait_recv()
            put(total(*terms, self.spots(2)))

        pl.when(jnp.logical_not(k.middle))(lambda: put(total(*terms)))

    def drain(self):
        self.near.wait_send()
        self.two.wait_send()
        if self.straight:
            self.third.wait_send()
            return
        pl.when(self.k.middle)(self.third.wait_send)
        pl.when(jnp.logical_not(self.k.middle))(self.passed.wait_send)


class GatherByLine:
    def __init__(self, view, links):
        self.view, self.k = view, links
        self.line = LineGather(lambda z: view(z, links.q), links)

    def L(self):
        self.line.launch()

    def R(self):
        self.line.relay()

    def X(self):
        k = self.k
        self.line.arrive()
        column = self.view(slice(None), k.q)
        self.sides = [k.send(column, column, k.x), k.send(column, column, k.y)]

    def C(self):
        k = self.k
        for copy in self.sides:
            copy.wait_recv()
        one, two = self.view(slice(0, HALF), k.qx), self.view(slice(HALF, LINE), k.qy)
        self.corners = [k.send(one, one, k.y), k.send(two, two, k.x)]

    def F(self):
        for copy in self.corners:
            copy.wait_recv()
        for copy in self.sides + self.corners:
            copy.wait_send()
        self.line.drain()


class GatherByPlane:
    def __init__(self, view, links, size):
        self.view, self.k, self.size = view, links, size
        self.lines = [
            LineGather(partial(lambda q, z: view(z, q), q), links) for q in links.columns
        ]

    def X(self):
        k = self.k
        own = self.view(k.z, k.q)
        self.sides = [k.send(own, own, k.x), k.send(own, own, k.y)]

    def C(self):
        k = self.k
        for copy in self.sides:
            copy.wait_recv()
        one = self.view(k.z, k.qx, 0, 1)
        self.corners = [k.send(one, one, k.y)]
        if self.size == 2:
            two = self.view(k.z, k.qy, 1, 1)
            self.corners.append(k.send(two, two, k.x))

    def L(self, column):
        if column == 3:
            for copy in self.corners:
                copy.wait_recv()
        self.lines[column].launch()

    def R(self, column):
        self.lines[column].relay()

    def F(self):
        for line in self.lines:
            line.arrive()
        for line in self.lines:
            line.drain()
        for copy in self.sides + self.corners:
            copy.wait_send()


class ScatterByPlane:
    def __init__(self, view, room, put, links, straight):
        self.view, self.room, self.put, self.k = view, room, put, links
        self.line = LineSum(lambda z: view(z, links.q), room.line, links, straight)

    def C(self):
        k = self.k
        self.corners, self.sides = self.room.plane()
        low, high = slice(0, HALF), slice(HALF, LINE)
        self.one = [
            k.send(self.view(low, k.qd), self.corners(0), k.x),
            k.send(self.view(high, k.qd), self.corners(1), k.y),
        ]
        self.two = [
            k.send(self.view(low, k.qx), self.sides(0, low), k.x),
            k.send(self.view(high, k.qy), self.sides(1, high), k.y),
        ]

    def X(self):
        k = self.k
        low, high = slice(0, HALF), slice(HALF, LINE)
        for number, half, q in ((0, low, k.qy), (1, high, k.qx)):
            self.one[number].wait_recv()
            part = self.view(half, q)
            part[...] = total(part, self.corners(number)).astype(part.dtype)
        self.two += [
            k.send(self.view(high, k.qx), self.sides(0, high), k.x),
            k.send(self.view(low, k.qy), self.sides(1, low), k.y),
        ]

    def L(self):
        k = self.k
        for copy in self.two:
            copy.wait_recv()
        part = self.view(slice(None), k.q)
        everything = slice(None)
        part[...] = total(part, self.sides(0, everything), self.sides(1, everything)).astype(part.dtype)
        self.line.launch()

    def B(self):
        self.line.bridge()

    def F(self):
        self.line.collect(self.put.sums)
        self.put.store()
        for copy in self.one + self.two:
            copy.wait_send()
        self.line.drain()


class PairGatherByLine:
    def __init__(self, view, links, first=None):
        self.view, self.k, self.first = view, links, first
        self.line = LineGather(lambda z: view(z, links.yy), links)

    def L(self):
        if self.first is not None:
            self.first().wait_recv()
        self.line.launch()

    def R(self):
        self.line.relay()

    def X(self):
        k = self.k
        self.line.arrive()
        column = self.view(slice(None), k.yy)
        self.side = k.send(column, column, k.y)

    def F(self):
        self.side.wait_recv()
        self.side.wait_send()
        self.line.drain()
        if self.first is not None:
            self.first().wait_send()


class PairGatherByPlane:
    def __init__(self, view, links):
        self.view, self.k = view, links
        self.lines = [
            LineGather(partial(lambda y, z: view(z, y), y), links) for y in (links.yy, 1 - links.yy)
        ]

    def X(self):
        k = self.k
        own = self.view(k.z, k.yy)
        self.side = k.send(own, own, k.y)

    def L(self, row):
        if row == 1:
            self.side.wait_recv()
        self.lines[row].launch()

    def R(self, row):
        self.lines[row].relay()

    def F(self):
        for line in self.lines:
            line.arrive()
        for line in self.lines:
            line.drain()
        self.side.wait_send()


class PairScatterByPlane:
    def __init__(self, view, room, put, links):
        self.view, self.room, self.put, self.k = view, room, put, links
        self.line = LineSum(lambda z: view(z, links.yy), room.line, links)

    def C(self):
        k = self.k
        self.side = self.room.column()
        self.two = k.send(self.view(slice(None), 1 - k.yy), self.side, k.y)

    def L(self):
        k = self.k
        self.two.wait_recv()
        part = self.view(slice(None), k.yy)
        part[...] = total(part, self.side).astype(part.dtype)
        self.line.launch()

    def B(self):
        self.line.bridge()

    def F(self):
        self.line.collect(self.put.sums)
        self.put.store()
        self.two.wait_send()
        self.line.drain()

    def G(self):
        self.put.G()


class PairScatterByLine:
    def __init__(self, view, side, room, put, links):
        self.view, self.side, self.put, self.k = view, side, put, links
        self.rows = (1 - links.yy, links.yy)
        self.lines = [
            LineSum(partial(lambda y, z: view(z, y), y), room.line, links) for y in self.rows
        ]

    def L(self, row):
        self.lines[row].launch()

    def B(self, row):
        self.lines[row].bridge()

    def M(self, row):
        part = self.view(self.k.z, self.rows[row])

        def put(value):
            part[...] = value.astype(part.dtype)

        self.lines[row].collect(put)

    def X(self):
        k = self.k
        self.two = k.send(self.view(k.z, 1 - k.yy), self.side, k.y)

    def F(self):
        k = self.k
        self.two.wait_recv()
        self.put.sums(total(self.view(k.z, k.yy), self.side))
        self.put.store()
        self.two.wait_send()
        for line in self.lines:
            line.drain()


def total(*refs):
    result = refs[0][...].astype(FULL)
    for ref in refs[1:]:
        result = result + ref[...].astype(FULL)
    return result


class Room:
    def __init__(self, size, corners, sides, lines, hops, used):
        self.size, self.used = size, used
        self.corners, self.sides, self.lines, self.hops = corners, sides, lines, hops

    def slot(self, ring):
        number = self.used.setdefault(id(ring), 0)
        self.used[id(ring)] += 1
        return ring.at[number % ring.shape[0]]

    def column(self):
        return self.slot(self.sides)

    def plane(self):
        corners, sides = self.slot(self.corners), self.slot(self.sides)
        some = pl.ds(0, self.size)
        return (lambda n: corners.at[n, :, some]), (lambda n, half: sides.at[half, n, some])

    def line(self):
        lines, hops = self.slot(self.lines), self.slot(self.hops)
        some = pl.ds(0, self.size)
        return (lambda n: lines.at[n, some]), hops.at[some]


class VectorRoom(Room):
    def plane(self):
        return (lambda n: self.corners.at[n]), (lambda n, half: self.sides.at[n, half])

    def line(self):
        return (lambda n: self.lines.at[n]), self.hops


class Put:
    def __init__(self, stage, targets, sems, first):
        self.stage, self.targets, self.sems, self.first = stage, targets, sems, first
        self.copies = []

    def sums(self, values):
        for i in range(len(self.targets)):
            self.stage(i)[...] = values[i]

    def store(self):
        for i, target in enumerate(self.targets):
            copy = pltpu.make_async_copy(self.stage(i), target, self.sems.at[self.first + i])
            copy.start()
            self.copies.append(copy)


class PutVectors:
    def __init__(self, target):
        self.target, self.copies = target, []

    def sums(self, values):
        rows, _, width = self.target.shape
        for row in range(rows):
            self.target[row] = values[row : row + 1, :width]

    def store(self):
        pass


def layer_kernel(
    rows,
    lengths,
    drops,
    x_in,
    cot_in,
    proj,
    outw,
    fin,
    fout,
    join,
    vec,
    joined,
    x_grad,
    proj_g,
    out_g,
    fin_g,
    fout_g,
    join_g,
    vec_g,
    sq,
    fi,
    wd,
    halves,
    vecs,
    corners,
    sides,
    lines,
    hops,
    side_room,
    pair_lines,
    pair_hops,
    vcorners,
    vsides,
    vlines,
    vhop,
    vw,
    vg,
    part,
    x,
    cot,
    nothing,
    h2a,
    ea,
    act,
    mid,
    slope,
    probs,
    unit,
    inv,
    work,
    load_sems,
    page_sems,
    store_sems,
    send_sems,
    recv_sems,
    ready,
):
    k = Links(send_sems, recv_sems)
    width = sq.shape[-1]
    count = x.shape[0]
    pages, slots = x_in.shape[:2]
    pairs = width // PAIR
    scale = HEAD**-0.5
    (k1, v1, q1, o1, h1, q2, k2, v2, o2, state, far, edge, back) = range(13)
    mine, theirs = pl.ds(0, count), pl.ds(count, count)
    acc, res, grd = (work.at[pl.ds(i * count, count)] for i in range(3))

    def weight(group, index):
        return sq[group, :, :, index].reshape(width, width)

    def in_weight(block):
        return fi[:, :, block].reshape(width, width)

    def out_weight(block):
        return wd[2 * block : 2 * block + 2].reshape(width, width)

    def free(slot):
        return mid.at[slot // 2, pl.ds((slot % 2) * count, count)]

    def spare(slot):
        return slope.at[slot // 2, pl.ds((slot % 2) * count, count)]

    def times(left, right):
        return jnp.dot(left, right, preferred_element_type=FULL)

    def times_transposed(left, right):
        return lax.dot_general(left, right, (((1,), (1,)), ((), ())), preferred_element_type=FULL)

    def outer(left, right):
        return lax.dot_general(left, right, (((0,), (0,)), ((), ())), preferred_element_type=FULL)

    def loop(first, last, body):
        def step(i, carry):
            body(i)
            return carry

        lax.fori_loop(first, last, step, 0)

    def by_rows(body, first=0, last=None):
        def step(i):
            body(pl.ds(pl.multiple_of(i * BLOCK, BLOCK), BLOCK), i)

        loop(first, count // BLOCK if last is None else last, step)

    def rows_of(i):
        return lax.broadcasted_iota(jnp.int32, (BLOCK, 1), 0) + i * BLOCK

    def narrow(source, target):
        def step(at, i):
            del i
            target[at] = source[at].astype(LOW)

        by_rows(step)

    def row_mask(i):
        row, mask = rows_of(i), jnp.zeros((BLOCK, 1), FULL)
        for page in range(pages):
            first = page * KEPT
            mask = jnp.where((row >= first) & (row < first + lengths[page]), 1.0, mask)
        return mask

    def keep(i):
        row, kept = rows_of(i), jnp.zeros((BLOCK, 1), FULL)
        for page in range(pages):
            kept = jnp.where(row >= page * KEPT, (1 - drops[page]).astype(FULL), kept)
        return kept

    def rows_in(slot):
        return act.at[slot, pl.ds(0, count)]

    def vector(row):
        return vw[row : row + 1, :]

    def norm(number, at, values):
        centre = values - jnp.mean(values, axis=-1, keepdims=True)
        inverse = lax.rsqrt(jnp.mean(centre * centre, axis=-1, keepdims=True) + EPSILON)
        plain = centre * inverse
        unit[number, at] = plain.astype(LOW)
        inv[number, at] = inverse
        return plain * vector(2 * number) + vector(2 * number + 1)

    def fold(values):
        return jnp.sum(values.reshape(BLOCK // 8, 8, width), axis=0)

    def norm_back(number, grad, after, run=None):
        part[...] = jnp.zeros_like(part)

        def step(at, i):
            value = grad(at)
            plain = unit[number, at].astype(FULL)
            part[0] += fold(value * plain)
            part[1] += fold(value)
            scaled = value * vector(2 * number)
            inner = (
                scaled
                - jnp.mean(scaled, axis=-1, keepdims=True)
                - plain * jnp.mean(scaled * plain, axis=-1, keepdims=True)
            )
            result = inv[number, at] * inner
            grd[at] = result
            after(at, i, result)

        (by_rows if run is None else run)(step)
        for i in range(2):
            vg[2 * number + i : 2 * number + i + 1, :] = jnp.sum(part[i], axis=0, keepdims=True)

    def split_heads(values):
        first = lax.broadcasted_iota(jnp.int32, values.shape, 1) < HEAD
        zero = jnp.zeros_like(values)
        return jnp.concatenate([jnp.where(first, values, zero), jnp.where(first, zero, values)], axis=0)

    def join_heads(values):
        first = lax.broadcasted_iota(jnp.int32, (KEPT, PAIR), 1) < HEAD
        return jnp.where(first, values[:KEPT], values[KEPT:])

    def by_heads(half, body):
        group = 6

        def step(i):
            page = i // (pairs // group)
            start = pl.multiple_of(page * KEPT, KEPT)
            at, keys_at = pl.ds(start, KEPT), pl.ds(start, slots)
            for j in range(group):
                pair = (i % (pairs // group)) * group + j
                lanes = pl.ds(pl.multiple_of(pair * PAIR, PAIR), PAIR)
                body(page, at, keys_at, lanes, i * group + j)

        steps = pages * (pairs // group)
        loop(half * (steps // 2), steps if half else steps // 2, step)

    def attend(half, which, query, keys, values, result):
        def body(page, at, keys_at, lanes, number):
            scores = times_transposed(split_heads(act[query, at, lanes]), act[keys, keys_at, lanes]) * scale
            spot = lax.broadcasted_iota(jnp.int32, scores.shape, 1)
            scores = jnp.where(spot < lengths[page], scores, -1e30)
            weights = jnp.exp(scores - jnp.max(scores, axis=-1, keepdims=True))
            chance = weights * (1.0 / jnp.sum(weights, axis=-1, keepdims=True))
            chance = chance.astype(LOW)
            probs[which, number] = chance
            act[result, at, lanes] = join_heads(times(chance, act[values, keys_at, lanes])).astype(LOW)

        by_heads(half, body)

    def attend_back(half, which, query, keys, values):
        grad, to_query, to_keys, to_values = free(0), spare(0), spare(1), spare(2)

        def body(page, at, keys_at, lanes, number):
            del page
            chance = probs[which, number]
            spread = split_heads(grad[at, lanes])
            pull = times_transposed(spread, act[values, keys_at, lanes])
            wide_chance = chance.astype(FULL)
            inner = pull - jnp.sum(pull * wide_chance, axis=-1, keepdims=True)
            delta = (wide_chance * inner).astype(LOW)
            to_query[at, lanes] = (join_heads(times(delta, act[keys, keys_at, lanes])) * scale).astype(LOW)
            key_grad = outer(delta, split_heads(act[query, at, lanes]))[:KEPT]
            to_keys[at, lanes] = (key_grad * scale).astype(LOW)
            to_values[at, lanes] = outer(chance, spread)[:KEPT].astype(LOW)

        by_heads(half, body)

    def square_grad(group, index, left, right):
        sq[group, :, :, index] = outer(left, right).astype(LOW).reshape(LINE, PLANE, rows, width)

    def view(item):
        if item is VECTORS:
            return lambda z, q: vecs.at[z, q]
        group, start, size = item
        return lambda z, q, first=0, some=size: sq.at[group, z, q, pl.ds(start + first, some)]

    def outputs(item):
        group, start, size = item
        places = []
        for i in range(start, start + size):
            if group == JOIN:
                places.append(join_g.at[i])
            elif group == KV_CROSS:
                places.append(proj_g.at[1 + i])
            elif group == QK_SELF:
                places.append(proj_g.at[3 + i])
            elif i == 1:
                places.append(out_g.at[0 if group == QO_CROSS else 1])
            else:
                places.append(proj_g.at[0 if group == QO_CROSS else 5])
        return places

    def put_for(item):
        if item is VECTORS:
            return PutVectors(vec_g)
        first = 2 * item[0] + item[1]
        return Put(lambda i: work.at[pl.ds((first + i) * rows, rows)], outputs(item), store_sems, first)

    used = {}

    def gather(item):
        return GatherByLine(view(item), k)

    def gather_by_plane(item):
        return GatherByPlane(view(item), k, item[2])

    def keep_scatter(item):
        scatters.append(item)
        return item

    def scatter(item, straight=False):
        if item is VECTORS:
            room = VectorRoom(0, vcorners, vsides, vlines, vhop, used)
        else:
            room = Room(item[2], corners, sides, lines, hops, used)
        return keep_scatter(ScatterByPlane(view(item), room, put_for(item), k, straight))

    def out_view(z, y):
        return wd.at[z, y]

    def in_view(z, y):
        return fi.at[z, pl.ds(2 * y, 2)]

    def stage_of(first):
        return lambda i: work.at[pl.ds((first + i) * rows, rows)]

    class PutOut(Put):
        def sums(self, values):
            for i in range(4):
                self.stage(i)[...] = values[i // 2, i % 2]

    class PutIn(Put):
        def sums(self, values):
            for i in range(4):
                self.stage(i)[...] = values[i // 2, i % 2]

        def two_rows(self, first, x_):
            return work.at[pl.ds(pl.multiple_of((first + 2 * x_) * rows, rows), 2 * rows)]

        def half(self, h, block):
            return work[(2 * h + block) * rows : (2 * h + block + 1) * rows]

        def store(self):
            self.two_rows(0, k.xx)[...] = self.two_rows(FFN_IN_ROWS, k.xx)[...]
            other = self.two_rows(FFN_IN_ROWS, 1 - k.xx)[...]
            halves[0] = other.astype(LOW).reshape(2, rows, width)
            self.swap = k.send(halves.at[0], halves.at[1], k.x)

        def G(self):
            self.swap.wait()
            other = halves[1].astype(FULL).reshape(2 * rows, width)
            self.two_rows(0, 1 - k.xx)[...] = other
            piece = width // 4
            for j in range(4):
                block, first = j // 2, (j % 2) * 2 * piece
                parts = [
                    self.half(h, block)[:, first + g * piece : first + (g + 1) * piece]
                    for g in range(2)
                    for h in range(2)
                ]
                self.stage(j)[...] = jnp.concatenate(parts, axis=1)
            Put.store(self)

    scatters = []
    pair_room = Room(2, corners, sides, pair_lines, pair_hops, used)
    put_out = PutOut(
        stage_of(FFN_OUT_ROWS),
        [fout_g.at[pl.ds(i * rows, rows)] for i in range(4)],
        store_sems,
        FFN_OUT_ROWS,
    )
    put_in = PutIn(
        stage_of(FFN_IN_ROWS),
        [fin_g.at[:, pl.ds(i * width, width)] for i in range(4)],
        store_sems,
        FFN_IN_ROWS,
    )
    gFO = PairGatherByPlane(out_view, k)
    gFI = PairGatherByLine(in_view, k, lambda: swaps["in"])
    sFO = keep_scatter(PairScatterByLine(out_view, side_room, pair_room, put_out, k))
    sFI = keep_scatter(PairScatterByPlane(in_view, pair_room, put_in, k))
    gK = gather(ITEMS[0])
    gV = gather(ITEMS[1])
    gQO = gather(ITEMS[2])
    gQK = gather(ITEMS[3])
    gVO = gather(ITEMS[4])
    gJ = gather_by_plane(ITEMS[5])
    gvec = gather(VECTORS)
    sK = scatter(ITEMS[0])
    sV = scatter(ITEMS[1])
    sQO = scatter(ITEMS[2])
    sQK = scatter(ITEMS[3])
    sVO = scatter(ITEMS[4])
    sJ0 = scatter(ITEMS[6])
    sJ1 = scatter(ITEMS[7])
    svec = scatter(VECTORS)
    swaps = {}

    def swap(name, source, target, peer=None):
        swaps[name] = k.send(source, target, k.twin if peer is None else peer)

    def swapped(*names):
        for name in names:
            swaps[name].wait()

    sources, first = [], 0
    for shard in (proj, outw, join, fout):
        sources.append((shard, pl.ds(first, shard.shape[0])))
        first += shard.shape[0]
    for j in range(4):
        sources.append((fin.at[:, pl.ds(j * width, width)], pl.ds(first, rows)))
        first += rows
    loads = [
        pltpu.make_async_copy(source, work.at[at], load_sems.at[i])
        for i, (source, at) in enumerate(sources)
    ]

    page_loads = [
        pltpu.make_async_copy(
            source.at[page, pl.ds(0, KEPT)],
            target.at[pl.ds(page * KEPT, KEPT)],
            page_sems.at[number * pages + page],
        )
        for number, (source, target) in enumerate(((x_in, x), (cot_in, cot)))
        for page in range(pages)
    ]
    page_copies = []

    def pages_out(source, target, number):
        for page in range(pages):
            for i, (piece, at) in enumerate(
                (
                    (source.at[pl.ds(page * KEPT, KEPT)], pl.ds(0, KEPT)),
                    (nothing, pl.ds(KEPT, slots - KEPT)),
                )
            ):
                sem = page_sems.at[2 * pages + (number * pages + page) * 2 + i]
                copy = pltpu.make_async_copy(piece, target.at[page, at], sem)
                copy.start()
                page_copies.append(copy)

    def cast(number):
        return work[number * rows : (number + 1) * rows].astype(LOW)

    def place(*blocks):
        for group, index, number in blocks:
            sq[group, k.z, k.q, index] = cast(number)

    def place_out():
        for j in range(4):
            wd[k.z, k.yy, j // 2, j % 2] = cast(FFN_OUT_ROWS + j)

    def place_in():
        piece = width // 4
        for h in range(2):
            for block in range(2):
                parts = [
                    cast(FFN_IN_ROWS + 2 * block + j)[:, (2 * g + h) * piece : (2 * g + h + 1) * piece]
                    for j in range(2)
                    for g in range(2)
                ]
                halves[h, block] = jnp.concatenate(parts, axis=1)
        fi[k.z, k.q] = halves[k.xx]
        swap("in", halves.at[1 - k.xx], fi.at[k.z, k.q], k.x)

    def start():
        k.greet()
        for copy in loads + page_loads:
            copy.start()
        vecs[k.z, k.q] = jnp.zeros(vecs.shape[2:], FULL)
        for row in range(vec.shape[0]):
            vecs[k.z, k.q, row : row + 1, :rows] = vec[row]
        loads[0].wait()
        place((KV_CROSS, 0, 1), (KV_CROSS, 1, 2))
        k.met()

    def cast1():
        loads[2].wait()
        loads[3].wait()
        place((JOIN, 0, 8), (JOIN, 1, 9))
        place_out()

    def cast2():
        for copy in (loads[1], *loads[4:], *page_loads):
            copy.wait()
        place((QO_CROSS, 0, 0), (QO_CROSS, 1, 6), (QK_SELF, 0, 3), (QK_SELF, 1, 4))
        place((VO_SELF, 0, 5), (VO_SELF, 1, 7))
        place_in()
        nothing[...] = jnp.zeros_like(nothing)
        for one in (k1, v1, k2, v2):
            act[one, pl.ds(count, slots - KEPT)] = jnp.zeros((slots - KEPT, width), LOW)

    def kv0():
        free(0)[...] = times(x[...], weight(KV_CROSS, 0)).astype(LOW)
        swap("keys", free(0), rows_in(k1))

    def kv1():
        free(1)[...] = times(x[...], weight(KV_CROSS, 1)).astype(LOW)
        swap("values", free(1), rows_in(v1))

    def vectors():
        sums = jnp.zeros((8, width), FULL)
        zeros = jnp.zeros((8, width - 128), FULL)
        for d in range(RANKS):
            tile = jnp.concatenate([vecs[d // PLANE, d % PLANE], zeros], axis=1)
            sums = sums + (pltpu.roll(tile, d * rows, 1) if d else tile)
        vw[...] = sums.astype(LOW).astype(FULL)

    def project_q1():
        rows_in(q1)[...] = times(x[...], weight(QO_CROSS, 0)).astype(LOW)
        swapped("keys", "values")

    def ln1():
        acc[...] = times(rows_in(o1)[...], weight(QO_CROSS, 1))

        def step(at, i):
            value = norm(0, at, x[at].astype(FULL) + acc[at] * keep(i))
            res[at] = value
            act[h1, at] = value.astype(LOW)

        by_rows(step)

    def project_self(slot_, group, index):
        rows_in(slot_)[...] = times(rows_in(h1)[...], weight(group, index)).astype(LOW)

    def in_two(step, name, buffer, target, peer):
        half = (count // BLOCK + 1) // 2
        for number, first, last in ((0, 0, half), (1, half, count // BLOCK)):
            by_rows(step, first, last)
            at = pl.ds(first * BLOCK, (last - first) * BLOCK)
            swap((name, number), buffer.at[at], target.at[at], peer)

    def theirs_in_two(name, result, target):
        half = (count // BLOCK + 1) // 2 * BLOCK
        for number, first, size in ((0, 0, half), (1, half, count - half)):
            at = pl.ds(first, size)
            acc[at] = result(pl.ds(count + first, size))
            act[edge, at] = acc[at].astype(LOW)
            swap((name, number), act.at[edge, at], target.at[at], k.x)

    def ln2():
        acc[...] = times(rows_in(o2)[...], weight(VO_SELF, 1))

        def step(at, i):
            del i
            value = norm(1, at, res[at] + acc[at])
            res[at] = value
            h2a[at] = value.astype(LOW)

        in_two(step, H2, h2a, h2a.at[theirs], k.x)

    def ffn_in(whose, block):
        if whose is theirs and block == 0:
            swapped((H2, 0), (H2, 1))
        first = 0 if whose is mine else count
        acc[...] = times(h2a[whose], in_weight(block))

        def step(at, i):
            value = acc[at]
            share = 0.5 + 0.5 * lax.erf(value * (0.5**0.5))
            bell = jnp.exp(value * value * -0.5) * (1.0 / (2.0 * math.pi) ** 0.5)
            to = pl.ds(pl.multiple_of(first + i * BLOCK, BLOCK), BLOCK)
            mid[block, to] = (value * share).astype(LOW)
            slope[block, to] = (share + value * bell).astype(LOW)

        by_rows(step)

    def ffn_out_theirs():
        def rows_of_result(to):
            return times(mid[0, to], out_weight(0)) + times(mid[1, to], out_weight(1))

        theirs_in_two(FFN, rows_of_result, rows_in(back))

    def ffn_out_mine():
        for block in range(2):
            res[...] += times(mid[block, mine], out_weight(block))

    def ln3():
        swapped((FFN, 0), (FFN, 1))

        def step(at, i):
            del i
            value = res[at] + act[back, at].astype(FULL)
            act[state, at] = norm(2, at, value).astype(LOW)

        in_two(step, STATE, rows_in(state), rows_in(far), k.twin)

    def join_own():
        acc[...] = times(rows_in(state)[...], weight(JOIN, 0))

    def join_far():
        swapped((STATE, 0), (STATE, 1))
        acc[...] += times(rows_in(far)[...], weight(JOIN, 1))

    def gate():
        part[...] = jnp.zeros_like(part)

        def step(at, i):
            own = act[state, at].astype(FULL)
            other = act[far, at].astype(FULL)
            share = jax.nn.sigmoid(acc[at] + vector(6))
            mask = row_mask(i)
            grad = cot[at].astype(FULL) * mask
            cot[at] = ((share * own + (1.0 - share) * other) * mask).astype(LOW)
            to_own, to_other = grad * share, grad * (1.0 - share)
            logits = (to_own * (own - other) * (1.0 - share)).astype(LOW)
            ea[at] = logits
            part[0] += fold(logits.astype(FULL))
            res[at] = to_own
            grd[at] = to_other

        by_rows(step)
        vg[6:7, :] = jnp.sum(part[0], axis=0, keepdims=True)
        vg[7:8, :] = jnp.zeros((1, width), FULL)
        pages_out(cot, joined, 0)

    def join_back():
        logits = ea.at[mine]
        rows_in(edge)[...] = (grd[...] + times_transposed(logits[...], weight(JOIN, 1))).astype(LOW)
        swap("edge", rows_in(edge), rows_in(back))

    def join_back_own():
        logits = ea.at[mine]
        res[...] += times_transposed(logits[...], weight(JOIN, 0))

    def join_grad(index):
        square_grad(JOIN, index, rows_in(state + index)[...], rows_in(edge)[...])

    def keep_err(at, i, result):
        del i
        ea[at] = result.astype(LOW)

    def keep_branch(at, i, result):
        ea[at] = (result * keep(i)).astype(LOW)

    def ln3_back():
        swapped("edge")

        def grad(at):
            act[edge, at] = ea[at]
            return res[at] + act[back, at].astype(FULL)

        norm_back(2, grad, keep_err, lambda step: in_two(step, ERR, ea, ea.at[theirs], k.x))

    def hidden_back(whose, block):
        if whose is theirs and block == 0:
            swapped((ERR, 0), (ERR, 1))
        first = 0 if whose is mine else count
        acc[...] = times_transposed(ea[whose], out_weight(block))

        def step(at, i):
            to = pl.ds(pl.multiple_of(first + i * BLOCK, BLOCK), BLOCK)
            slope[block, to] = (acc[at] * slope[block, to].astype(FULL)).astype(LOW)

        by_rows(step)

    def out_grad(block):
        for at in TILES:
            grad = outer(mid[block], ea[:, at]).astype(LOW)
            wd[2 * block : 2 * block + 2, :, :, :, :, at] = grad.reshape(2, 2, 2, 2, rows, TILE)
        if block == 1:
            pl.semaphore_signal(ready, inc=1, device_id=k.twin, device_id_type=MESH)

    def ffn_in_back_theirs():
        def rows_of_result(to):
            one = times_transposed(slope[0, to], in_weight(0))
            return one + times_transposed(slope[1, to], in_weight(1))

        theirs_in_two(FFN_BACK, rows_of_result, rows_in(far))

    def ffn_in_back_mine():
        for block in range(2):
            grd[...] += times_transposed(slope[block, mine], in_weight(block))

    def in_grad(block):
        for at in TILES:
            grad = outer(h2a[...], slope[block, :, at]).astype(LOW)
            fi[:, :, block, :, at] = grad.reshape(LINE, PLANE, rows, TILE)

    def ln2_back():
        swapped((FFN_BACK, 0), (FFN_BACK, 1))
        norm_back(1, lambda at: grd[at] + act[far, at].astype(FULL), keep_err)
        free(0)[...] = times_transposed(ea[mine], weight(VO_SELF, 1)).astype(LOW)
        square_grad(VO_SELF, 1, rows_in(o2)[...], ea[mine])

    def self_back(group, index, which):
        grd[...] += times_transposed(spare(which)[...], weight(group, index))
        square_grad(group, index, rows_in(h1)[...], spare(which)[...])

    def ln1_back():
        norm_back(0, lambda at: grd[at], keep_branch)
        for d in range(RANKS):
            moved = pltpu.roll(vg[...], width - d * rows, 1) if d else vg[...]
            vecs[d // PLANE, d % PLANE] = moved[:, :128]
        free(0)[...] = times_transposed(ea[mine], weight(QO_CROSS, 1)).astype(LOW)
        square_grad(QO_CROSS, 1, rows_in(o1)[...], ea[mine])

    def cross_query_back():
        pl.semaphore_wait(ready, 1)
        swap("back_keys", spare(1), free(2))
        swap("back_values", spare(2), free(3))
        grd[...] += times_transposed(spare(0)[...], weight(QO_CROSS, 0))
        square_grad(QO_CROSS, 0, x[...], spare(0)[...])

    def cross_back(index):
        swapped(("back_keys", "back_values")[index])
        grd[...] += times_transposed(free(2 + index)[...], weight(KV_CROSS, index))
        square_grad(KV_CROSS, index, x[...], free(2 + index)[...])

    def last_cross_back():
        cross_back(1)
        narrow(grd, ea)
        pages_out(ea.at[mine], x_grad, 1)

    start(); gV.L(); gvec.L(); cast1(); gFO.X(); cast2(); gQO.L(); gJ.X(); gV.R(); gvec.R(); gV.X(); gvec.X()
    gQO.R(); gK.L(); gQK.L(); gJ.C(); gQO.X(); gV.C(); gvec.C(); gK.R(); gQK.R(); gVO.L(); gK.X(); gFI.L(); gQO.C()
    gQK.X(); gFO.L(0); gVO.R(); gK.C(); gVO.X(); gFI.R(); gFO.L(1); gQO.F(); gK.F(); kv0(); gV.F(); gvec.F()
    vectors(); kv1(); gQK.C(); project_q1(); attend(0, 0, q1, k1, v1, o1); gVO.C(); attend(1, 0, q1, k1, v1, o1)
    ln1(); gQK.F(); project_self(q2, QK_SELF, 0); gFI.X(); gJ.L(0); project_self(k2, QK_SELF, 1); gVO.F()
    project_self(v2, VO_SELF, 0); gFO.R(0); attend(0, 1, q2, k2, v2, o2); attend(1, 1, q2, k2, v2, o2); ln2()
    gJ.L(1); gFO.R(1); gJ.L(3); gFI.F(); gJ.L(2); ffn_in(theirs, 0); gFO.F(); ffn_in(theirs, 1); ffn_out_theirs()
    gJ.R(0); ffn_in(mine, 0); gJ.R(1); gJ.R(3); ffn_in(mine, 1); ffn_out_mine(); gJ.R(2); ln3(); gJ.F(); join_own()
    join_far(); gate(); join_back(); join_back_own(); ln3_back(); hidden_back(mine, 1); hidden_back(mine, 0)
    join_grad(1); ffn_in_back_mine(); sJ1.C(); join_grad(0); sJ0.C(); hidden_back(theirs, 0); sJ1.X()
    hidden_back(theirs, 1); ffn_in_back_theirs(); in_grad(1); in_grad(0); sFI.C(); sJ1.L(); out_grad(0); sJ1.B()
    out_grad(1); sFO.L(0); ln2_back(); attend_back(0, 1, q2, k2, v2); sFO.B(0); sJ0.X()
    attend_back(1, 1, q2, k2, v2); sJ1.F(); sFI.L(); self_back(VO_SELF, 0, 2); sVO.C(); self_back(QK_SELF, 0, 0)
    sJ0.L(); self_back(QK_SELF, 1, 1); sQK.C(); sFI.B(); ln1_back(); sVO.X(); sFO.L(1)
    attend_back(0, 0, q1, k1, v1); sQK.X(); sJ0.B(); attend_back(1, 0, q1, k1, v1); cross_query_back(); sVO.L()
    sQO.C(); svec.C(); sJ0.F(); sFO.B(1); cross_back(0); sVO.B(); sQO.X(); svec.X(); last_cross_back(); sK.C()
    sQK.L(); sFO.M(1); sQK.B(); sK.X(); sV.C(); sQO.L(); svec.L(); sK.L(); sFO.M(0); sV.X(); sQO.B(); svec.B()
    sQK.F(); sFO.X(); sFI.F(); sK.B(); sV.L(); sV.B(); sFI.G(); sK.F(); sVO.F(); sQO.F(); svec.F(); sFO.F(); sV.F()
    for copy in page_copies:
        copy.wait()
    for item in scatters:
        for copy in item.put.copies:
            copy.wait()


def hand_over(count, *refs):
    sources, targets, rooms, sems = refs[:count], refs[count : 2 * count], refs[2 * count : -1], refs[-1]
    loads = [
        pltpu.make_async_copy(source, room, sems.at[0, i])
        for i, (source, room) in enumerate(zip(sources, rooms))
    ]
    stores = [
        pltpu.make_async_copy(room, target, sems.at[1, i])
        for i, (room, target) in enumerate(zip(rooms, targets))
    ]
    for copy in loads:
        copy.start()
    for load, copy in zip(loads, stores):
        load.wait()
        copy.start()
    for copy in stores:
        copy.wait()


def run_layer(x_in, lengths, drops, proj, outw, fin, fout, join, vectors, cot):
    pages, slots, width = x_in.shape[1:]
    rows = proj.shape[3]
    count = pages * KEPT
    vec = jnp.transpose(vectors, (1, 0, 2))
    vmem = pl.BlockSpec(memory_space=pltpu.VMEM)
    smem = pl.BlockSpec(memory_space=pltpu.SMEM)
    hbm = pl.BlockSpec(memory_space=pl.ANY)
    slab = (2, rows, width)
    scratch = [
        pltpu.VMEM((SQUARES, LINE, PLANE) + slab, LOW),
        pltpu.VMEM((LINE, PLANE) + slab, LOW),
        pltpu.VMEM((LINE, 2, 2) + slab, LOW),
        pltpu.VMEM((2,) + slab, LOW),
        pltpu.VMEM((LINE, PLANE, 8, 128), FULL),
        pltpu.VMEM((CORNER_RING, 2, HALF) + slab, LOW),
        pltpu.VMEM((SIDE_RING, LINE, 2) + slab, LOW),
        pltpu.VMEM((LINE_RING, LINE - 1) + slab, LOW),
        pltpu.VMEM((HOP_RING,) + slab, LOW),
        pltpu.VMEM((2,) + slab, LOW),
        pltpu.VMEM((PAIR_RING, LINE - 1, 2) + slab, LOW),
        pltpu.VMEM((PAIR_RING, 2) + slab, LOW),
        pltpu.VMEM((2, HALF, 8, 128), FULL),
        pltpu.VMEM((2, LINE, 8, 128), FULL),
        pltpu.VMEM((LINE - 1, 8, 128), FULL),
        pltpu.VMEM((8, 128), FULL),
        pltpu.VMEM((8, width), FULL),
        pltpu.VMEM((8, width), FULL),
        pltpu.VMEM((2, 8, width), FULL),
        pltpu.VMEM((count, width), LOW),
        pltpu.VMEM((count, width), LOW),
        pltpu.VMEM((slots - KEPT, width), LOW),
        pltpu.VMEM((2 * count, width), LOW),
        pltpu.VMEM((2 * count, width), LOW),
        pltpu.VMEM((13, count + slots - KEPT, width), LOW),
        pltpu.VMEM((2, 2 * count, width), LOW),
        pltpu.VMEM((2, 2 * count, width), LOW),
        pltpu.VMEM((2, pages * (width // PAIR), 2 * KEPT, slots), LOW),
        pltpu.VMEM((3, count, width), LOW),
        pltpu.VMEM((3, count, 1), FULL),
        pltpu.VMEM((3 * count, width), FULL),
        pltpu.SemaphoreType.DMA((8,)),
        pltpu.SemaphoreType.DMA((6 * pages,)),
        pltpu.SemaphoreType.DMA((18,)),
        pltpu.SemaphoreType.DMA((TRANSFERS,)),
        pltpu.SemaphoreType.DMA((TRANSFERS,)),
        pltpu.SemaphoreType.REGULAR,
    ]
    shapes = (
        ((pages, slots, width), LOW),
        ((pages, slots, width), LOW),
        ((6, rows, width), FULL),
        ((2, rows, width), FULL),
        ((rows, 4 * width), FULL),
        ((4 * rows, width), FULL),
        ((2, rows, width), FULL),
        ((vectors.shape[1], 1, rows), FULL),
    )
    results = pl.pallas_call(
        partial(layer_kernel, rows),
        out_shape=[jax.ShapeDtypeStruct(*shape) for shape in shapes],
        in_specs=[smem, smem] + [hbm] * 7 + [vmem],
        out_specs=[hbm] * 7 + [vmem],
        scratch_shapes=scratch,
        compiler_params=pltpu.CompilerParams(
            collective_id=0, has_side_effects=True, vmem_limit_bytes=VMEM_LIMIT
        ),
    )(
        lengths,
        drops,
        x_in[0],
        cot[0],
        proj.reshape(6 * rows, width),
        outw.reshape(2 * rows, width),
        fin[0],
        fout[0],
        join.reshape(2 * rows, width),
        vec,
    )
    results = pl.pallas_call(
        partial(hand_over, len(shapes)),
        out_shape=[jax.ShapeDtypeStruct(*shape) for shape in shapes],
        in_specs=[hbm] * len(shapes),
        out_specs=[hbm] * len(shapes),
        scratch_shapes=[pltpu.VMEM(*shape) for shape in shapes]
        + [pltpu.SemaphoreType.DMA((2, len(shapes)))],
        compiler_params=pltpu.CompilerParams(vmem_limit_bytes=VMEM_LIMIT),
    )(*results)
    joined, x_grad, proj_g, out_g, fin_g, fout_g, join_g, vec_g = results
    return (
        joined[None],
        x_grad[None],
        proj_g.reshape(proj.shape),
        out_g[None],
        fin_g[None],
        fout_g[None],
        join_g[None],
        jnp.transpose(vec_g, (1, 0, 2)),
    )


def fits(ranks, x_in, proj, fout):
    rows, width = proj.shape[3:]
    return (
        ranks == RANKS
        and x_in.shape[1] == 4
        and x_in.shape[2] == 2 * HEAD
        and rows % 16 == 0
        and rows <= 128
        and width == HEADS * HEAD
        and fout.shape[1] == 4 * rows
    )


def swapped(array, axis, stride):
    return lax.ppermute(array, axis, [(i, i ^ 1 << stride) for i in range(lax.axis_size(axis))])


def product(left, right):
    return jnp.dot(left, right, preferred_element_type=jnp.float32)


def outer_sum(left, right):
    return lax.dot_general(
        left, right, (((0,), (0,)), ((), ())), preferred_element_type=jnp.float32
    )


def times_transposed(left, right):
    return lax.dot_general(
        left, right, (((1,), (1,)), ((), ())), preferred_element_type=jnp.float32
    )


def norm_forward(values, gain, shift):
    centre = values - jnp.mean(values, axis=-1, keepdims=True)
    inverse = lax.rsqrt(jnp.mean(centre * centre, axis=-1, keepdims=True) + EPSILON)
    unit = centre * inverse
    return (unit * gain + shift, unit, inverse)


def norm_backward(grad, unit, inverse, gain):
    scaled = grad * gain
    inner = (
        scaled
        - jnp.mean(scaled, axis=-1, keepdims=True)
        - unit * jnp.mean(scaled * unit, axis=-1, keepdims=True)
    )
    return (inverse * inner, jnp.sum(grad * unit, axis=0), jnp.sum(grad, axis=0))


def heads_view(values, pages):
    return values.reshape(pages, values.shape[0] // pages, HEADS, values.shape[1] // HEADS)


def masked_scores(query, keys, key_mask, pages):
    scale = (query.shape[1] // HEADS) ** (-0.5)
    scores = (
        jnp.einsum(
            "pqhe,pkhe->phqk",
            heads_view(query, pages),
            heads_view(keys, pages),
            preferred_element_type=jnp.float32,
        )
        * scale
    )
    return jnp.where(key_mask[:, None, None, :], scores, -1e30)


def attend_forward(query, keys, values, key_mask, pages):
    scores = masked_scores(query, keys, key_mask, pages)
    top = jnp.max(scores, axis=-1, keepdims=True)
    weights = jnp.exp(scores - top)
    total = jnp.sum(weights, axis=-1, keepdims=True)
    probs = (weights / total).astype(jnp.bfloat16)
    mixed = jnp.einsum(
        "phqk,pkhe->pqhe", probs, heads_view(values, pages), preferred_element_type=jnp.float32
    )
    return (mixed.reshape(query.shape).astype(jnp.bfloat16), top + jnp.log(total))


def attend_backward(grad_out, query, keys, values, key_mask, logsum, pages):
    scale = (query.shape[1] // HEADS) ** (-0.5)
    probs = jnp.exp(masked_scores(query, keys, key_mask, pages) - logsum)
    grad_heads = heads_view(grad_out, pages)
    grad_probs = jnp.einsum(
        "pqhe,pkhe->phqk", grad_heads, heads_view(values, pages), preferred_element_type=jnp.float32
    )
    grad_scores = (
        probs * (grad_probs - jnp.sum(grad_probs * probs, axis=-1, keepdims=True))
    ).astype(jnp.bfloat16)
    grad_query = (
        jnp.einsum(
            "phqk,pkhe->pqhe",
            grad_scores,
            heads_view(keys, pages),
            preferred_element_type=jnp.float32,
        )
        * scale
    )
    grad_keys = (
        jnp.einsum(
            "phqk,pqhe->pkhe",
            grad_scores,
            heads_view(query, pages),
            preferred_element_type=jnp.float32,
        )
        * scale
    )
    grad_values = jnp.einsum(
        "phqk,pqhe->pkhe",
        probs.astype(jnp.bfloat16),
        grad_heads,
        preferred_element_type=jnp.float32,
    )
    shape = query.shape
    return (
        grad_query.reshape(shape).astype(jnp.bfloat16),
        grad_keys.reshape(shape).astype(jnp.bfloat16),
        grad_values.reshape(shape).astype(jnp.bfloat16),
    )


def local(
    x_in,
    lengths,
    drops,
    proj_master,
    out_master,
    ffn_in_master,
    ffn_out_master,
    join_master,
    vectors,
    cotangent,
):
    if fits(lax.axis_size("dp"), x_in, proj_master, ffn_out_master):
        return run_layer(
            x_in,
            lengths,
            drops,
            proj_master,
            out_master,
            ffn_in_master,
            ffn_out_master,
            join_master,
            vectors,
            cotangent,
        )
    pages = x_in.shape[1]
    slots = x_in.shape[2]
    width = x_in.shape[3]
    rows = pages * slots
    gathered = (
        lax.all_gather(proj_master.astype(jnp.bfloat16), "dp", axis=3, tiled=True),
        lax.all_gather(out_master.astype(jnp.bfloat16), "dp", axis=2, tiled=True),
        lax.all_gather(ffn_in_master.astype(jnp.bfloat16), "dp", axis=1, tiled=True),
        lax.all_gather(ffn_out_master.astype(jnp.bfloat16), "dp", axis=1, tiled=True),
        lax.all_gather(join_master.astype(jnp.bfloat16), "dp", axis=2, tiled=True),
        lax.all_gather(vectors.astype(jnp.bfloat16), "dp", axis=2, tiled=True),
    )
    proj_w = gathered[0][0]
    out_w = gathered[1][0]
    ffin_w = gathered[2][0]
    ffout_w = gathered[3][0]
    join_w = gathered[4][0]
    vec_w = gathered[5][0].astype(jnp.float32)
    key_mask = jnp.arange(slots, dtype=jnp.int32)[None, :] < lengths[:, None]
    row_mask = key_mask.reshape(rows, 1).astype(jnp.float32)
    keep = (1 - drops).astype(jnp.float32)
    keep_rows = jnp.broadcast_to(keep[:, None], (pages, slots)).reshape(rows, 1)
    source = x_in[0].reshape(rows, width)
    own_keys = product(source, proj_w[0, 1]).astype(jnp.bfloat16)
    own_values = product(source, proj_w[0, 2]).astype(jnp.bfloat16)
    far_keys, far_values = swapped((own_keys, own_values), "stream", 0)
    cross_query = product(source, proj_w[0, 0]).astype(jnp.bfloat16)
    cross_out, cross_logsum = attend_forward(cross_query, far_keys, far_values, key_mask, pages)
    first, unit_one, inverse_one = norm_forward(
        source.astype(jnp.float32) + product(cross_out, out_w[0]) * keep_rows, vec_w[0], vec_w[1]
    )
    first_low = first.astype(jnp.bfloat16)
    self_query = product(first_low, proj_w[1, 0]).astype(jnp.bfloat16)
    self_keys = product(first_low, proj_w[1, 1]).astype(jnp.bfloat16)
    self_values = product(first_low, proj_w[1, 2]).astype(jnp.bfloat16)
    self_out, self_logsum = attend_forward(self_query, self_keys, self_values, key_mask, pages)
    second, unit_two, inverse_two = norm_forward(
        first + product(self_out, out_w[1]), vec_w[2], vec_w[3]
    )
    second_low = second.astype(jnp.bfloat16)
    hidden = product(second_low, ffin_w)
    gelu_exact = partial(jax.nn.gelu, approximate=False)
    active_f32, gelu_pull = jax.vjp(gelu_exact, hidden)
    active = active_f32.astype(jnp.bfloat16)
    third, unit_three, inverse_three = norm_forward(
        second + product(active, ffout_w), vec_w[4], vec_w[5]
    )
    state = third.astype(jnp.bfloat16)
    far_state = swapped(state, "stream", 0)
    state_f32 = state.astype(jnp.float32)
    far_f32 = far_state.astype(jnp.float32)
    gate = jax.nn.sigmoid(product(state, join_w[0]) + product(far_state, join_w[1]) + vec_w[6])
    joined = ((gate * state_f32 + (1.0 - gate) * far_f32) * row_mask).astype(jnp.bfloat16)
    grad_joined = cotangent[0].reshape(rows, width).astype(jnp.float32) * row_mask
    grad_logits = (grad_joined * (state_f32 - far_f32) * gate * (1.0 - gate)).astype(jnp.bfloat16)
    grad_join = jnp.stack([outer_sum(state, grad_logits), outer_sum(far_state, grad_logits)])
    grad_bias = jnp.sum(grad_logits.astype(jnp.float32), axis=0)
    grad_far = (grad_joined * (1.0 - gate) + times_transposed(grad_logits, join_w[1])).astype(
        jnp.bfloat16
    )
    returned = swapped(grad_far, "stream", 0)
    grad_third = (
        grad_joined * gate + times_transposed(grad_logits, join_w[0]) + returned.astype(jnp.float32)
    )
    grad_res3, gain_three, shift_three = norm_backward(
        grad_third, unit_three, inverse_three, vec_w[4]
    )
    grad_res3_low = grad_res3.astype(jnp.bfloat16)
    grad_ffout = outer_sum(active, grad_res3_low)
    grad_hidden = gelu_pull(times_transposed(grad_res3_low, ffout_w))[0].astype(jnp.bfloat16)
    grad_ffin = outer_sum(second_low, grad_hidden)
    grad_second = grad_res3 + times_transposed(grad_hidden, ffin_w)
    grad_res2, gain_two, shift_two = norm_backward(grad_second, unit_two, inverse_two, vec_w[2])
    grad_res2_low = grad_res2.astype(jnp.bfloat16)
    grad_out_self = outer_sum(self_out, grad_res2_low)
    grad_self_out = times_transposed(grad_res2_low, out_w[1]).astype(jnp.bfloat16)
    grad_q2, grad_k2, grad_v2 = attend_backward(
        grad_self_out, self_query, self_keys, self_values, key_mask, self_logsum, pages
    )
    grad_proj_self = jnp.stack(
        [
            outer_sum(first_low, grad_q2),
            outer_sum(first_low, grad_k2),
            outer_sum(first_low, grad_v2),
        ]
    )
    grad_first = (
        grad_res2
        + times_transposed(grad_q2, proj_w[1, 0])
        + times_transposed(grad_k2, proj_w[1, 1])
        + times_transposed(grad_v2, proj_w[1, 2])
    )
    grad_res1, gain_one, shift_one = norm_backward(grad_first, unit_one, inverse_one, vec_w[0])
    grad_branch = (grad_res1 * keep_rows).astype(jnp.bfloat16)
    grad_out_cross = outer_sum(cross_out, grad_branch)
    grad_cross_out = times_transposed(grad_branch, out_w[0]).astype(jnp.bfloat16)
    grad_q1, grad_far_keys, grad_far_values = attend_backward(
        grad_cross_out, cross_query, far_keys, far_values, key_mask, cross_logsum, pages
    )
    back_keys, back_values = swapped((grad_far_keys, grad_far_values), "stream", 0)
    grad_proj_cross = jnp.stack(
        [outer_sum(source, grad_q1), outer_sum(source, back_keys), outer_sum(source, back_values)]
    )
    grad_source = (
        grad_res1
        + times_transposed(grad_q1, proj_w[0, 0])
        + times_transposed(back_keys, proj_w[0, 1])
        + times_transposed(back_values, proj_w[0, 2])
    )
    grad_proj = jnp.stack([grad_proj_cross, grad_proj_self])[None]
    grad_out = jnp.stack([grad_out_cross, grad_out_self])[None]
    grad_vectors = jnp.stack(
        [gain_one, shift_one, gain_two, shift_two, gain_three, shift_three, grad_bias]
    )[None]
    all_sums = (
        lax.psum_scatter(grad_proj, "dp", scatter_dimension=3, tiled=True),
        lax.psum_scatter(grad_out, "dp", scatter_dimension=2, tiled=True),
        lax.psum_scatter(grad_ffin[None], "dp", scatter_dimension=1, tiled=True),
        lax.psum_scatter(grad_ffout[None], "dp", scatter_dimension=1, tiled=True),
        lax.psum_scatter(grad_join[None], "dp", scatter_dimension=2, tiled=True),
        lax.psum_scatter(grad_vectors, "dp", scatter_dimension=2, tiled=True),
    )
    proj_part, out_part, ffin_part, ffout_part, join_part, vectors_part = all_sums
    joined_out = joined.reshape(1, pages, slots, width)
    x_grad = grad_source.astype(jnp.bfloat16).reshape(1, pages, slots, width)
    return (joined_out, x_grad, proj_part, out_part, ffin_part, ffout_part, join_part, vectors_part)


def solution(mesh):
    placed = (
        P("stream", "dp", None, None),
        P("dp"),
        P("dp"),
        P("stream", None, None, "dp", None),
        P("stream", None, "dp", None),
        P("stream", "dp", None),
        P("stream", "dp", None),
        P("stream", None, "dp", None),
        P("stream", None, "dp"),
        P("stream", "dp", None, None),
    )
    return jax.shard_map(
        local,
        mesh=mesh,
        in_specs=placed,
        out_specs=(
            P("stream", "dp", None, None),
            P("stream", "dp", None, None),
            P("stream", None, None, "dp", None),
            P("stream", None, "dp", None),
            P("stream", "dp", None),
            P("stream", "dp", None),
            P("stream", None, "dp", None),
            P("stream", None, "dp"),
        ),
        check_vma=False,
    )
```

```python
import math
from functools import partial

import jax
import jax.numpy as jnp
from jax import lax
from jax.experimental import pallas as pl
from jax.experimental.pallas import tpu as pltpu
from jax.sharding import PartitionSpec as P

HEADS = 12

EPSILON = 1e-05
VMEM_LIMIT = 62 * 2**20
TRANSFERS = 300
MESH = pl.DeviceIdType.MESH
LOW = jnp.bfloat16
FULL = jnp.float32
LINE, PLANE = 4, 4
RANKS = LINE * PLANE
HALF = LINE // 2
KV_CROSS, QO_CROSS, QK_SELF, VO_SELF, JOIN = range(5)
SQUARES = 5
FFN_OUT_ROWS, FFN_IN_ROWS = 10, 14
ITEMS = (
    (KV_CROSS, 0, 1),
    (KV_CROSS, 1, 1),
    (QO_CROSS, 0, 2),
    (QK_SELF, 0, 2),
    (VO_SELF, 0, 2),
    (JOIN, 0, 2),
    (JOIN, 0, 1),
    (JOIN, 1, 1),
)
VECTORS = None
H2, FFN, STATE, ERR, FFN_BACK = range(5)
CORNER_RING, SIDE_RING, LINE_RING, HOP_RING, PAIR_RING = 3, 4, 5, 5, 3
BLOCK = 64
KEPT = 112
TILE = 256
TILES = tuple(pl.ds(at, TILE) for at in range(0, 768, TILE))
HEAD = 64
PAIR = 2 * HEAD


class Links:
    def __init__(self, send_sems, recv_sems):
        self.stream = lax.axis_index("stream")
        self.me = lax.axis_index("dp")
        self.z = self.me // PLANE
        self.q = self.me % PLANE
        self.qx = self.q + 1 - 2 * (self.q % 2)
        self.qy = (self.q + 2) % PLANE
        self.qd = PLANE - 1 - self.q
        self.xx, self.yy = self.q % 2, self.q // 2
        self.columns = (self.q, self.qx, self.qy, self.qd)
        self.z_near = self.z + 1 - 2 * (self.z % 2)
        self.z_two = (self.z + 2) % LINE
        self.z_third = LINE - 1 - self.z
        self.middle = (self.z == 1) | (self.z == 2)
        self.x = (self.stream, self.z * PLANE + self.qx)
        self.y = (self.stream, self.z * PLANE + self.qy)
        self.near, self.two, self.third = (
            (self.stream, at * PLANE + self.q) for at in (self.z_near, self.z_two, self.z_third)
        )
        self.twin = (1 - self.stream, self.me)
        self.sems = (send_sems, recv_sems)
        self.used = 0

    def greet(self):
        for peer in (self.x, self.y, self.near, self.two, self.third, self.twin):
            pl.semaphore_signal(
                pltpu.get_barrier_semaphore(), inc=1, device_id=peer, device_id_type=MESH
            )

    def met(self):
        pl.semaphore_wait(pltpu.get_barrier_semaphore(), 6)

    def copy(self, source, target, peer, landing=None):
        number = self.used
        self.used += 1
        return pltpu.make_async_remote_copy(
            src_ref=source,
            dst_ref=target,
            send_sem=self.sems[0].at[number],
            recv_sem=self.sems[1].at[number if landing is None else landing],
            device_id=peer,
            device_id_type=MESH,
        )

    def send(self, source, target, peer):
        copy = self.copy(source, target, peer)
        copy.start()
        return copy


class LineGather:
    def __init__(self, view, links):
        self.view, self.k = view, links

    def launch(self):
        k = self.k
        own = self.view(k.z)
        self.near = k.send(own, own, k.near)
        self.two = k.send(own, own, k.two)
        landing = k.used
        self.third = k.copy(own, own, k.third)
        passed = self.view(k.z_two)
        self.passed = k.copy(passed, passed, k.near, landing)
        pl.when(k.middle)(self.third.start)

    def relay(self):
        self.two.wait_recv()
        pl.when(self.k.middle)(self.passed.start)

    def arrive(self):
        self.near.wait_recv()
        self.third.wait_recv()

    def drain(self):
        self.near.wait_send()
        self.two.wait_send()

        @pl.when(self.k.middle)
        def _():
            self.third.wait_send()
            self.passed.wait_send()


class LineSum:
    def __init__(self, view, room, links, straight=False):
        self.view, self.room, self.k, self.straight = view, room, links, straight

    def launch(self):
        k = self.k
        self.spots, self.hop = self.room()
        self.near = k.send(self.view(k.z_near), self.spots(0), k.near)
        away = self.view(k.z_third)
        self.third = k.copy(away, self.spots(2), k.third)
        if self.straight:
            self.third.start()
            self.two = k.send(self.view(k.z_two), self.spots(1), k.two)
            return
        self.passed = k.copy(away, self.hop, k.near)
        pl.when(k.middle)(self.third.start)
        pl.when(jnp.logical_not(k.middle))(self.passed.start)

    def bridge(self):
        k = self.k
        if self.straight:
            return
        part = self.view(k.z_two)

        @pl.when(k.middle)
        def _():
            self.passed.wait_recv()
            part[...] = total(part, self.hop).astype(part.dtype)

        self.two = k.send(part, self.spots(1), k.two)

    def collect(self, put):
        k = self.k
        self.near.wait_recv()
        self.two.wait_recv()
        terms = [self.view(k.z), self.spots(0), self.spots(1)]
        if self.straight:
            self.third.wait_recv()
            put(total(*terms, self.spots(2)))
            return

        @pl.when(k.middle)
        def _():
            self.third.wait_recv()
            put(total(*terms, self.spots(2)))

        pl.when(jnp.logical_not(k.middle))(lambda: put(total(*terms)))

    def drain(self):
        self.near.wait_send()
        self.two.wait_send()
        if self.straight:
            self.third.wait_send()
            return
        pl.when(self.k.middle)(self.third.wait_send)
        pl.when(jnp.logical_not(self.k.middle))(self.passed.wait_send)


class GatherByLine:
    def __init__(self, view, links):
        self.view, self.k = view, links
        self.line = LineGather(lambda z: view(z, links.q), links)

    def L(self):
        self.line.launch()

    def R(self):
        self.line.relay()

    def X(self):
        k = self.k
        self.line.arrive()
        column = self.view(slice(None), k.q)
        self.sides = [k.send(column, column, k.x), k.send(column, column, k.y)]

    def C(self):
        k = self.k
        for copy in self.sides:
            copy.wait_recv()
        one, two = self.view(slice(0, HALF), k.qx), self.view(slice(HALF, LINE), k.qy)
        self.corners = [k.send(one, one, k.y), k.send(two, two, k.x)]

    def F(self):
        for copy in self.corners:
            copy.wait_recv()
        for copy in self.sides + self.corners:
            copy.wait_send()
        self.line.drain()


class GatherByPlane:
    def __init__(self, view, links, size):
        self.view, self.k, self.size = view, links, size
        self.lines = [
            LineGather(partial(lambda q, z: view(z, q), q), links) for q in links.columns
        ]

    def X(self):
        k = self.k
        own = self.view(k.z, k.q)
        self.sides = [k.send(own, own, k.x), k.send(own, own, k.y)]

    def C(self):
        k = self.k
        for copy in self.sides:
            copy.wait_recv()
        one = self.view(k.z, k.qx, 0, 1)
        self.corners = [k.send(one, one, k.y)]
        if self.size == 2:
            two = self.view(k.z, k.qy, 1, 1)
            self.corners.append(k.send(two, two, k.x))

    def L(self, column):
        if column == 3:
            for copy in self.corners:
                copy.wait_recv()
        self.lines[column].launch()

    def R(self, column):
        self.lines[column].relay()

    def F(self):
        for line in self.lines:
            line.arrive()
        for line in self.lines:
            line.drain()
        for copy in self.sides + self.corners:
            copy.wait_send()


class ScatterByPlane:
    def __init__(self, view, room, put, links, straight):
        self.view, self.room, self.put, self.k = view, room, put, links
        self.line = LineSum(lambda z: view(z, links.q), room.line, links, straight)

    def C(self):
        k = self.k
        self.corners, self.sides = self.room.plane()
        low, high = slice(0, HALF), slice(HALF, LINE)
        self.one = [
            k.send(self.view(low, k.qd), self.corners(0), k.x),
            k.send(self.view(high, k.qd), self.corners(1), k.y),
        ]
        self.two = [
            k.send(self.view(low, k.qx), self.sides(0, low), k.x),
            k.send(self.view(high, k.qy), self.sides(1, high), k.y),
        ]

    def X(self):
        k = self.k
        low, high = slice(0, HALF), slice(HALF, LINE)
        for number, half, q in ((0, low, k.qy), (1, high, k.qx)):
            self.one[number].wait_recv()
            part = self.view(half, q)
            part[...] = total(part, self.corners(number)).astype(part.dtype)
        self.two += [
            k.send(self.view(high, k.qx), self.sides(0, high), k.x),
            k.send(self.view(low, k.qy), self.sides(1, low), k.y),
        ]

    def L(self):
        k = self.k
        for copy in self.two:
            copy.wait_recv()
        part = self.view(slice(None), k.q)
        everything = slice(None)
        part[...] = total(part, self.sides(0, everything), self.sides(1, everything)).astype(part.dtype)
        self.line.launch()

    def B(self):
        self.line.bridge()

    def F(self):
        self.line.collect(self.put.sums)
        self.put.store()
        for copy in self.one + self.two:
            copy.wait_send()
        self.line.drain()


class PairGatherByLine:
    def __init__(self, view, links, first=None):
        self.view, self.k, self.first = view, links, first
        self.line = LineGather(lambda z: view(z, links.yy), links)

    def L(self):
        if self.first is not None:
            self.first().wait_recv()
        self.line.launch()

    def R(self):
        self.line.relay()

    def X(self):
        k = self.k
        self.line.arrive()
        column = self.view(slice(None), k.yy)
        self.side = k.send(column, column, k.y)

    def F(self):
        self.side.wait_recv()
        self.side.wait_send()
        self.line.drain()
        if self.first is not None:
            self.first().wait_send()


class PairGatherByPlane:
    def __init__(self, view, links):
        self.view, self.k = view, links
        self.lines = [
            LineGather(partial(lambda y, z: view(z, y), y), links) for y in (links.yy, 1 - links.yy)
        ]

    def X(self):
        k = self.k
        own = self.view(k.z, k.yy)
        self.side = k.send(own, own, k.y)

    def L(self, row):
        if row == 1:
            self.side.wait_recv()
        self.lines[row].launch()

    def R(self, row):
        self.lines[row].relay()

    def F(self):
        for line in self.lines:
            line.arrive()
        for line in self.lines:
            line.drain()
        self.side.wait_send()


class PairScatterByPlane:
    def __init__(self, view, room, put, links):
        self.view, self.room, self.put, self.k = view, room, put, links
        self.line = LineSum(lambda z: view(z, links.yy), room.line, links)

    def C(self):
        k = self.k
        self.side = self.room.column()
        self.two = k.send(self.view(slice(None), 1 - k.yy), self.side, k.y)

    def L(self):
        k = self.k
        self.two.wait_recv()
        part = self.view(slice(None), k.yy)
        part[...] = total(part, self.side).astype(part.dtype)
        self.line.launch()

    def B(self):
        self.line.bridge()

    def F(self):
        self.line.collect(self.put.sums)
        self.put.store()
        self.two.wait_send()
        self.line.drain()

    def G(self):
        self.put.G()


class PairScatterByLine:
    def __init__(self, view, side, room, put, links):
        self.view, self.side, self.put, self.k = view, side, put, links
        self.rows = (1 - links.yy, links.yy)
        self.lines = [
            LineSum(partial(lambda y, z: view(z, y), y), room.line, links) for y in self.rows
        ]

    def L(self, row):
        self.lines[row].launch()

    def B(self, row):
        self.lines[row].bridge()

    def M(self, row):
        part = self.view(self.k.z, self.rows[row])

        def put(value):
            part[...] = value.astype(part.dtype)

        self.lines[row].collect(put)

    def X(self):
        k = self.k
        self.two = k.send(self.view(k.z, 1 - k.yy), self.side, k.y)

    def F(self):
        k = self.k
        self.two.wait_recv()
        self.put.sums(total(self.view(k.z, k.yy), self.side))
        self.put.store()
        self.two.wait_send()
        for line in self.lines:
            line.drain()


def total(*refs):
    result = refs[0][...].astype(FULL)
    for ref in refs[1:]:
        result = result + ref[...].astype(FULL)
    return result


class Room:
    def __init__(self, size, corners, sides, lines, hops, used):
        self.size, self.used = size, used
        self.corners, self.sides, self.lines, self.hops = corners, sides, lines, hops

    def slot(self, ring):
        number = self.used.setdefault(id(ring), 0)
        self.used[id(ring)] += 1
        return ring.at[number % ring.shape[0]]

    def column(self):
        return self.slot(self.sides)

    def plane(self):
        corners, sides = self.slot(self.corners), self.slot(self.sides)
        some = pl.ds(0, self.size)
        return (lambda n: corners.at[n, :, some]), (lambda n, half: sides.at[half, n, some])

    def line(self):
        lines, hops = self.slot(self.lines), self.slot(self.hops)
        some = pl.ds(0, self.size)
        return (lambda n: lines.at[n, some]), hops.at[some]


class VectorRoom(Room):
    def plane(self):
        return (lambda n: self.corners.at[n]), (lambda n, half: self.sides.at[n, half])

    def line(self):
        return (lambda n: self.lines.at[n]), self.hops


class Put:
    def __init__(self, stage, targets, sems, first):
        self.stage, self.targets, self.sems, self.first = stage, targets, sems, first
        self.copies = []

    def sums(self, values):
        for i in range(len(self.targets)):
            self.stage(i)[...] = values[i]

    def store(self):
        for i, target in enumerate(self.targets):
            copy = pltpu.make_async_copy(self.stage(i), target, self.sems.at[self.first + i])
            copy.start()
            self.copies.append(copy)


class PutVectors:
    def __init__(self, target):
        self.target, self.copies = target, []

    def sums(self, values):
        rows, _, width = self.target.shape
        for row in range(rows):
            self.target[row] = values[row : row + 1, :width]

    def store(self):
        pass


def layer_kernel(
    rows,
    lengths,
    drops,
    x_in,
    cot_in,
    proj,
    outw,
    fin,
    fout,
    join,
    vec,
    joined,
    x_grad,
    proj_g,
    out_g,
    fin_g,
    fout_g,
    join_g,
    vec_g,
    sq,
    fi,
    wd,
    halves,
    vecs,
    corners,
    sides,
    lines,
    hops,
    side_room,
    pair_lines,
    pair_hops,
    vcorners,
    vsides,
    vlines,
    vhop,
    vw,
    vg,
    part,
    x,
    cot,
    nothing,
    h2a,
    ea,
    act,
    mid,
    slope,
    probs,
    unit,
    inv,
    work,
    load_sems,
    page_sems,
    store_sems,
    send_sems,
    recv_sems,
    ready,
):
    k = Links(send_sems, recv_sems)
    width = sq.shape[-1]
    count = x.shape[0]
    pages, slots = x_in.shape[:2]
    pairs = width // PAIR
    scale = HEAD**-0.5
    (k1, v1, q1, o1, h1, q2, k2, v2, o2, state, far, edge, back) = range(13)
    mine, theirs = pl.ds(0, count), pl.ds(count, count)
    acc, res, grd = (work.at[pl.ds(i * count, count)] for i in range(3))

    def weight(group, index):
        return sq[group, :, :, index].reshape(width, width)

    def in_weight(block):
        return fi[:, :, block].reshape(width, width)

    def out_weight(block):
        return wd[2 * block : 2 * block + 2].reshape(width, width)

    def free(slot):
        return mid.at[slot // 2, pl.ds((slot % 2) * count, count)]

    def spare(slot):
        return slope.at[slot // 2, pl.ds((slot % 2) * count, count)]

    def times(left, right):
        return jnp.dot(left, right, preferred_element_type=FULL)

    def times_transposed(left, right):
        return lax.dot_general(left, right, (((1,), (1,)), ((), ())), preferred_element_type=FULL)

    def outer(left, right):
        return lax.dot_general(left, right, (((0,), (0,)), ((), ())), preferred_element_type=FULL)

    def loop(first, last, body):
        def step(i, carry):
            body(i)
            return carry

        lax.fori_loop(first, last, step, 0)

    def by_rows(body, first=0, last=None):
        def step(i):
            body(pl.ds(pl.multiple_of(i * BLOCK, BLOCK), BLOCK), i)

        loop(first, count // BLOCK if last is None else last, step)

    def rows_of(i):
        return lax.broadcasted_iota(jnp.int32, (BLOCK, 1), 0) + i * BLOCK

    def narrow(source, target):
        def step(at, i):
            del i
            target[at] = source[at].astype(LOW)

        by_rows(step)

    def row_mask(i):
        row, mask = rows_of(i), jnp.zeros((BLOCK, 1), FULL)
        for page in range(pages):
            first = page * KEPT
            mask = jnp.where((row >= first) & (row < first + lengths[page]), 1.0, mask)
        return mask

    def keep(i):
        row, kept = rows_of(i), jnp.zeros((BLOCK, 1), FULL)
        for page in range(pages):
            kept = jnp.where(row >= page * KEPT, (1 - drops[page]).astype(FULL), kept)
        return kept

    def rows_in(slot):
        return act.at[slot, pl.ds(0, count)]

    def vector(row):
        return vw[row : row + 1, :]

    def norm(number, at, values):
        centre = values - jnp.mean(values, axis=-1, keepdims=True)
        inverse = lax.rsqrt(jnp.mean(centre * centre, axis=-1, keepdims=True) + EPSILON)
        plain = centre * inverse
        unit[number, at] = plain.astype(LOW)
        inv[number, at] = inverse
        return plain * vector(2 * number) + vector(2 * number + 1)

    def fold(values):
        return jnp.sum(values.reshape(BLOCK // 8, 8, width), axis=0)

    def norm_back(number, grad, after, run=None):
        part[...] = jnp.zeros_like(part)

        def step(at, i):
            value = grad(at)
            plain = unit[number, at].astype(FULL)
            part[0] += fold(value * plain)
            part[1] += fold(value)
            scaled = value * vector(2 * number)
            inner = (
                scaled
                - jnp.mean(scaled, axis=-1, keepdims=True)
                - plain * jnp.mean(scaled * plain, axis=-1, keepdims=True)
            )
            result = inv[number, at] * inner
            grd[at] = result
            after(at, i, result)

        (by_rows if run is None else run)(step)
        for i in range(2):
            vg[2 * number + i : 2 * number + i + 1, :] = jnp.sum(part[i], axis=0, keepdims=True)

    def split_heads(values):
        first = lax.broadcasted_iota(jnp.int32, values.shape, 1) < HEAD
        zero = jnp.zeros_like(values)
        return jnp.concatenate([jnp.where(first, values, zero), jnp.where(first, zero, values)], axis=0)

    def join_heads(values):
        first = lax.broadcasted_iota(jnp.int32, (KEPT, PAIR), 1) < HEAD
        return jnp.where(first, values[:KEPT], values[KEPT:])

    def by_heads(half, body):
        group = 6

        def step(i):
            page = i // (pairs // group)
            start = pl.multiple_of(page * KEPT, KEPT)
            at, keys_at = pl.ds(start, KEPT), pl.ds(start, slots)
            for j in range(group):
                pair = (i % (pairs // group)) * group + j
                lanes = pl.ds(pl.multiple_of(pair * PAIR, PAIR), PAIR)
                body(page, at, keys_at, lanes, i * group + j)

        steps = pages * (pairs // group)
        loop(half * (steps // 2), steps if half else steps // 2, step)

    def attend(half, which, query, keys, values, result):
        def body(page, at, keys_at, lanes, number):
            scores = times_transposed(split_heads(act[query, at, lanes]), act[keys, keys_at, lanes]) * scale
            spot = lax.broadcasted_iota(jnp.int32, scores.shape, 1)
            scores = jnp.where(spot < lengths[page], scores, -1e30)
            weights = jnp.exp(scores - jnp.max(scores, axis=-1, keepdims=True))
            chance = weights * (1.0 / jnp.sum(weights, axis=-1, keepdims=True))
            chance = chance.astype(LOW)
            probs[which, number] = chance
            act[result, at, lanes] = join_heads(times(chance, act[values, keys_at, lanes])).astype(LOW)

        by_heads(half, body)

    def attend_back(half, which, query, keys, values):
        grad, to_query, to_keys, to_values = free(0), spare(0), spare(1), spare(2)

        def body(page, at, keys_at, lanes, number):
            del page
            chance = probs[which, number]
            spread = split_heads(grad[at, lanes])
            pull = times_transposed(spread, act[values, keys_at, lanes])
            wide_chance = chance.astype(FULL)
            inner = pull - jnp.sum(pull * wide_chance, axis=-1, keepdims=True)
            delta = (wide_chance * inner).astype(LOW)
            to_query[at, lanes] = (join_heads(times(delta, act[keys, keys_at, lanes])) * scale).astype(LOW)
            key_grad = outer(delta, split_heads(act[query, at, lanes]))[:KEPT]
            to_keys[at, lanes] = (key_grad * scale).astype(LOW)
            to_values[at, lanes] = outer(chance, spread)[:KEPT].astype(LOW)

        by_heads(half, body)

    def square_grad(group, index, left, right):
        sq[group, :, :, index] = outer(left, right).astype(LOW).reshape(LINE, PLANE, rows, width)

    def view(item):
        if item is VECTORS:
            return lambda z, q: vecs.at[z, q]
        group, start, size = item
        return lambda z, q, first=0, some=size: sq.at[group, z, q, pl.ds(start + first, some)]

    def outputs(item):
        group, start, size = item
        places = []
        for i in range(start, start + size):
            if group == JOIN:
                places.append(join_g.at[i])
            elif group == KV_CROSS:
                places.append(proj_g.at[1 + i])
            elif group == QK_SELF:
                places.append(proj_g.at[3 + i])
            elif i == 1:
                places.append(out_g.at[0 if group == QO_CROSS else 1])
            else:
                places.append(proj_g.at[0 if group == QO_CROSS else 5])
        return places

    def put_for(item):
        if item is VECTORS:
            return PutVectors(vec_g)
        first = 2 * item[0] + item[1]
        return Put(lambda i: work.at[pl.ds((first + i) * rows, rows)], outputs(item), store_sems, first)

    used = {}

    def gather(item):
        return GatherByLine(view(item), k)

    def gather_by_plane(item):
        return GatherByPlane(view(item), k, item[2])

    def keep_scatter(item):
        scatters.append(item)
        return item

    def scatter(item, straight=False):
        if item is VECTORS:
            room = VectorRoom(0, vcorners, vsides, vlines, vhop, used)
        else:
            room = Room(item[2], corners, sides, lines, hops, used)
        return keep_scatter(ScatterByPlane(view(item), room, put_for(item), k, straight))

    def out_view(z, y):
        return wd.at[z, y]

    def in_view(z, y):
        return fi.at[z, pl.ds(2 * y, 2)]

    def stage_of(first):
        return lambda i: work.at[pl.ds((first + i) * rows, rows)]

    class PutOut(Put):
        def sums(self, values):
            for i in range(4):
                self.stage(i)[...] = values[i // 2, i % 2]

    class PutIn(Put):
        def sums(self, values):
            for i in range(4):
                self.stage(i)[...] = values[i // 2, i % 2]

        def two_rows(self, first, x_):
            return work.at[pl.ds(pl.multiple_of((first + 2 * x_) * rows, rows), 2 * rows)]

        def half(self, h, block):
            return work[(2 * h + block) * rows : (2 * h + block + 1) * rows]

        def store(self):
            self.two_rows(0, k.xx)[...] = self.two_rows(FFN_IN_ROWS, k.xx)[...]
            other = self.two_rows(FFN_IN_ROWS, 1 - k.xx)[...]
            halves[0] = other.astype(LOW).reshape(2, rows, width)
            self.swap = k.send(halves.at[0], halves.at[1], k.x)

        def G(self):
            self.swap.wait()
            other = halves[1].astype(FULL).reshape(2 * rows, width)
            self.two_rows(0, 1 - k.xx)[...] = other
            piece = width // 4
            for j in range(4):
                block, first = j // 2, (j % 2) * 2 * piece
                parts = [
                    self.half(h, block)[:, first + g * piece : first + (g + 1) * piece]
                    for g in range(2)
                    for h in range(2)
                ]
                self.stage(j)[...] = jnp.concatenate(parts, axis=1)
            Put.store(self)

    scatters = []
    pair_room = Room(2, corners, sides, pair_lines, pair_hops, used)
    put_out = PutOut(
        stage_of(FFN_OUT_ROWS),
        [fout_g.at[pl.ds(i * rows, rows)] for i in range(4)],
        store_sems,
        FFN_OUT_ROWS,
    )
    put_in = PutIn(
        stage_of(FFN_IN_ROWS),
        [fin_g.at[:, pl.ds(i * width, width)] for i in range(4)],
        store_sems,
        FFN_IN_ROWS,
    )
    gFO = PairGatherByPlane(out_view, k)
    gFI = PairGatherByLine(in_view, k, lambda: swaps["in"])
    sFO = keep_scatter(PairScatterByLine(out_view, side_room, pair_room, put_out, k))
    sFI = keep_scatter(PairScatterByPlane(in_view, pair_room, put_in, k))
    gK = gather(ITEMS[0])
    gV = gather(ITEMS[1])
    gQO = gather(ITEMS[2])
    gQK = gather(ITEMS[3])
    gVO = gather(ITEMS[4])
    gJ = gather_by_plane(ITEMS[5])
    gvec = gather(VECTORS)
    sK = scatter(ITEMS[0])
    sV = scatter(ITEMS[1])
    sQO = scatter(ITEMS[2])
    sQK = scatter(ITEMS[3])
    sVO = scatter(ITEMS[4])
    sJ0 = scatter(ITEMS[6])
    sJ1 = scatter(ITEMS[7])
    svec = scatter(VECTORS)
    swaps = {}

    def swap(name, source, target, peer=None):
        swaps[name] = k.send(source, target, k.twin if peer is None else peer)

    def swapped(*names):
        for name in names:
            swaps[name].wait()

    sources, first = [], 0
    for shard in (proj, outw, join, fout):
        sources.append((shard, pl.ds(first, shard.shape[0])))
        first += shard.shape[0]
    for j in range(4):
        sources.append((fin.at[:, pl.ds(j * width, width)], pl.ds(first, rows)))
        first += rows
    loads = [
        pltpu.make_async_copy(source, work.at[at], load_sems.at[i])
        for i, (source, at) in enumerate(sources)
    ]

    page_loads = [
        pltpu.make_async_copy(
            source.at[page, pl.ds(0, KEPT)],
            target.at[pl.ds(page * KEPT, KEPT)],
            page_sems.at[number * pages + page],
        )
        for number, (source, target) in enumerate(((x_in, x), (cot_in, cot)))
        for page in range(pages)
    ]
    page_copies = []

    def pages_out(source, target, number):
        for page in range(pages):
            for i, (piece, at) in enumerate(
                (
                    (source.at[pl.ds(page * KEPT, KEPT)], pl.ds(0, KEPT)),
                    (nothing, pl.ds(KEPT, slots - KEPT)),
                )
            ):
                sem = page_sems.at[2 * pages + (number * pages + page) * 2 + i]
                copy = pltpu.make_async_copy(piece, target.at[page, at], sem)
                copy.start()
                page_copies.append(copy)

    def cast(number):
        return work[number * rows : (number + 1) * rows].astype(LOW)

    def place(*blocks):
        for group, index, number in blocks:
            sq[group, k.z, k.q, index] = cast(number)

    def place_out():
        for j in range(4):
            wd[k.z, k.yy, j // 2, j % 2] = cast(FFN_OUT_ROWS + j)

    def place_in():
        piece = width // 4
        for h in range(2):
            for block in range(2):
                parts = [
                    cast(FFN_IN_ROWS + 2 * block + j)[:, (2 * g + h) * piece : (2 * g + h + 1) * piece]
                    for j in range(2)
                    for g in range(2)
                ]
                halves[h, block] = jnp.concatenate(parts, axis=1)
        fi[k.z, k.q] = halves[k.xx]
        swap("in", halves.at[1 - k.xx], fi.at[k.z, k.q], k.x)

    def start():
        k.greet()
        for copy in loads + page_loads:
            copy.start()
        vecs[k.z, k.q] = jnp.zeros(vecs.shape[2:], FULL)
        for row in range(vec.shape[0]):
            vecs[k.z, k.q, row : row + 1, :rows] = vec[row]
        loads[0].wait()
        place((KV_CROSS, 0, 1), (KV_CROSS, 1, 2))
        k.met()

    def cast1():
        loads[2].wait()
        loads[3].wait()
        place((JOIN, 0, 8), (JOIN, 1, 9))
        place_out()

    def cast2():
        for copy in (loads[1], *loads[4:], *page_loads):
            copy.wait()
        place((QO_CROSS, 0, 0), (QO_CROSS, 1, 6), (QK_SELF, 0, 3), (QK_SELF, 1, 4))
        place((VO_SELF, 0, 5), (VO_SELF, 1, 7))
        place_in()
        nothing[...] = jnp.zeros_like(nothing)
        for one in (k1, v1, k2, v2):
            act[one, pl.ds(count, slots - KEPT)] = jnp.zeros((slots - KEPT, width), LOW)

    def kv0():
        free(0)[...] = times(x[...], weight(KV_CROSS, 0)).astype(LOW)
        swap("keys", free(0), rows_in(k1))

    def kv1():
        free(1)[...] = times(x[...], weight(KV_CROSS, 1)).astype(LOW)
        swap("values", free(1), rows_in(v1))

    def vectors():
        sums = jnp.zeros((8, width), FULL)
        zeros = jnp.zeros((8, width - 128), FULL)
        for d in range(RANKS):
            tile = jnp.concatenate([vecs[d // PLANE, d % PLANE], zeros], axis=1)
            sums = sums + (pltpu.roll(tile, d * rows, 1) if d else tile)
        vw[...] = sums.astype(LOW).astype(FULL)

    def project_q1():
        rows_in(q1)[...] = times(x[...], weight(QO_CROSS, 0)).astype(LOW)
        swapped("keys", "values")

    def ln1():
        acc[...] = times(rows_in(o1)[...], weight(QO_CROSS, 1))

        def step(at, i):
            value = norm(0, at, x[at].astype(FULL) + acc[at] * keep(i))
            res[at] = value
            act[h1, at] = value.astype(LOW)

        by_rows(step)

    def project_self(slot_, group, index):
        rows_in(slot_)[...] = times(rows_in(h1)[...], weight(group, index)).astype(LOW)

    def in_two(step, name, buffer, target, peer):
        half = (count // BLOCK + 1) // 2
        for number, first, last in ((0, 0, half), (1, half, count // BLOCK)):
            by_rows(step, first, last)
            at = pl.ds(first * BLOCK, (last - first) * BLOCK)
            swap((name, number), buffer.at[at], target.at[at], peer)

    def theirs_in_two(name, result, target):
        half = (count // BLOCK + 1) // 2 * BLOCK
        for number, first, size in ((0, 0, half), (1, half, count - half)):
            at = pl.ds(first, size)
            acc[at] = result(pl.ds(count + first, size))
            act[edge, at] = acc[at].astype(LOW)
            swap((name, number), act.at[edge, at], target.at[at], k.x)

    def ln2():
        acc[...] = times(rows_in(o2)[...], weight(VO_SELF, 1))

        def step(at, i):
            del i
            value = norm(1, at, res[at] + acc[at])
            res[at] = value
            h2a[at] = value.astype(LOW)

        in_two(step, H2, h2a, h2a.at[theirs], k.x)

    def ffn_in(whose, block):
        if whose is theirs and block == 0:
            swapped((H2, 0), (H2, 1))
        first = 0 if whose is mine else count
        acc[...] = times(h2a[whose], in_weight(block))

        def step(at, i):
            value = acc[at]
            share = 0.5 + 0.5 * lax.erf(value * (0.5**0.5))
            bell = jnp.exp(value * value * -0.5) * (1.0 / (2.0 * math.pi) ** 0.5)
            to = pl.ds(pl.multiple_of(first + i * BLOCK, BLOCK), BLOCK)
            mid[block, to] = (value * share).astype(LOW)
            slope[block, to] = (share + value * bell).astype(LOW)

        by_rows(step)

    def ffn_out_theirs():
        def rows_of_result(to):
            return times(mid[0, to], out_weight(0)) + times(mid[1, to], out_weight(1))

        theirs_in_two(FFN, rows_of_result, rows_in(back))

    def ffn_out_mine():
        for block in range(2):
            res[...] += times(mid[block, mine], out_weight(block))

    def ln3():
        swapped((FFN, 0), (FFN, 1))

        def step(at, i):
            del i
            value = res[at] + act[back, at].astype(FULL)
            act[state, at] = norm(2, at, value).astype(LOW)

        in_two(step, STATE, rows_in(state), rows_in(far), k.twin)

    def join_own():
        acc[...] = times(rows_in(state)[...], weight(JOIN, 0))

    def join_far():
        swapped((STATE, 0), (STATE, 1))
        acc[...] += times(rows_in(far)[...], weight(JOIN, 1))

    def gate():
        part[...] = jnp.zeros_like(part)

        def step(at, i):
            own = act[state, at].astype(FULL)
            other = act[far, at].astype(FULL)
            share = jax.nn.sigmoid(acc[at] + vector(6))
            mask = row_mask(i)
            grad = cot[at].astype(FULL) * mask
            cot[at] = ((share * own + (1.0 - share) * other) * mask).astype(LOW)
            to_own, to_other = grad * share, grad * (1.0 - share)
            logits = (to_own * (own - other) * (1.0 - share)).astype(LOW)
            ea[at] = logits
            part[0] += fold(logits.astype(FULL))
            res[at] = to_own
            grd[at] = to_other

        by_rows(step)
        vg[6:7, :] = jnp.sum(part[0], axis=0, keepdims=True)
        vg[7:8, :] = jnp.zeros((1, width), FULL)
        pages_out(cot, joined, 0)

    def join_back():
        logits = ea.at[mine]
        rows_in(edge)[...] = (grd[...] + times_transposed(logits[...], weight(JOIN, 1))).astype(LOW)
        swap("edge", rows_in(edge), rows_in(back))

    def join_back_own():
        logits = ea.at[mine]
        res[...] += times_transposed(logits[...], weight(JOIN, 0))

    def join_grad(index):
        square_grad(JOIN, index, rows_in(state + index)[...], rows_in(edge)[...])

    def keep_err(at, i, result):
        del i
        ea[at] = result.astype(LOW)

    def keep_branch(at, i, result):
        ea[at] = (result * keep(i)).astype(LOW)

    def ln3_back():
        swapped("edge")

        def grad(at):
            act[edge, at] = ea[at]
            return res[at] + act[back, at].astype(FULL)

        norm_back(2, grad, keep_err, lambda step: in_two(step, ERR, ea, ea.at[theirs], k.x))

    def hidden_back(whose, block):
        if whose is theirs and block == 0:
            swapped((ERR, 0), (ERR, 1))
        first = 0 if whose is mine else count
        acc[...] = times_transposed(ea[whose], out_weight(block))

        def step(at, i):
            to = pl.ds(pl.multiple_of(first + i * BLOCK, BLOCK), BLOCK)
            slope[block, to] = (acc[at] * slope[block, to].astype(FULL)).astype(LOW)

        by_rows(step)

    def out_grad(block):
        for at in TILES:
            grad = outer(mid[block], ea[:, at]).astype(LOW)
            wd[2 * block : 2 * block + 2, :, :, :, :, at] = grad.reshape(2, 2, 2, 2, rows, TILE)
        if block == 1:
            pl.semaphore_signal(ready, inc=1, device_id=k.twin, device_id_type=MESH)

    def ffn_in_back_theirs():
        def rows_of_result(to):
            one = times_transposed(slope[0, to], in_weight(0))
            return one + times_transposed(slope[1, to], in_weight(1))

        theirs_in_two(FFN_BACK, rows_of_result, rows_in(far))

    def ffn_in_back_mine():
        for block in range(2):
            grd[...] += times_transposed(slope[block, mine], in_weight(block))

    def in_grad(block):
        for at in TILES:
            grad = outer(h2a[...], slope[block, :, at]).astype(LOW)
            fi[:, :, block, :, at] = grad.reshape(LINE, PLANE, rows, TILE)

    def ln2_back():
        swapped((FFN_BACK, 0), (FFN_BACK, 1))
        norm_back(1, lambda at: grd[at] + act[far, at].astype(FULL), keep_err)
        free(0)[...] = times_transposed(ea[mine], weight(VO_SELF, 1)).astype(LOW)
        square_grad(VO_SELF, 1, rows_in(o2)[...], ea[mine])

    def self_back(group, index, which):
        grd[...] += times_transposed(spare(which)[...], weight(group, index))
        square_grad(group, index, rows_in(h1)[...], spare(which)[...])

    def ln1_back():
        norm_back(0, lambda at: grd[at], keep_branch)
        for d in range(RANKS):
            moved = pltpu.roll(vg[...], width - d * rows, 1) if d else vg[...]
            vecs[d // PLANE, d % PLANE] = moved[:, :128]
        free(0)[...] = times_transposed(ea[mine], weight(QO_CROSS, 1)).astype(LOW)
        square_grad(QO_CROSS, 1, rows_in(o1)[...], ea[mine])

    def cross_query_back():
        pl.semaphore_wait(ready, 1)
        swap("back_keys", spare(1), free(2))
        swap("back_values", spare(2), free(3))
        grd[...] += times_transposed(spare(0)[...], weight(QO_CROSS, 0))
        square_grad(QO_CROSS, 0, x[...], spare(0)[...])

    def cross_back(index):
        swapped(("back_keys", "back_values")[index])
        grd[...] += times_transposed(free(2 + index)[...], weight(KV_CROSS, index))
        square_grad(KV_CROSS, index, x[...], free(2 + index)[...])

    def last_cross_back():
        cross_back(1)
        narrow(grd, ea)
        pages_out(ea.at[mine], x_grad, 1)

    start(); gV.L(); gvec.L(); cast1(); gFO.X(); cast2(); gQO.L(); gJ.X(); gV.R(); gvec.R(); gV.X(); gvec.X()
    gQO.R(); gK.L(); gQK.L(); gJ.C(); gQO.X(); gV.C(); gvec.C(); gK.R(); gQK.R(); gVO.L(); gK.X(); gFI.L(); gQO.C()
    gQK.X(); gFO.L(0); gVO.R(); gK.C(); gVO.X(); gFI.R(); gFO.L(1); gQO.F(); gK.F(); kv0(); gV.F(); gvec.F()
    vectors(); kv1(); gQK.C(); project_q1(); attend(0, 0, q1, k1, v1, o1); gVO.C(); attend(1, 0, q1, k1, v1, o1)
    ln1(); gQK.F(); project_self(q2, QK_SELF, 0); gFI.X(); gJ.L(0); project_self(k2, QK_SELF, 1); gVO.F()
    project_self(v2, VO_SELF, 0); gFO.R(0); attend(0, 1, q2, k2, v2, o2); attend(1, 1, q2, k2, v2, o2); ln2()
    gJ.L(1); gFO.R(1); gJ.L(3); gFI.F(); gJ.L(2); ffn_in(theirs, 0); gFO.F(); ffn_in(theirs, 1); ffn_out_theirs()
    gJ.R(0); ffn_in(mine, 0); gJ.R(1); gJ.R(3); ffn_in(mine, 1); ffn_out_mine(); gJ.R(2); ln3(); gJ.F(); join_own()
    join_far(); gate(); join_back(); join_back_own(); ln3_back(); hidden_back(mine, 1); hidden_back(mine, 0)
    join_grad(1); ffn_in_back_mine(); sJ1.C(); join_grad(0); sJ0.C(); hidden_back(theirs, 0); sJ1.X()
    hidden_back(theirs, 1); ffn_in_back_theirs(); in_grad(1); in_grad(0); sFI.C(); sJ1.L(); out_grad(0); sJ1.B()
    out_grad(1); sFO.L(0); ln2_back(); attend_back(0, 1, q2, k2, v2); sFO.B(0); sJ0.X()
    attend_back(1, 1, q2, k2, v2); sJ1.F(); sFI.L(); self_back(VO_SELF, 0, 2); sVO.C(); self_back(QK_SELF, 0, 0)
    sJ0.L(); self_back(QK_SELF, 1, 1); sQK.C(); sFI.B(); ln1_back(); sVO.X(); sFO.L(1)
    attend_back(0, 0, q1, k1, v1); sQK.X(); sJ0.B(); attend_back(1, 0, q1, k1, v1); cross_query_back(); sVO.L()
    sQO.C(); svec.C(); sJ0.F(); sFO.B(1); cross_back(0); sVO.B(); sQO.X(); svec.X(); last_cross_back(); sK.C()
    sQK.L(); sFO.M(1); sQK.B(); sK.X(); sV.C(); sQO.L(); svec.L(); sK.L(); sFO.M(0); sV.X(); sQO.B(); svec.B()
    sQK.F(); sFO.X(); sFI.F(); sK.B(); sV.L(); sV.B(); sFI.G(); sK.F(); sVO.F(); sQO.F(); svec.F(); sFO.F(); sV.F()
    for copy in page_copies:
        copy.wait()
    for item in scatters:
        for copy in item.put.copies:
            copy.wait()


def hand_over(count, *refs):
    sources, targets, rooms, sems = refs[:count], refs[count : 2 * count], refs[2 * count : -1], refs[-1]
    loads = [
        pltpu.make_async_copy(source, room, sems.at[0, i])
        for i, (source, room) in enumerate(zip(sources, rooms))
    ]
    stores = [
        pltpu.make_async_copy(room, target, sems.at[1, i])
        for i, (room, target) in enumerate(zip(rooms, targets))
    ]
    for copy in loads:
        copy.start()
    for load, copy in zip(loads, stores):
        load.wait()
        copy.start()
    for copy in stores:
        copy.wait()


def run_layer(x_in, lengths, drops, proj, outw, fin, fout, join, vectors, cot):
    pages, slots, width = x_in.shape[1:]
    rows = proj.shape[3]
    count = pages * KEPT
    vec = jnp.transpose(vectors, (1, 0, 2))
    vmem = pl.BlockSpec(memory_space=pltpu.VMEM)
    smem = pl.BlockSpec(memory_space=pltpu.SMEM)
    hbm = pl.BlockSpec(memory_space=pl.ANY)
    slab = (2, rows, width)
    scratch = [
        pltpu.VMEM((SQUARES, LINE, PLANE) + slab, LOW),
        pltpu.VMEM((LINE, PLANE) + slab, LOW),
        pltpu.VMEM((LINE, 2, 2) + slab, LOW),
        pltpu.VMEM((2,) + slab, LOW),
        pltpu.VMEM((LINE, PLANE, 8, 128), FULL),
        pltpu.VMEM((CORNER_RING, 2, HALF) + slab, LOW),
        pltpu.VMEM((SIDE_RING, LINE, 2) + slab, LOW),
        pltpu.VMEM((LINE_RING, LINE - 1) + slab, LOW),
        pltpu.VMEM((HOP_RING,) + slab, LOW),
        pltpu.VMEM((2,) + slab, LOW),
        pltpu.VMEM((PAIR_RING, LINE - 1, 2) + slab, LOW),
        pltpu.VMEM((PAIR_RING, 2) + slab, LOW),
        pltpu.VMEM((2, HALF, 8, 128), FULL),
        pltpu.VMEM((2, LINE, 8, 128), FULL),
        pltpu.VMEM((LINE - 1, 8, 128), FULL),
        pltpu.VMEM((8, 128), FULL),
        pltpu.VMEM((8, width), FULL),
        pltpu.VMEM((8, width), FULL),
        pltpu.VMEM((2, 8, width), FULL),
        pltpu.VMEM((count, width), LOW),
        pltpu.VMEM((count, width), LOW),
        pltpu.VMEM((slots - KEPT, width), LOW),
        pltpu.VMEM((2 * count, width), LOW),
        pltpu.VMEM((2 * count, width), LOW),
        pltpu.VMEM((13, count + slots - KEPT, width), LOW),
        pltpu.VMEM((2, 2 * count, width), LOW),
        pltpu.VMEM((2, 2 * count, width), LOW),
        pltpu.VMEM((2, pages * (width // PAIR), 2 * KEPT, slots), LOW),
        pltpu.VMEM((3, count, width), LOW),
        pltpu.VMEM((3, count, 1), FULL),
        pltpu.VMEM((3 * count, width), FULL),
        pltpu.SemaphoreType.DMA((8,)),
        pltpu.SemaphoreType.DMA((6 * pages,)),
        pltpu.SemaphoreType.DMA((18,)),
        pltpu.SemaphoreType.DMA((TRANSFERS,)),
        pltpu.SemaphoreType.DMA((TRANSFERS,)),
        pltpu.SemaphoreType.REGULAR,
    ]
    shapes = (
        ((pages, slots, width), LOW),
        ((pages, slots, width), LOW),
        ((6, rows, width), FULL),
        ((2, rows, width), FULL),
        ((rows, 4 * width), FULL),
        ((4 * rows, width), FULL),
        ((2, rows, width), FULL),
        ((vectors.shape[1], 1, rows), FULL),
    )
    results = pl.pallas_call(
        partial(layer_kernel, rows),
        out_shape=[jax.ShapeDtypeStruct(*shape) for shape in shapes],
        in_specs=[smem, smem] + [hbm] * 7 + [vmem],
        out_specs=[hbm] * 7 + [vmem],
        scratch_shapes=scratch,
        compiler_params=pltpu.CompilerParams(
            collective_id=0, has_side_effects=True, vmem_limit_bytes=VMEM_LIMIT
        ),
    )(
        lengths,
        drops,
        x_in[0],
        cot[0],
        proj.reshape(6 * rows, width),
        outw.reshape(2 * rows, width),
        fin[0],
        fout[0],
        join.reshape(2 * rows, width),
        vec,
    )
    results = pl.pallas_call(
        partial(hand_over, len(shapes)),
        out_shape=[jax.ShapeDtypeStruct(*shape) for shape in shapes],
        in_specs=[hbm] * len(shapes),
        out_specs=[hbm] * len(shapes),
        scratch_shapes=[pltpu.VMEM(*shape) for shape in shapes]
        + [pltpu.SemaphoreType.DMA((2, len(shapes)))],
        compiler_params=pltpu.CompilerParams(vmem_limit_bytes=VMEM_LIMIT),
    )(*results)
    joined, x_grad, proj_g, out_g, fin_g, fout_g, join_g, vec_g = results
    return (
        joined[None],
        x_grad[None],
        proj_g.reshape(proj.shape),
        out_g[None],
        fin_g[None],
        fout_g[None],
        join_g[None],
        jnp.transpose(vec_g, (1, 0, 2)),
    )


def fits(ranks, x_in, proj, fout):
    rows, width = proj.shape[3:]
    return (
        ranks == RANKS
        and x_in.shape[1] == 4
        and x_in.shape[2] == 2 * HEAD
        and rows % 16 == 0
        and rows <= 128
        and width == HEADS * HEAD
        and fout.shape[1] == 4 * rows
    )


def swapped(array, axis, stride):
    return lax.ppermute(array, axis, [(i, i ^ 1 << stride) for i in range(lax.axis_size(axis))])


def product(left, right):
    return jnp.dot(left, right, preferred_element_type=jnp.float32)


def outer_sum(left, right):
    return lax.dot_general(
        left, right, (((0,), (0,)), ((), ())), preferred_element_type=jnp.float32
    )


def times_transposed(left, right):
    return lax.dot_general(
        left, right, (((1,), (1,)), ((), ())), preferred_element_type=jnp.float32
    )


def norm_forward(values, gain, shift):
    centre = values - jnp.mean(values, axis=-1, keepdims=True)
    inverse = lax.rsqrt(jnp.mean(centre * centre, axis=-1, keepdims=True) + EPSILON)
    unit = centre * inverse
    return (unit * gain + shift, unit, inverse)


def norm_backward(grad, unit, inverse, gain):
    scaled = grad * gain
    inner = (
        scaled
        - jnp.mean(scaled, axis=-1, keepdims=True)
        - unit * jnp.mean(scaled * unit, axis=-1, keepdims=True)
    )
    return (inverse * inner, jnp.sum(grad * unit, axis=0), jnp.sum(grad, axis=0))


def heads_view(values, pages):
    return values.reshape(pages, values.shape[0] // pages, HEADS, values.shape[1] // HEADS)


def masked_scores(query, keys, key_mask, pages):
    scale = (query.shape[1] // HEADS) ** (-0.5)
    scores = (
        jnp.einsum(
            "pqhe,pkhe->phqk",
            heads_view(query, pages),
            heads_view(keys, pages),
            preferred_element_type=jnp.float32,
        )
        * scale
    )
    return jnp.where(key_mask[:, None, None, :], scores, -1e30)


def attend_forward(query, keys, values, key_mask, pages):
    scores = masked_scores(query, keys, key_mask, pages)
    top = jnp.max(scores, axis=-1, keepdims=True)
    weights = jnp.exp(scores - top)
    total = jnp.sum(weights, axis=-1, keepdims=True)
    probs = (weights / total).astype(jnp.bfloat16)
    mixed = jnp.einsum(
        "phqk,pkhe->pqhe", probs, heads_view(values, pages), preferred_element_type=jnp.float32
    )
    return (mixed.reshape(query.shape).astype(jnp.bfloat16), top + jnp.log(total))


def attend_backward(grad_out, query, keys, values, key_mask, logsum, pages):
    scale = (query.shape[1] // HEADS) ** (-0.5)
    probs = jnp.exp(masked_scores(query, keys, key_mask, pages) - logsum)
    grad_heads = heads_view(grad_out, pages)
    grad_probs = jnp.einsum(
        "pqhe,pkhe->phqk", grad_heads, heads_view(values, pages), preferred_element_type=jnp.float32
    )
    grad_scores = (
        probs * (grad_probs - jnp.sum(grad_probs * probs, axis=-1, keepdims=True))
    ).astype(jnp.bfloat16)
    grad_query = (
        jnp.einsum(
            "phqk,pkhe->pqhe",
            grad_scores,
            heads_view(keys, pages),
            preferred_element_type=jnp.float32,
        )
        * scale
    )
    grad_keys = (
        jnp.einsum(
            "phqk,pqhe->pkhe",
            grad_scores,
            heads_view(query, pages),
            preferred_element_type=jnp.float32,
        )
        * scale
    )
    grad_values = jnp.einsum(
        "phqk,pqhe->pkhe",
        probs.astype(jnp.bfloat16),
        grad_heads,
        preferred_element_type=jnp.float32,
    )
    shape = query.shape
    return (
        grad_query.reshape(shape).astype(jnp.bfloat16),
        grad_keys.reshape(shape).astype(jnp.bfloat16),
        grad_values.reshape(shape).astype(jnp.bfloat16),
    )


def local(
    x_in,
    lengths,
    drops,
    proj_master,
    out_master,
    ffn_in_master,
    ffn_out_master,
    join_master,
    vectors,
    cotangent,
):
    if fits(lax.axis_size("dp"), x_in, proj_master, ffn_out_master):
        return run_layer(
            x_in,
            lengths,
            drops,
            proj_master,
            out_master,
            ffn_in_master,
            ffn_out_master,
            join_master,
            vectors,
            cotangent,
        )
    pages = x_in.shape[1]
    slots = x_in.shape[2]
    width = x_in.shape[3]
    rows = pages * slots
    gathered = (
        lax.all_gather(proj_master.astype(jnp.bfloat16), "dp", axis=3, tiled=True),
        lax.all_gather(out_master.astype(jnp.bfloat16), "dp", axis=2, tiled=True),
        lax.all_gather(ffn_in_master.astype(jnp.bfloat16), "dp", axis=1, tiled=True),
        lax.all_gather(ffn_out_master.astype(jnp.bfloat16), "dp", axis=1, tiled=True),
        lax.all_gather(join_master.astype(jnp.bfloat16), "dp", axis=2, tiled=True),
        lax.all_gather(vectors.astype(jnp.bfloat16), "dp", axis=2, tiled=True),
    )
    proj_w = gathered[0][0]
    out_w = gathered[1][0]
    ffin_w = gathered[2][0]
    ffout_w = gathered[3][0]
    join_w = gathered[4][0]
    vec_w = gathered[5][0].astype(jnp.float32)
    key_mask = jnp.arange(slots, dtype=jnp.int32)[None, :] < lengths[:, None]
    row_mask = key_mask.reshape(rows, 1).astype(jnp.float32)
    keep = (1 - drops).astype(jnp.float32)
    keep_rows = jnp.broadcast_to(keep[:, None], (pages, slots)).reshape(rows, 1)
    source = x_in[0].reshape(rows, width)
    own_keys = product(source, proj_w[0, 1]).astype(jnp.bfloat16)
    own_values = product(source, proj_w[0, 2]).astype(jnp.bfloat16)
    far_keys, far_values = swapped((own_keys, own_values), "stream", 0)
    cross_query = product(source, proj_w[0, 0]).astype(jnp.bfloat16)
    cross_out, cross_logsum = attend_forward(cross_query, far_keys, far_values, key_mask, pages)
    first, unit_one, inverse_one = norm_forward(
        source.astype(jnp.float32) + product(cross_out, out_w[0]) * keep_rows, vec_w[0], vec_w[1]
    )
    first_low = first.astype(jnp.bfloat16)
    self_query = product(first_low, proj_w[1, 0]).astype(jnp.bfloat16)
    self_keys = product(first_low, proj_w[1, 1]).astype(jnp.bfloat16)
    self_values = product(first_low, proj_w[1, 2]).astype(jnp.bfloat16)
    self_out, self_logsum = attend_forward(self_query, self_keys, self_values, key_mask, pages)
    second, unit_two, inverse_two = norm_forward(
        first + product(self_out, out_w[1]), vec_w[2], vec_w[3]
    )
    second_low = second.astype(jnp.bfloat16)
    hidden = product(second_low, ffin_w)
    gelu_exact = partial(jax.nn.gelu, approximate=False)
    active_f32, gelu_pull = jax.vjp(gelu_exact, hidden)
    active = active_f32.astype(jnp.bfloat16)
    third, unit_three, inverse_three = norm_forward(
        second + product(active, ffout_w), vec_w[4], vec_w[5]
    )
    state = third.astype(jnp.bfloat16)
    far_state = swapped(state, "stream", 0)
    state_f32 = state.astype(jnp.float32)
    far_f32 = far_state.astype(jnp.float32)
    gate = jax.nn.sigmoid(product(state, join_w[0]) + product(far_state, join_w[1]) + vec_w[6])
    joined = ((gate * state_f32 + (1.0 - gate) * far_f32) * row_mask).astype(jnp.bfloat16)
    grad_joined = cotangent[0].reshape(rows, width).astype(jnp.float32) * row_mask
    grad_logits = (grad_joined * (state_f32 - far_f32) * gate * (1.0 - gate)).astype(jnp.bfloat16)
    grad_join = jnp.stack([outer_sum(state, grad_logits), outer_sum(far_state, grad_logits)])
    grad_bias = jnp.sum(grad_logits.astype(jnp.float32), axis=0)
    grad_far = (grad_joined * (1.0 - gate) + times_transposed(grad_logits, join_w[1])).astype(
        jnp.bfloat16
    )
    returned = swapped(grad_far, "stream", 0)
    grad_third = (
        grad_joined * gate + times_transposed(grad_logits, join_w[0]) + returned.astype(jnp.float32)
    )
    grad_res3, gain_three, shift_three = norm_backward(
        grad_third, unit_three, inverse_three, vec_w[4]
    )
    grad_res3_low = grad_res3.astype(jnp.bfloat16)
    grad_ffout = outer_sum(active, grad_res3_low)
    grad_hidden = gelu_pull(times_transposed(grad_res3_low, ffout_w))[0].astype(jnp.bfloat16)
    grad_ffin = outer_sum(second_low, grad_hidden)
    grad_second = grad_res3 + times_transposed(grad_hidden, ffin_w)
    grad_res2, gain_two, shift_two = norm_backward(grad_second, unit_two, inverse_two, vec_w[2])
    grad_res2_low = grad_res2.astype(jnp.bfloat16)
    grad_out_self = outer_sum(self_out, grad_res2_low)
    grad_self_out = times_transposed(grad_res2_low, out_w[1]).astype(jnp.bfloat16)
    grad_q2, grad_k2, grad_v2 = attend_backward(
        grad_self_out, self_query, self_keys, self_values, key_mask, self_logsum, pages
    )
    grad_proj_self = jnp.stack(
        [
            outer_sum(first_low, grad_q2),
            outer_sum(first_low, grad_k2),
            outer_sum(first_low, grad_v2),
        ]
    )
    grad_first = (
        grad_res2
        + times_transposed(grad_q2, proj_w[1, 0])
        + times_transposed(grad_k2, proj_w[1, 1])
        + times_transposed(grad_v2, proj_w[1, 2])
    )
    grad_res1, gain_one, shift_one = norm_backward(grad_first, unit_one, inverse_one, vec_w[0])
    grad_branch = (grad_res1 * keep_rows).astype(jnp.bfloat16)
    grad_out_cross = outer_sum(cross_out, grad_branch)
    grad_cross_out = times_transposed(grad_branch, out_w[0]).astype(jnp.bfloat16)
    grad_q1, grad_far_keys, grad_far_values = attend_backward(
        grad_cross_out, cross_query, far_keys, far_values, key_mask, cross_logsum, pages
    )
    back_keys, back_values = swapped((grad_far_keys, grad_far_values), "stream", 0)
    grad_proj_cross = jnp.stack(
        [outer_sum(source, grad_q1), outer_sum(source, back_keys), outer_sum(source, back_values)]
    )
    grad_source = (
        grad_res1
        + times_transposed(grad_q1, proj_w[0, 0])
        + times_transposed(back_keys, proj_w[0, 1])
        + times_transposed(back_values, proj_w[0, 2])
    )
    grad_proj = jnp.stack([grad_proj_cross, grad_proj_self])[None]
    grad_out = jnp.stack([grad_out_cross, grad_out_self])[None]
    grad_vectors = jnp.stack(
        [gain_one, shift_one, gain_two, shift_two, gain_three, shift_three, grad_bias]
    )[None]
    all_sums = (
        lax.psum_scatter(grad_proj, "dp", scatter_dimension=3, tiled=True),
        lax.psum_scatter(grad_out, "dp", scatter_dimension=2, tiled=True),
        lax.psum_scatter(grad_ffin[None], "dp", scatter_dimension=1, tiled=True),
        lax.psum_scatter(grad_ffout[None], "dp", scatter_dimension=1, tiled=True),
        lax.psum_scatter(grad_join[None], "dp", scatter_dimension=2, tiled=True),
        lax.psum_scatter(grad_vectors, "dp", scatter_dimension=2, tiled=True),
    )
    proj_part, out_part, ffin_part, ffout_part, join_part, vectors_part = all_sums
    joined_out = joined.reshape(1, pages, slots, width)
    x_grad = grad_source.astype(jnp.bfloat16).reshape(1, pages, slots, width)
    return (joined_out, x_grad, proj_part, out_part, ffin_part, ffout_part, join_part, vectors_part)


def solution(mesh):
    placed = (
        P("stream", "dp", None, None),
        P("dp"),
        P("dp"),
        P("stream", None, None, "dp", None),
        P("stream", None, "dp", None),
        P("stream", "dp", None),
        P("stream", "dp", None),
        P("stream", None, "dp", None),
        P("stream", None, "dp"),
        P("stream", "dp", None, None),
    )
    return jax.shard_map(
        local,
        mesh=mesh,
        in_specs=placed,
        out_specs=(
            P("stream", "dp", None, None),
            P("stream", "dp", None, None),
            P("stream", None, None, "dp", None),
            P("stream", None, "dp", None),
            P("stream", "dp", None),
            P("stream", "dp", None),
            P("stream", None, "dp", None),
            P("stream", None, "dp"),
        ),
        check_vma=False,
    )
```
